32 devices in a mesh: dom: 4 (over z), src: 4 (over y, x), rel: 2 (over core).
Axes of the slice: x: 2, y: 2, z: 4, core: 2. Of those that a mesh axis runs over, the one named last changes fastest.
Arguments:
- source_feats: bfloat16 [8192, 256], P(('dom', 'src', 'rel')), may hold values from -6 to 6
- rel_weight: bfloat16 [12, 256, 256], P('rel'), may hold values from -0.375 to 0.375
- halo_pick: int32 [4, 4, 2, 4], P('dom', 'src', 'rel'), may hold values from 0 to 1
- entry_index: int32 [4, 4, 2, 3, 64], P('dom', 'src', 'rel'), may hold values from 0 to 15, as said below
- entry_count: int32 [4, 4, 2], P('dom', 'src', 'rel'), may hold values from 1 to 64, as said below
- entry_values: bfloat16 [4, 4, 2, 64, 128, 128], P('dom', 'src', 'rel'), may hold values from -0.125 to 0.125
- cotangent: bfloat16 [8192, 256], P(('dom', 'src', 'rel')), may hold values from -0.21875 to 0.21875
Outputs:
- out_feats: bfloat16 [8192, 256], P(('dom', 'src', 'rel'))
- grad_rel: float32 [12, 256, 256], P('rel')
The draws below stay inside these ranges and needn't reach their ends.
Inputs may be any that keep to these rules, and one draw needn't show every extreme that they name: `entry_index`: row 0 of an entry is a target block below 16, row 1 a partition below 4, row 2 a relation below 6. Over all 64 entries of one (p,s,g), every partition is named 64 // 4 times or once more. `entry_count`: live entries come first; some (p,s,g) has all 64 entries live in every draw.
All inputs are finite; a program needn't handle non-finite values.
Results may differ from the reference program's by a relative error of at most 0.0057.
Values may be sent and summed in bfloat16 or wider, within the bound.
No kernel may reach another device: no remote copies, remote signals or barrier semaphores. Data moves between devices by JAX's collectives and lax.ppermute only.
A program may use at most 64 MiB of HBM per device.

```python
import jax
import jax.numpy as jnp
from jax import lax

D = 256
REL = 12
BLOCK = 128
SRC_BLOCKS = 2
NNZ = 64
PARTS_SIZE = 4
SRC_GROUPS = 4
REL_GROUPS = 2
REL_DEV = 6
TGT_BLOCKS = 16
TGT = 8192
SRC_ROWS = 8192
N_SRC = 4
N_REL = 2


def draw_entry_index(key, part):

    def one_device(device_key):
        keys = jax.random.split(device_key, 3)
        targets = jax.random.randint(keys[0], (NNZ,), 0, TGT_BLOCKS)
        peers = jax.random.permutation(keys[1], jnp.arange(NNZ, dtype=jnp.int32)) % PARTS_SIZE
        relations = jax.random.randint(keys[2], (NNZ,), 0, REL_DEV)
        return jnp.stack([targets, peers, relations]).astype(jnp.int32)
    keys = jax.random.split(jax.random.fold_in(key, 11), PARTS_SIZE * SRC_GROUPS * REL_GROUPS)
    table = jax.vmap(one_device)(keys)
    return table.reshape(PARTS_SIZE, SRC_GROUPS, REL_GROUPS, 3, NNZ)


def draw_entry_count(key, part):
    keys = jax.random.split(jax.random.fold_in(key, 23), 2)
    devices_all = PARTS_SIZE * SRC_GROUPS * REL_GROUPS
    counts = jax.random.randint(keys[0], (devices_all,), 1, NNZ + 1)
    full_device = jax.random.randint(keys[1], (), 0, devices_all)
    counts = counts.at[full_device].set(NNZ)
    return counts.reshape(PARTS_SIZE, SRC_GROUPS, REL_GROUPS).astype(jnp.int32)


def place_ends(result, own_key, low, top_value):
    index_at = [jax.random.randint(jax.random.fold_in(own_key, axis), (), 0, length) for axis, length in enumerate(result.shape)]
    widest = result.shape.index(max(result.shape))
    next_to = index_at[:widest] + [(index_at[widest] + 1) % result.shape[widest]] + index_at[widest + 1:]
    return result.at[tuple(index_at)].set(low).at[tuple(next_to)].set(top_value)


def block_levels(stream_key, extent, shards, least, largest):
    def one(dim, parts):
        steps = jax.random.uniform(jax.random.fold_in(jax.random.fold_in(stream_key, 6), dim), (parts,), jnp.float32, least / len(shards), largest / len(shards))
        return jnp.repeat(jnp.exp(steps), extent[dim] // parts).reshape((-1,) + (1,) * (len(extent) - dim - 1))

    factor_of = one(*shards[0])
    for cut in shards[1:]:
        factor_of = factor_of * one(*cut)
    return factor_of


def noise(key, dims, width, limit, cuts=(), kind=jnp.bfloat16):
    entries = jax.random.normal(key, dims, jnp.float32) * width
    if len(cuts) > 0:
        entries = block_levels(key, dims, cuts, -0.22, 0.18) * entries
    return jnp.clip(entries, min=-limit, max=limit).astype(kind)


def setup_inputs(seed: int = 0) -> dict:
    key_list = jax.random.split(jax.random.key(seed), 8)
    source_feats = noise(key_list[0], (SRC_ROWS, D), 1.0, 6.0, ((0, 32),))
    rel_weight = noise(key_list[1], (REL, D, D), D ** -0.5, 0.375, ((0, 2),))
    halo_pick = place_ends(jax.random.randint(key_list[2], (PARTS_SIZE, SRC_GROUPS, REL_GROUPS, PARTS_SIZE), 0, SRC_BLOCKS), jax.random.fold_in(key_list[2], 1), 0, SRC_BLOCKS - 1).astype(jnp.int32)
    entry_index = draw_entry_index(jax.random.fold_in(key_list[7], 71), 0)
    entry_count = draw_entry_count(jax.random.fold_in(key_list[7], 71), 0)
    entry_values = noise(key_list[5], (PARTS_SIZE, SRC_GROUPS, REL_GROUPS, NNZ, BLOCK, BLOCK), ((TGT_BLOCKS / (0.5 * BLOCK * NNZ * N_SRC * N_REL)) ** 0.5), 0.125, ((0, 4), (1, 4), (2, 2)))
    cotangent = noise(key_list[6], (TGT, D), ((REL / TGT) ** 0.5), 0.21875, ((0, 32),))
    return dict(source_feats=source_feats, rel_weight=rel_weight, halo_pick=halo_pick, entry_index=entry_index, entry_count=entry_count, entry_values=entry_values, cotangent=cotangent)


def silu_slope(pre_values):
    logistic = jax.nn.sigmoid(pre_values)
    return logistic * (1.0 + pre_values * (1.0 - logistic))


def reference(source_feats, rel_weight, halo_pick, entry_index, entry_count, entry_values, cotangent):
    source_view = source_feats.reshape(PARTS_SIZE, SRC_GROUPS, REL_GROUPS, SRC_BLOCKS, BLOCK, D)
    grouped_weight = rel_weight.reshape(REL_GROUPS, REL_DEV, D, D).astype(jnp.float32)
    cotangent_view = cotangent.reshape(PARTS_SIZE, TGT_BLOCKS * BLOCK, D)
    peer_index = jnp.arange(PARTS_SIZE, dtype=jnp.int32)
    entry_number = jnp.arange(NNZ, dtype=jnp.int32)
    highest = lax.Precision.HIGHEST

    def one_partition(grad_total, inputs):
        chosen, entry_table, live_count, values, cotangent_rows = inputs
        pre_sum = jnp.zeros((TGT_BLOCKS * BLOCK, D), jnp.float32)
        merged_groups = []
        for group in range(REL_GROUPS):
            merged = jnp.zeros((REL_DEV, TGT_BLOCKS * BLOCK, D), jnp.float32)
            for panel in range(SRC_GROUPS):
                halo_blocks = source_view[:, panel, group][peer_index, chosen[panel, group]]
                table = entry_table[panel, group]
                picked = halo_blocks[table[1]]
                messages = jnp.einsum("eij,ejd->eid", values[panel, group].astype(jnp.float32),
                                      picked.astype(jnp.float32), precision=highest)
                live_mask = (entry_number < live_count[panel, group]).astype(jnp.float32)
                messages = messages * live_mask[:, None, None]
                segment_ids = (table[2] * TGT_BLOCKS + table[0]).astype(jnp.int32)
                sums = jax.ops.segment_sum(messages, segment_ids, num_segments=REL_DEV * TGT_BLOCKS)
                relation_terms = lax.optimization_barrier(sums.astype(jnp.bfloat16))
                merged = merged + relation_terms.astype(jnp.float32).reshape(REL_DEV, TGT_BLOCKS * BLOCK, D)
            pre_sum = pre_sum + jnp.einsum("rtd,rde->te", merged, grouped_weight[group], precision=highest)
            merged_groups.append(merged)
        out_rows = jax.nn.silu(pre_sum).astype(jnp.bfloat16)
        grad_pre = lax.optimization_barrier((cotangent_rows.astype(jnp.float32) * silu_slope(pre_sum)).astype(jnp.bfloat16))
        grad_float = grad_pre.astype(jnp.float32)
        weight_terms = jnp.stack([jnp.einsum("rtd,te->rde", merged, grad_float, precision=highest)
                                  for merged in merged_groups])
        return grad_total + weight_terms, out_rows

    start_total = jnp.zeros((REL_GROUPS, REL_DEV, D, D), jnp.float32)
    grad_total, out_rows = lax.scan(one_partition, start_total,
                                    (halo_pick, entry_index, entry_count, entry_values, cotangent_view))
    return out_rows.reshape(TGT, D), grad_total.reshape(REL, D, D)
```

```python
import functools

import jax
import jax.numpy as jnp
from jax import lax
from jax.experimental import pallas as pl
from jax.experimental.pallas import tpu as pltpu
from jax.sharding import PartitionSpec as P

F32, BF16 = jnp.float32, jnp.bfloat16
VMEM_BYTES = 56 * 1024 * 1024
WHOLE = pl.BlockSpec(memory_space=pltpu.VMEM)
SCALARS = pl.BlockSpec(memory_space=pltpu.SMEM)


def partner_pairs(size, mask):
    return [(i, i ^ mask) for i in range(size)]


def swap(value, axis, mask):
    return lax.ppermute(value, axis, partner_pairs(lax.axis_size(axis), mask))


def halo_slot(places, partition, masked):
    return partition ^ places[0] if masked else partition


def forward_kernel(masked, tile, halo_count, places, chosen, table, count, *refs):
    halo_refs, (weight, values, keep, send, projected, pre) = refs[:halo_count], refs[halo_count:]
    relations, features = weight.shape[0], weight.shape[1]
    per_call = halo_refs[0].shape[0]
    slots = halo_count * per_call
    for slot in range(slots):
        partition = halo_slot(places, slot, masked)
        first = pl.multiple_of(chosen[partition] * tile, tile)
        block = halo_refs[slot // per_call][slot % per_call, pl.ds(first, tile), :]
        for r in range(relations):
            projected[slot * relations + r] = jnp.dot(
                block, weight[r], preferred_element_type=F32
            ).astype(BF16)
    pre[...] = jnp.zeros_like(pre)

    def entry(e, carry):
        slot = halo_slot(places, table[1, e], masked)
        term = jnp.dot(
            values[e], projected[slot * relations + table[2, e]], preferred_element_type=F32
        )
        target = table[0, e]
        pre[target] = pre[target] + term
        return carry

    lax.fori_loop(0, count[0], entry, 0)
    panels, per_owner = keep.shape[0], keep.shape[1] // tile
    groups = pre.shape[0] // (panels * per_owner)
    for distance in range(panels):
        panel = places[1] ^ distance
        for part in range(per_owner):
            rows = pl.ds(part * tile, tile)
            mine = (panel * groups + places[2]) * per_owner + part
            keep[distance, rows, :] = pre[mine]
            other = (panel * groups + (places[2] ^ 1)) * per_owner + part
            send[distance, rows, :] = pre[other].astype(BF16)


def terms_kernel(masked, tile, halo_count, places, chosen, table, count, *refs):
    halo_refs, (values, terms, turned, total) = refs[:halo_count], refs[halo_count:]
    per_call = halo_refs[0].shape[0]
    targets = terms.shape[2] // tile
    for slot in range(halo_count * per_call):
        partition = halo_slot(places, slot, masked)
        first = pl.multiple_of(chosen[partition] * tile, tile)
        block = halo_refs[slot // per_call][slot % per_call, pl.ds(first, tile), :]
        turned[slot] = block.astype(F32).T.astype(BF16)
    total[...] = jnp.zeros_like(total)

    def entry(e, carry):
        slot = halo_slot(places, table[1, e], masked)
        message = lax.dot_general(
            turned[slot], values[e], (((1,), (1,)), ((), ())), preferred_element_type=F32
        )
        columns = pl.ds(pl.multiple_of(table[0, e] * tile, tile), tile)
        relation = table[2, e]
        total[relation, :, columns] = total[relation, :, columns] + message
        return carry

    lax.fori_loop(0, count[0], entry, 0)
    terms[...] = total[...].astype(BF16)


def weight_kernel(terms, grads, out):
    out[0] = jnp.dot(terms[0], grads[...], preferred_element_type=F32).astype(BF16)


def silu_slope(pre_values):
    logistic = jax.nn.sigmoid(pre_values)
    return logistic * (1.0 + pre_values * (1.0 - logistic))


def reduce_scatter(pieces, axis):
    arrived = [swap(pieces[m].astype(BF16), axis, m) for m in range(len(pieces) - 1, 0, -1)]
    total = pieces[0].astype(F32)
    for value in arrived:
        total = total + value.astype(F32)
    return total


def gather(value, axis):
    return [value] + [swap(value, axis, m) for m in range(1, lax.axis_size(axis))]


def in_axis_order(pieces, axis):
    me = lax.axis_index(axis)
    stacked = jnp.stack(pieces)
    return stacked[me ^ jnp.arange(len(pieces), dtype=jnp.int32)]


def local(source_feats, rel_weight, halo_pick, entry_index, entry_count, entry_values, cotangent):
    partitions, panels = lax.axis_size("dom"), lax.axis_size("src")
    groups = lax.axis_size("rel")
    tile = entry_values.shape[-1]
    own_rows, features = cotangent.shape
    relations = rel_weight.shape[0]
    values = entry_values.reshape(-1, tile, tile)
    table = entry_index.reshape(3, -1)
    count = entry_count.reshape(1)
    chosen = halo_pick.reshape(-1)
    places = jnp.stack(
        [lax.axis_index("dom"), lax.axis_index("src"), lax.axis_index("rel")]
    ).astype(jnp.int32)
    target_rows = own_rows * panels * groups
    direct = partitions <= 8

    if direct:
        halo = [source_feats[None]] + [
            swap(source_feats, "dom", m)[None] for m in range(1, partitions)
        ]
    else:
        halo = [lax.all_gather(source_feats, "dom", axis=0)]
    slots = sum(h.shape[0] for h in halo)

    keep, send = pl.pallas_call(
        functools.partial(forward_kernel, direct, tile, len(halo)),
        out_shape=(
            jax.ShapeDtypeStruct((panels, own_rows, features), F32),
            jax.ShapeDtypeStruct((panels, own_rows, features), BF16),
        ),
        in_specs=[SCALARS] * 4 + [WHOLE] * (len(halo) + 2),
        out_specs=(WHOLE, WHOLE),
        scratch_shapes=[
            pltpu.VMEM((slots * relations, tile, features), BF16),
            pltpu.VMEM((target_rows // tile, tile, features), F32),
        ],
        compiler_params=pltpu.CompilerParams(vmem_limit_bytes=VMEM_BYTES),
        name="forward",
    )(places, chosen, table, count, *halo, rel_weight, values)

    chip_sum = keep + swap(send, "rel", 1).astype(F32)
    pre = reduce_scatter([chip_sum[m] for m in range(panels)], "src")

    terms = pl.pallas_call(
        functools.partial(terms_kernel, direct, tile, len(halo)),
        out_shape=jax.ShapeDtypeStruct((relations, features, target_rows), BF16),
        in_specs=[SCALARS] * 4 + [WHOLE] * (len(halo) + 1),
        out_specs=WHOLE,
        scratch_shapes=[
            pltpu.VMEM((slots, features, tile), BF16),
            pltpu.VMEM((relations, features, target_rows), F32),
        ],
        compiler_params=pltpu.CompilerParams(vmem_limit_bytes=VMEM_BYTES),
        cost_estimate=pl.CostEstimate(
            flops=2 * values.shape[0] * tile * tile * features,
            bytes_accessed=2 * relations * target_rows * features,
            transcendentals=0,
        ),
        name="terms",
    )(places, chosen, table, count, *halo, values)

    out_feats = jax.nn.silu(pre).astype(BF16)
    local_grad = (cotangent.astype(F32) * silu_slope(pre)).astype(BF16)

    chip_grads = in_axis_order(gather(local_grad, "src"), "src")
    both = in_axis_order([chip_grads, swap(chip_grads, "rel", 1)], "rel")
    grad_rows = both.transpose(1, 0, 2, 3).reshape(target_rows, features)

    weight_terms = pl.pallas_call(
        weight_kernel,
        grid=(relations,),
        out_shape=jax.ShapeDtypeStruct((relations, features, features), BF16),
        in_specs=[
            pl.BlockSpec((1, features, target_rows), lambda r: (r, 0, 0)),
            pl.BlockSpec((target_rows, features), lambda r: (0, 0)),
        ],
        out_specs=pl.BlockSpec((1, features, features), lambda r: (r, 0, 0)),
        compiler_params=pltpu.CompilerParams(vmem_limit_bytes=VMEM_BYTES),
        name="weight_terms",
    )(terms, grad_rows)

    flat = weight_terms.reshape(panels, -1, features)
    panel = lax.axis_index("src")
    pieces = [
        lax.dynamic_index_in_dim(flat, panel ^ m, 0, keepdims=False) for m in range(panels)
    ]
    panel_sum = reduce_scatter(pieces, "src").astype(BF16)
    if direct:
        parts = panel_sum.reshape(partitions, -1, features)
        part = lax.axis_index("dom")
        pieces = [
            lax.dynamic_index_in_dim(parts, part ^ m, 0, keepdims=False)
            for m in range(partitions)
        ]
        whole_sum = reduce_scatter(pieces, "dom").astype(BF16)
        dom_sum = in_axis_order(gather(whole_sum, "dom"), "dom").reshape(panel_sum.shape)
    else:
        dom_sum = lax.psum(panel_sum.astype(F32), "dom").astype(BF16)
    grad_rel = in_axis_order(gather(dom_sum, "src"), "src")
    grad_rel = grad_rel.reshape(relations, features, features).astype(F32)
    return (out_feats, grad_rel)


def solution(mesh):
    return jax.shard_map(
        local,
        mesh=mesh,
        in_specs=(
            P(("dom", "src", "rel"), None),
            P("rel", None, None),
            P("dom", "src", "rel", None),
            P("dom", "src", "rel", None, None),
            P("dom", "src", "rel"),
            P("dom", "src", "rel", None, None, None),
            P(("dom", "src", "rel"), None),
        ),
        out_specs=(P(("dom", "src", "rel"), None), P("rel", None, None)),
        check_vma=False,
    )
```

```python
import functools
import math

import jax
import jax.numpy as jnp
from jax import lax
from jax.experimental import pallas as pl
from jax.experimental.pallas import tpu as pltpu
from jax.sharding import PartitionSpec as P

F32, BF16, I32 = jnp.float32, jnp.bfloat16, jnp.int32
WHOLE = pl.BlockSpec(memory_space=pltpu.VMEM)
SCALARS = pl.BlockSpec(memory_space=pltpu.SMEM)
UNROLL = 16


def vmem_for(*arrays):
    held = sum(math.prod(a.shape) * jnp.dtype(a.dtype).itemsize for a in arrays)
    return pltpu.CompilerParams(vmem_limit_bytes=held + held // 8 + 3 * 1024 * 1024)


def partner_pairs(size, mask):
    return [(i, i ^ mask) for i in range(size)]


def swap(value, axis, mask):
    return lax.ppermute(value, axis, partner_pairs(lax.axis_size(axis), mask))


def slot_of(places, partition, masked):
    return partition ^ places[0] if masked else partition


def for_entries(total, body):
    def step(i, carry):
        body([(jnp.minimum(i * UNROLL + u, total - 1), i * UNROLL + u < total) for u in range(UNROLL)])
        return carry

    lax.fori_loop(0, (total + UNROLL - 1) // UNROLL, step, 0)


def halo_block(places, chosen, halo_refs, i, first_slot, masked, tile):
    per_call = halo_refs[0].shape[0]
    first = pl.multiple_of(chosen[slot_of(places, i + first_slot, masked)] * tile, tile)
    return halo_refs[i // per_call][i % per_call, pl.ds(first, tile), :]


def forward_kernel(masked, tile, first_slot, halo_count, earlier, last, combine, *refs):
    places, chosen, table, count = refs[:4]
    halo_refs, refs = refs[4 : 4 + halo_count], refs[4 + halo_count :]
    weight, values, refs = refs[0], refs[1], refs[2:]
    before, refs = (refs[0], refs[1:]) if earlier else (None, refs)
    if last:
        keep, send, pre, projected, order = refs
    else:
        pre, projected, order = refs
    relations = weight.shape[0]
    slots = halo_count * halo_refs[0].shape[0]

    def pick(e, found):
        slot = slot_of(places, table[1, e], masked) - first_slot

        @pl.when((slot >= 0) & (slot < slots))
        def _():
            order[found] = e

        return found + ((slot >= 0) & (slot < slots)).astype(I32)

    total = lax.fori_loop(0, count[0], pick, jnp.int32(0))
    for i in range(slots):
        block = halo_block(places, chosen, halo_refs, i, first_slot, masked, tile)
        if combine:
            for r in range(relations):
                projected[i * relations + r] = jnp.dot(
                    block, weight[r], preferred_element_type=F32
                ).astype(BF16)
        else:
            projected[i] = block
    pre[...] = jnp.zeros_like(pre)
    spare = pre.shape[0] - 1

    def body(positions):
        terms = []
        for position, _ in positions:
            e = order[position]
            slot = slot_of(places, table[1, e], masked) - first_slot
            relation = table[2, e]
            if combine:
                term = jnp.dot(
                    values[e], projected[slot * relations + relation], preferred_element_type=F32
                )
            else:
                message = jnp.dot(values[e], projected[slot], preferred_element_type=F32)
                term = jnp.dot(message.astype(BF16), weight[relation], preferred_element_type=F32)
            terms.append(term)
        for (position, real), term in zip(positions, terms):
            target = jnp.where(real, table[0, order[position]], spare)
            pre[target] = pre[target] + term

    for_entries(total, body)
    if not last:
        return
    panels, per_owner = keep.shape[0], keep.shape[1] // tile
    groups = spare // (panels * per_owner)
    for distance in range(panels):
        panel = places[1] ^ distance
        for part in range(per_owner):
            rows = pl.ds(part * tile, tile)
            mine = (panel * groups + places[2]) * per_owner + part
            other = (panel * groups + (places[2] ^ 1)) * per_owner + part
            mine_rows, other_rows = pre[mine], pre[other]
            if earlier:
                mine_rows, other_rows = mine_rows + before[mine], other_rows + before[other]
            keep[distance, rows, :] = mine_rows
            send[distance, rows, :] = other_rows.astype(BF16)


def turn_kernel(masked, tile, halo_count, shares, places, chosen, *refs):
    halo_refs = refs[:halo_count]
    values, values_turned, halo_turned, scratch = refs[halo_count:]
    panels, parts = shares
    per_call = halo_refs[0].shape[0]
    features = scratch.shape[0]
    share = features // (panels * parts)
    for slot in range(halo_count * per_call):
        block = halo_block(places, chosen, halo_refs, slot, 0, masked, tile)
        scratch[...] = block.astype(F32).T
        for m in range(panels):
            for k in range(parts):
                part = (places[0] ^ k) if parts > 1 else 0
                start = pl.multiple_of(((places[1] ^ m) * parts + part) * share, share)
                halo_turned[pl.ds((m * parts + k) * share, share), pl.ds(slot * tile, tile)] = (
                    scratch[pl.ds(start, share), :].astype(BF16)
                )

    batch = 8

    def step(i, carry):
        for u in range(batch):
            values_turned[i * batch + u] = values[i * batch + u].T
        return carry

    lax.fori_loop(0, values.shape[0] // batch, step, 0)


def weight_kernel(masked, tile, shares, combine, places, table, count, *refs):
    panels, parts = shares
    values_turned, halo_turned = refs[:2]
    grad_refs, refs = refs[2 : 2 + 2 * panels], refs[2 + 2 * panels :]
    outs, (grads, sums) = refs[:panels], refs[panels:]
    features = halo_turned.shape[0]
    slots = halo_turned.shape[1] // tile
    relations = outs[0].shape[1]
    share = features // (panels * parts)
    own_rows = grad_refs[0].shape[0]
    per_owner = own_rows // tile
    for g in range(2):
        for m in range(panels):
            owner = (places[1] ^ m) * 2 + (places[2] ^ g)
            for part in range(per_owner):
                grads[owner * per_owner + part] = grad_refs[g * panels + m][
                    pl.ds(part * tile, tile), :
                ]
    sums[...] = jnp.zeros_like(sums)
    spare = sums.shape[0] - 1

    def body(positions):
        terms = []
        for e, _ in positions:
            term = jnp.dot(values_turned[e], grads[table[0, e]], preferred_element_type=F32)
            if not combine:
                slot = slot_of(places, table[1, e], masked)
                columns = pl.ds(pl.multiple_of(slot * tile, tile), tile)
                term = jnp.dot(
                    halo_turned[:, columns], term.astype(BF16), preferred_element_type=F32
                )
            terms.append(term)
        for (e, real), term in zip(positions, terms):
            place = table[2, e]
            if combine:
                place = place * slots + slot_of(places, table[1, e], masked)
            place = jnp.where(real, place, spare)
            sums[place] = sums[place] + term

    for_entries(count[0], body)
    for r in range(relations):
        if combine:
            stacked = sums[r * slots : (r + 1) * slots].reshape(slots * tile, features)
            grad = jnp.dot(halo_turned[...], stacked.astype(BF16), preferred_element_type=F32)
        else:
            grad = sums[r]
        for m in range(panels):
            for k in range(parts):
                rows = slice((m * parts + k) * share, (m * parts + k + 1) * share)
                outs[m][k, r] = grad[rows].astype(BF16)


def spread_kernel(shares, places, *refs):
    panels, parts = shares
    shares_in, out = refs[:panels], refs[panels]
    share = shares_in[0].shape[2]
    for m in range(panels):
        for k in range(parts):
            part = (places[0] ^ k) if parts > 1 else 0
            start = pl.multiple_of(((places[1] ^ m) * parts + part) * share, share)
            for r in range(out.shape[0]):
                out[r, pl.ds(start, share), :] = shares_in[m][k, r].astype(F32)


def silu_slope(pre_values):
    logistic = jax.nn.sigmoid(pre_values)
    return logistic * (1.0 + pre_values * (1.0 - logistic))


def exchange(pieces, axis):
    return [swap(pieces[m].astype(BF16), axis, m) for m in range(len(pieces) - 1, 0, -1)]


def added(own, arrived):
    total = own.astype(F32)
    for value in arrived:
        total = total + value.astype(F32)
    return total


def gather(value, axis):
    return [value] + [swap(value, axis, m) for m in range(1, lax.axis_size(axis))]


def local(source_feats, rel_weight, halo_pick, entry_index, entry_count, entry_values, cotangent):
    partitions, panels = lax.axis_size("dom"), lax.axis_size("src")
    groups = lax.axis_size("rel")
    tile = entry_values.shape[-1]
    own_rows, features = cotangent.shape
    relations = rel_weight.shape[0]
    values = entry_values.reshape(-1, tile, tile)
    table = entry_index.reshape(3, -1)
    entries = table.shape[1]
    count = entry_count.reshape(1)
    chosen = halo_pick.reshape(-1)
    places = jnp.stack([lax.axis_index(a) for a in ("dom", "src", "rel")]).astype(I32)
    targets = own_rows * panels * groups // tile
    direct = partitions <= 8
    parts = partitions if direct else 1
    shares = (panels, parts)
    share = features // (panels * parts)

    if direct:
        halo = gather(source_feats, "dom")
        halo = [h[None] for h in halo]
        calls = [halo[: partitions // 2], halo[partitions // 2 :]]
    else:
        halo = [lax.all_gather(source_feats, "dom", axis=0)]
        calls = [halo]
    slots = sum(h.shape[0] for h in halo)
    combine = slots * relations <= entries

    before, first_slot = [], 0
    for number, part in enumerate(calls):
        last = number == len(calls) - 1
        here = sum(h.shape[0] for h in part)
        sums = jax.ShapeDtypeStruct((targets + 1, tile, features), F32)
        projected = (here * relations if combine else here, tile, features)
        projected = jax.ShapeDtypeStruct(projected, BF16)
        scratch = [pltpu.VMEM(projected.shape, BF16), pltpu.SMEM((entries,), I32)]
        grant = vmem_for(sums, projected, *part, rel_weight, values, *before)
        if last:
            out_shape = (
                jax.ShapeDtypeStruct((panels, own_rows, features), F32),
                jax.ShapeDtypeStruct((panels, own_rows, features), BF16),
            )
            scratch = [pltpu.VMEM(sums.shape, F32)] + scratch
            grant = vmem_for(sums, projected, *part, rel_weight, values, *before, *out_shape)
        else:
            out_shape = (sums,)
        before = pl.pallas_call(
            functools.partial(
                forward_kernel, direct, tile, first_slot, len(part), bool(before), last, combine
            ),
            out_shape=out_shape,
            in_specs=[SCALARS] * 4 + [WHOLE] * (len(part) + 2 + len(before)),
            out_specs=(WHOLE,) * len(out_shape),
            scratch_shapes=scratch,
            compiler_params=grant,
            cost_estimate=pl.CostEstimate(
                flops=2 * entries * tile * tile * features * 4,
                bytes_accessed=values.size * 2,
                transcendentals=0,
            ),
            name="forward",
        )(places, chosen, table, count, *part, rel_weight, values, *before)
        first_slot += here
    keep, send = before

    chip_sum = keep + swap(send, "rel", 1).astype(F32)
    arrived = exchange([chip_sum[m] for m in range(panels)], "src")

    turned = (
        jax.ShapeDtypeStruct(values.shape, BF16),
        jax.ShapeDtypeStruct((features, slots * tile), BF16),
    )
    values_turned, halo_turned = pl.pallas_call(
        functools.partial(turn_kernel, direct, tile, len(halo), shares),
        out_shape=turned,
        in_specs=[SCALARS] * 2 + [WHOLE] * (len(halo) + 1),
        out_specs=(WHOLE, WHOLE),
        scratch_shapes=[pltpu.VMEM((features, tile), F32)],
        compiler_params=vmem_for(*turned, values, *halo),
        cost_estimate=pl.CostEstimate(
            flops=0, bytes_accessed=4 * values.size, transcendentals=0
        ),
        name="turn",
    )(places, chosen, *halo, values)
    arrived, values_turned, halo_turned = lax.optimization_barrier(
        (arrived, values_turned, halo_turned)
    )
    pre = added(chip_sum[0], arrived)

    out_feats = jax.nn.silu(pre).astype(BF16)
    local_grad = (cotangent.astype(F32) * silu_slope(pre)).astype(BF16)

    core_grads = gather(local_grad, "src")
    other_grads = [swap(value, "rel", 1) for value in core_grads]

    rows = shares[1], relations, share, features
    grads = jax.ShapeDtypeStruct((targets, tile, features), BF16)
    sums = jax.ShapeDtypeStruct(
        (relations * slots + 1, tile, features) if combine else (relations + 1, features, features),
        F32,
    )
    weight_shares = pl.pallas_call(
        functools.partial(weight_kernel, direct, tile, shares, combine),
        out_shape=(jax.ShapeDtypeStruct(rows, BF16),) * panels,
        in_specs=[SCALARS] * 3 + [WHOLE] * (2 + 2 * panels),
        out_specs=(WHOLE,) * panels,
        scratch_shapes=[pltpu.VMEM(grads.shape, BF16), pltpu.VMEM(sums.shape, F32)],
        compiler_params=vmem_for(grads, grads, sums, *turned, rel_weight),
        name="weight_terms",
    )(places, table, count, values_turned, halo_turned, *core_grads, *other_grads)

    panel_sum = added(weight_shares[0], exchange(weight_shares, "src"))
    if direct:
        part_sum = added(
            panel_sum[0], exchange([panel_sum[k] for k in range(parts)], "dom")
        ).astype(BF16)
        whole_sum = jnp.stack(gather(part_sum, "dom"))
    else:
        whole_sum = lax.psum(panel_sum, "dom").astype(BF16)
    total = jax.ShapeDtypeStruct((relations, features, features), F32)
    grad_rel = pl.pallas_call(
        functools.partial(spread_kernel, shares),
        out_shape=total,
        in_specs=[SCALARS] + [WHOLE] * panels,
        out_specs=WHOLE,
        compiler_params=vmem_for(total, rel_weight),
        name="spread",
    )(places, *gather(whole_sum, "src"))
    return (out_feats, grad_rel)


def solution(mesh):
    return jax.shard_map(
        local,
        mesh=mesh,
        in_specs=(
            P(("dom", "src", "rel"), None),
            P("rel", None, None),
            P("dom", "src", "rel", None),
            P("dom", "src", "rel", None, None),
            P("dom", "src", "rel"),
            P("dom", "src", "rel", None, None, None),
            P(("dom", "src", "rel"), None),
        ),
        out_specs=(P(("dom", "src", "rel"), None), P("rel", None, None)),
        check_vma=False,
    )
```

```python
import functools
import math

import jax
import jax.numpy as jnp
from jax import lax
from jax.experimental import pallas as pl
from jax.experimental.pallas import tpu as pltpu
from jax.sharding import PartitionSpec as P

F32, BF16, I32 = jnp.float32, jnp.bfloat16, jnp.int32
WHOLE = pl.BlockSpec(memory_space=pltpu.VMEM)
SCALARS = pl.BlockSpec(memory_space=pltpu.SMEM)
ANYWHERE = pl.BlockSpec(memory_space=pl.ANY)
UNROLL = 16


def vmem_for(*arrays):
    held = sum(math.prod(a.shape) * jnp.dtype(a.dtype).itemsize for a in arrays)
    return pltpu.CompilerParams(vmem_limit_bytes=held + held // 8 + 3 * 1024 * 1024)


def partner_pairs(size, mask):
    return [(i, i ^ mask) for i in range(size)]


def swap(value, axis, mask):
    return lax.ppermute(value, axis, partner_pairs(lax.axis_size(axis), mask))


def slot_of(places, partition, masked):
    return partition ^ places[0] if masked else partition


def for_entries(total, body):
    def step(i, carry):
        body([(jnp.minimum(i * UNROLL + u, total - 1), i * UNROLL + u < total) for u in range(UNROLL)])
        return carry

    lax.fori_loop(0, (total + UNROLL - 1) // UNROLL, step, 0)


def halo_block(places, chosen, halo_refs, i, first_slot, masked, tile):
    per_call = halo_refs[0].shape[0]
    first = pl.multiple_of(chosen[slot_of(places, i + first_slot, masked)] * tile, tile)
    return halo_refs[i // per_call][i % per_call, pl.ds(first, tile), :]


def near_kernel(masked, tile, combine, near, bounds, places, chosen, table, count, *refs):
    halo_refs, refs = refs[:near], refs[near:]
    (weight, values, pre, others), lists, (projected, order) = refs[:4], refs[4:-2], refs[-2:]
    list_chunks(table, count, bounds, lists)
    entries = values.shape[0]

    def sort(e, found):
        mine = slot_of(places, table[1, e], masked) < near

        @pl.when(mine)
        def _():
            order[found] = e

        @pl.when(jnp.logical_not(mine))
        def _():
            others[e - found] = e

        return found + mine.astype(I32)

    total = lax.fori_loop(0, count[0], sort, jnp.int32(0))
    others[entries] = count[0] - total
    pre[...] = jnp.zeros_like(pre)
    project(masked, tile, combine, 0, places, chosen, halo_refs, weight, projected)
    add_entries(masked, combine, 0, places, table, values, weight, projected, order, total, pre)


def far_kernel(masked, tile, combine, near, places, chosen, table, order, *refs):
    halo_refs, refs = refs[:-7], refs[-7:]
    weight, values, before, pre, keep, send, projected = refs
    del before
    project(masked, tile, combine, near, places, chosen, halo_refs, weight, projected)
    total = order[values.shape[0]]
    add_entries(masked, combine, near, places, table, values, weight, projected, order, total, pre)
    hand_out(tile, places, pre, keep, send)


def all_kernel(masked, tile, combine, bounds, places, chosen, table, count, *refs):
    halo_refs, refs = refs[:1], refs[1:]
    (weight, values, keep, send), lists, (pre, projected, order) = refs[:4], refs[4:-3], refs[-3:]
    list_chunks(table, count, bounds, lists)

    def put(e, carry):
        order[e] = e
        return carry

    lax.fori_loop(0, count[0], put, 0)
    pre[...] = jnp.zeros_like(pre)
    project(masked, tile, combine, 0, places, chosen, halo_refs, weight, projected)
    add_entries(masked, combine, 0, places, table, values, weight, projected, order, count[0], pre)
    hand_out(tile, places, pre, keep, send)


def project(masked, tile, combine, first_slot, places, chosen, halo_refs, weight, projected):
    slots = len(halo_refs) * halo_refs[0].shape[0]
    relations = weight.shape[0]
    blocks = [
        halo_block(places, chosen, halo_refs, i, first_slot, masked, tile) for i in range(slots)
    ]
    if not combine:
        for i, block in enumerate(blocks):
            projected[i] = block
        return
    stacked = jnp.concatenate(blocks, axis=0)
    for r in range(relations):
        product = jnp.dot(stacked, weight[r], preferred_element_type=F32).astype(BF16)
        for i in range(slots):
            projected[i * relations + r] = product[i * tile : (i + 1) * tile]


def list_chunks(table, count, bounds, lists):
    def sort(e, found):
        relation = table[2, e]
        here = [(relation >= low) & (relation < high) for low, high in zip(bounds, bounds[1:])]
        for c, listed in enumerate(lists):

            @pl.when(here[c])
            def _():
                listed[found[c]] = e

        return tuple(f + h.astype(I32) for f, h in zip(found, here))

    found = lax.fori_loop(0, count[0], sort, (jnp.int32(0),) * len(lists))
    for listed, number in zip(lists, found):
        listed[listed.shape[0] - 1] = number


def add_entries(
    masked, combine, first_slot, places, table, values, weight, projected, order, total, pre
):
    relations = weight.shape[0]
    spare = pre.shape[0] - 1

    def body(positions):
        terms = []
        for position, _ in positions:
            e = order[position]
            slot = slot_of(places, table[1, e], masked) - first_slot
            relation = table[2, e]
            if combine:
                term = jnp.dot(
                    values[e], projected[slot * relations + relation], preferred_element_type=F32
                )
            else:
                message = jnp.dot(values[e], projected[slot], preferred_element_type=F32)
                term = jnp.dot(message.astype(BF16), weight[relation], preferred_element_type=F32)
            terms.append(term)
        for (position, real), term in zip(positions, terms):
            target = jnp.where(real, table[0, order[position]], spare)
            pre[target] = pre[target] + term

    for_entries(total, body)


def hand_out(tile, places, pre, keep, send):
    panels, per_owner = keep.shape[0], keep.shape[1] // tile
    groups = (pre.shape[0] - 1) // (panels * per_owner)
    for distance in range(panels):
        panel = places[1] ^ distance
        for part in range(per_owner):
            rows = pl.ds(part * tile, tile)
            mine = (panel * groups + places[2]) * per_owner + part
            other = (panel * groups + (places[2] ^ 1)) * per_owner + part
            send[distance, rows, :] = pre[other].astype(BF16)
            keep[distance, rows, :] = pre[mine]


def grad_kernel(own, first, second, third, cotangent, grad):
    pre = own[...] + first[...].astype(F32) + second[...].astype(F32) + third[...].astype(F32)
    grad[...] = (cotangent[...].astype(F32) * silu_slope(pre)).astype(BF16)


def turn_kernel(masked, tile, halo_count, panels, places, chosen, *refs):
    halo_refs, refs = refs[:halo_count], refs[halo_count:]
    values, values_turned, halo_turned, scratch = refs[0], refs[1], refs[2], refs[-1]
    entries = values.shape[0]
    for each in refs[3:-1]:
        each[...] = jnp.zeros_like(each)

    per_call = halo_refs[0].shape[0]
    features = scratch.shape[0]
    share = features // panels
    for slot in range(halo_count * per_call):
        block = halo_block(places, chosen, halo_refs, slot, 0, masked, tile)
        scratch[...] = block.astype(F32).T
        for m in range(panels):
            start = pl.multiple_of((places[1] ^ m) * share, share)
            halo_turned[pl.ds(m * share, share), pl.ds(slot * tile, tile)] = (
                scratch[pl.ds(start, share), :].astype(BF16)
            )

    batch = 8

    def step(i, carry):
        for u in range(batch):
            values_turned[i * batch + u] = values[i * batch + u].T
        return carry

    lax.fori_loop(0, entries // batch, step, 0)


def collect_kernel(tile, *refs):
    grad_refs, grads = refs[:-1], refs[-1]
    panels = len(grad_refs) // 2
    per_owner = grad_refs[0].shape[0] // tile
    for g in range(2):
        for m in range(panels):
            owner = (lax.axis_index("src") ^ m) * 2 + (lax.axis_index("rel") ^ g)
            for part in range(per_owner):
                grads[owner * per_owner + part] = grad_refs[g * panels + m][
                    pl.ds(part * tile, tile), :
                ]


def weight_kernel(masked, tile, first_relation, combine, places, table, listed, *refs):
    values_turned, halo_turned, grads = refs[:3]
    outs, sums = refs[4:-1], refs[-1]
    features = halo_turned.shape[0]
    slots = halo_turned.shape[1] // tile
    relations, share = outs[0].shape[0], outs[0].shape[1]
    spare = sums.shape[0] - 1

    def body(positions):
        terms = []
        for position, _ in positions:
            e = listed[position]
            term = jnp.dot(values_turned[e], grads[table[0, e]], preferred_element_type=F32)
            if not combine:
                slot = slot_of(places, table[1, e], masked)
                columns = pl.ds(pl.multiple_of(slot * tile, tile), tile)
                term = jnp.dot(
                    halo_turned[:, columns], term.astype(BF16), preferred_element_type=F32
                )
            terms.append(term)
        for (position, real), term in zip(positions, terms):
            e = listed[position]
            place = table[2, e] - first_relation
            if combine:
                place = place * slots + slot_of(places, table[1, e], masked)
            place = jnp.where(real, place, spare)
            sums[place] = sums[place] + term

    for_entries(listed[values_turned.shape[0]], body)
    for r in range(relations):
        if combine:
            stacked = sums[r * slots : (r + 1) * slots].reshape(slots * tile, features)
            grad = jnp.dot(halo_turned[...], stacked.astype(BF16), preferred_element_type=F32)
        else:
            grad = sums[r]
        for m, out in enumerate(outs):
            out[r] = grad[m * share : (m + 1) * share].astype(out.dtype)


def spread_kernel(first_relation, *refs):
    out, scratch, sems = refs[-3:]
    shares = refs[: scratch.shape[0]]
    relations, share = scratch.shape[1], scratch.shape[2]
    copies = []
    for m in reversed(range(len(shares))):
        scratch[m] = shares[m][...].astype(F32)
        panel = lax.axis_index("src") ^ m
        rows = pl.ds(pl.multiple_of(panel * share, share), share)
        copies.append(
            pltpu.make_async_copy(
                scratch.at[m],
                out.at[pl.ds(first_relation, relations), rows, :],
                sems.at[m],
            )
        )
        copies[-1].start()
    for copy in copies:
        copy.wait()


def spread(first_relation, shares, total, so_far):
    scratch = jax.ShapeDtypeStruct((len(shares), *shares[0].shape), F32)
    return pl.pallas_call(
        functools.partial(spread_kernel, first_relation),
        out_shape=total,
        in_specs=[WHOLE] * len(shares) + [ANYWHERE] * len(so_far),
        out_specs=ANYWHERE,
        scratch_shapes=[
            pltpu.VMEM(scratch.shape, F32),
            pltpu.SemaphoreType.DMA((len(shares),)),
        ],
        input_output_aliases={len(shares): 0} if so_far else {},
        compiler_params=vmem_for(scratch, *shares),
        name="spread",
    )(*shares, *so_far)


def sum_kernel(*refs):
    total = refs[0][...].astype(F32)
    for ref in refs[1:-1]:
        total = total + ref[...].astype(F32)
    refs[-1][...] = total.astype(refs[-1].dtype)


def summed(values, dtype=BF16):
    out = jax.ShapeDtypeStruct(values[0].shape, dtype)
    return pl.pallas_call(
        sum_kernel,
        out_shape=out,
        in_specs=[WHOLE] * len(values),
        out_specs=WHOLE,
        compiler_params=vmem_for(out, *values),
        name="sum",
    )(*values)


def silu_slope(pre_values):
    logistic = jax.nn.sigmoid(pre_values)
    return logistic * (1.0 + pre_values * (1.0 - logistic))


def exchange(pieces, axis):
    return [swap(pieces[m].astype(BF16), axis, m) for m in range(len(pieces) - 1, 0, -1)]


def added(own, arrived):
    total = own.astype(F32)
    for value in arrived:
        total = total + value.astype(F32)
    return total


def gather(value, axis):
    return [value] + [swap(value, axis, m) for m in range(1, lax.axis_size(axis))]


def local(source_feats, rel_weight, halo_pick, entry_index, entry_count, entry_values, cotangent):
    partitions, panels = lax.axis_size("dom"), lax.axis_size("src")
    groups = lax.axis_size("rel")
    tile = entry_values.shape[-1]
    own_rows, features = cotangent.shape
    relations = rel_weight.shape[0]
    values = entry_values.reshape(-1, tile, tile)
    table = entry_index.reshape(3, -1)
    entries = table.shape[1]
    count = entry_count.reshape(1)
    chosen = halo_pick.reshape(-1)
    places = jnp.stack([lax.axis_index(a) for a in ("dom", "src", "rel")]).astype(I32)
    targets = own_rows * panels * groups // tile
    direct = partitions <= 8
    share = features // panels
    bounds = tuple(sorted({0, relations // 2, relations}))
    chunks = len(bounds) - 1
    lists = (jax.ShapeDtypeStruct((entries + 1,), I32),) * chunks

    kept = (
        jax.ShapeDtypeStruct((panels, own_rows, features), F32),
        jax.ShapeDtypeStruct((panels, own_rows, features), BF16),
    )
    pre_sums = jax.ShapeDtypeStruct((targets + 1, tile, features), F32)
    if direct:
        halo = [h[None] for h in gather(source_feats, "dom")]
    else:
        halo = [lax.all_gather(source_feats, "dom", axis=0)]
    slots = sum(h.shape[0] for h in halo)
    combine = slots * relations <= entries
    near = partitions // 2
    projected = jax.ShapeDtypeStruct(
        ((near if direct else slots) * (relations if combine else 1), tile, features), BF16
    )
    cost = pl.CostEstimate(
        flops=4 * entries * tile * tile * features, bytes_accessed=values.size, transcendentals=0
    )
    if direct:
        before, others, *lists = pl.pallas_call(
            functools.partial(near_kernel, direct, tile, combine, near, bounds),
            out_shape=(pre_sums, lists[0], *lists),
            in_specs=[SCALARS] * 4 + [WHOLE] * (near + 2),
            out_specs=(WHOLE, SCALARS) + (SCALARS,) * chunks,
            scratch_shapes=[pltpu.VMEM(projected.shape, BF16), pltpu.SMEM((entries,), I32)],
            compiler_params=vmem_for(pre_sums, projected, *halo[:near], rel_weight, values),
            cost_estimate=cost,
            name="forward_near",
        )(places, chosen, table, count, *halo[:near], rel_weight, values)
        far = halo[near:]
        _, keep, send = pl.pallas_call(
            functools.partial(far_kernel, direct, tile, combine, near),
            out_shape=(pre_sums, *kept),
            in_specs=[SCALARS] * 4 + [WHOLE] * (len(far) + 3),
            out_specs=(WHOLE,) * 3,
            scratch_shapes=[pltpu.VMEM(projected.shape, BF16)],
            input_output_aliases={4 + len(far) + 2: 0},
            compiler_params=vmem_for(pre_sums, projected, *far, rel_weight, values, *kept),
            cost_estimate=cost,
            name="forward_far",
        )(places, chosen, table, others, *far, rel_weight, values, before)
    else:
        keep, send, *lists = pl.pallas_call(
            functools.partial(all_kernel, direct, tile, combine, bounds),
            out_shape=kept + lists,
            in_specs=[SCALARS] * 4 + [WHOLE] * (len(halo) + 2),
            out_specs=(WHOLE,) * 2 + (SCALARS,) * chunks,
            scratch_shapes=[
                pltpu.VMEM(pre_sums.shape, F32),
                pltpu.VMEM(projected.shape, BF16),
                pltpu.SMEM((entries,), I32),
            ],
            compiler_params=vmem_for(pre_sums, projected, *halo, rel_weight, values, *kept),
            cost_estimate=cost,
            name="forward_all",
        )(places, chosen, table, count, *halo, rel_weight, values)

    chip_sum = keep + swap(send, "rel", 1).astype(F32)
    leaving = [chip_sum[m] for m in range(panels)]
    leaving, values_then = lax.optimization_barrier((leaving, values))
    arrived = exchange(leaving, "src")

    sums = [
        jax.ShapeDtypeStruct(
            ((high - low) * slots + 1, tile, features)
            if combine
            else (high - low + 1, features, features),
            F32,
        )
        for low, high in zip(bounds, bounds[1:])
    ]
    turned = (
        jax.ShapeDtypeStruct(values.shape, BF16),
        jax.ShapeDtypeStruct((features, slots * tile), BF16),
    )
    prepared = pl.pallas_call(
        functools.partial(turn_kernel, direct, tile, len(halo), panels),
        out_shape=(*turned, *sums),
        in_specs=[SCALARS] * 2 + [WHOLE] * (len(halo) + 1),
        out_specs=(WHOLE,) * (2 + chunks),
        scratch_shapes=[pltpu.VMEM((features, tile), F32)],
        compiler_params=vmem_for(*turned, *sums, values, *halo),
        cost_estimate=pl.CostEstimate(
            flops=0, bytes_accessed=4 * values.size, transcendentals=0
        ),
        name="turn",
    )(places, chosen, *halo, values_then)
    arrived, prepared = lax.optimization_barrier((arrived, prepared))
    block = jax.ShapeDtypeStruct((own_rows, features), BF16)
    if len(arrived) == 3:
        local_grad = pl.pallas_call(
            grad_kernel,
            out_shape=block,
            in_specs=[WHOLE] * 5,
            out_specs=WHOLE,
            compiler_params=vmem_for(leaving[0], block, block, block, block, block),
            name="grad",
        )(leaving[0], *arrived, cotangent)
    else:
        local_grad = cotangent.astype(F32) * silu_slope(added(leaving[0], arrived))
        local_grad = local_grad.astype(BF16)
    out_feats = jax.nn.silu(added(leaving[0], arrived)).astype(BF16)

    core_grads = gather(local_grad, "src")
    other_grads = [swap(value, "rel", 1) for value in core_grads]

    by_target = jax.ShapeDtypeStruct((targets, tile, features), BF16)
    grads = pl.pallas_call(
        functools.partial(collect_kernel, tile),
        out_shape=by_target,
        in_specs=[WHOLE] * (2 * panels),
        out_specs=WHOLE,
        compiler_params=vmem_for(by_target, by_target),
        name="collect",
    )(*core_grads, *other_grads)

    total = jax.ShapeDtypeStruct((relations, features, features), F32)
    panel_sums, pieces, done = [], [], []
    for c in range(chunks):
        own_share = jax.ShapeDtypeStruct((bounds[c + 1] - bounds[c], share, features), F32)
        sent_share = jax.ShapeDtypeStruct(own_share.shape, BF16)
        *shares, _ = pl.pallas_call(
            functools.partial(weight_kernel, direct, tile, bounds[c], combine),
            out_shape=(own_share,) + (sent_share,) * (panels - 1) + (sums[c],),
            in_specs=[SCALARS] * 3 + [WHOLE] * 4,
            out_specs=(WHOLE,) * (panels + 1),
            input_output_aliases={6: panels},
            compiler_params=vmem_for(*(own_share,) * panels, sums[c], by_target, *turned),
            name="weight_terms",
        )(places, table, lists[c], *prepared[:2], grads, prepared[2 + c])
        panel_sums.append(
            summed([shares[0]] + exchange(shares, "src"), BF16 if direct else F32)
        )
    for panel_sum in panel_sums:
        if direct:
            mask = 1
            while mask < partitions:
                panel_sum = summed([panel_sum, swap(panel_sum, "dom", mask)])
                mask *= 2
        else:
            panel_sum = lax.psum(panel_sum, "dom").astype(BF16)
        pieces.append(gather(panel_sum, "src"))
    for c in range(chunks):
        done = [spread(bounds[c], pieces[c], total, done)]
    grad_rel = done[0]
    return (out_feats, grad_rel)


def solution(mesh):
    return jax.shard_map(
        local,
        mesh=mesh,
        in_specs=(
            P(("dom", "src", "rel"), None),
            P("rel", None, None),
            P("dom", "src", "rel", None),
            P("dom", "src", "rel", None, None),
            P("dom", "src", "rel"),
            P("dom", "src", "rel", None, None, None),
            P(("dom", "src", "rel"), None),
        ),
        out_specs=(P(("dom", "src", "rel"), None), P("rel", None, None)),
        check_vma=False,
    )
```

```python
import functools
import math

import jax
import jax.numpy as jnp
from jax import lax
from jax.experimental import pallas as pl
from jax.experimental.pallas import tpu as pltpu
from jax.sharding import PartitionSpec as P

F32, BF16, I32 = jnp.float32, jnp.bfloat16, jnp.int32
WHOLE = pl.BlockSpec(memory_space=pltpu.VMEM)
SCALARS = pl.BlockSpec(memory_space=pltpu.SMEM)
ANYWHERE = pl.BlockSpec(memory_space=pl.ANY)
UNROLL = 16


def vmem_for(*arrays):
    held = sum(math.prod(a.shape) * jnp.dtype(a.dtype).itemsize for a in arrays)
    return pltpu.CompilerParams(vmem_limit_bytes=held + held // 8 + 3 * 1024 * 1024)


def partner_pairs(size, mask):
    return [(i, i ^ mask) for i in range(size)]


def swap(value, axis, mask):
    return lax.ppermute(value, axis, partner_pairs(lax.axis_size(axis), mask))


def here():
    return [lax.axis_index(axis) for axis in ("dom", "src", "rel")]


def slot_of(places, partition, masked):
    return partition ^ places[0] if masked else partition


def packed(entries, targets, e, target, place):
    bits = (entries - 1).bit_length()
    return e | (target << bits) | (place << (bits + (targets - 1).bit_length()))


def unpacked(entries, targets, code):
    bits, more = (entries - 1).bit_length(), (targets - 1).bit_length()
    return code & ((1 << bits) - 1), (code >> bits) & ((1 << more) - 1), code >> (bits + more)


def for_entries(total, body):
    def step(i, carry):
        body([(jnp.minimum(i * UNROLL + u, total - 1), i * UNROLL + u < total) for u in range(UNROLL)])
        return carry

    lax.fori_loop(0, (total + UNROLL - 1) // UNROLL, step, 0)


def halo_block(first_block, halo_refs, i, tile):
    per_call = halo_refs[0].shape[0]
    rows = pl.ds(pl.multiple_of(first_block * tile, tile), tile)
    return halo_refs[i // per_call][i % per_call, rows, :]


def prepare_kernel(masked, combine, slot_bounds, bounds, targets, chosen, table, count, *refs):
    values, weight, values_here, weight_here, values_turned = refs[:5]
    by_slot = refs[5 : 4 + len(slot_bounds)]
    by_relation = refs[4 + len(slot_bounds) : 3 + len(slot_bounds) + len(bounds)]
    zeros, sems = refs[3 + len(slot_bounds) + len(bounds) : -1], refs[-1]
    entries, relations = values.shape[0], weight.shape[0]
    parts = sems.shape[0] - 1
    batch = entries // parts
    copies = [
        pltpu.make_async_copy(
            values.at[pl.ds(i * batch, batch)], values_here.at[pl.ds(i * batch, batch)], sems.at[i]
        )
        for i in range(parts)
    ]
    copies.append(pltpu.make_async_copy(weight, weight_here, sems.at[parts]))
    for copy in copies:
        copy.start()
    for each in zeros:
        each[...] = jnp.zeros_like(each)
    places = here()
    slots = slot_bounds[-1]

    def put(e, found):
        target, relation = table[0, e], table[2, e]
        slot = slot_of(places, table[1, e], masked)
        now = []
        for listed, low, high in zip(by_slot, slot_bounds, slot_bounds[1:]):
            place = (slot - low) * relations + relation
            listed[found[len(now)]] = packed(entries, targets, e, target, place)
            now.append((slot >= low) & (slot < high))
        for listed, low, high in zip(by_relation, bounds, bounds[1:]):
            place = (relation - low) * slots + slot
            listed[found[len(now)]] = packed(entries, targets, e, target, place)
            now.append((relation >= low) & (relation < high))
        return tuple(f + n.astype(I32) for f, n in zip(found, now))

    lists = (*by_slot, *by_relation)
    found = lax.fori_loop(0, count[0], put, (jnp.int32(0),) * len(lists))
    for listed, number in zip(lists, found):
        listed[entries] = number
    for listed, low, high in zip(by_slot, slot_bounds, slot_bounds[1:]):
        for i in range(low, high):
            listed[entries + 1 + i - low] = chosen[slot_of(places, i, masked)]

    for i, copy in enumerate(copies):
        copy.wait()
        if i < parts:

            def turn(j, carry):
                values_turned[i * batch + 2 * j] = values_here[i * batch + 2 * j].T
                values_turned[i * batch + 2 * j + 1] = values_here[i * batch + 2 * j + 1].T
                return carry

            lax.fori_loop(0, batch // 2, turn, 0, unroll=4)


def forward_kernel(tile, combine, halo_count, last, order, *refs):
    halo_refs, refs = refs[:halo_count], refs[halo_count:]
    weight, values, pre, outs, projected = refs[0], refs[1], refs[3], refs[4:-1], refs[-1]
    entries = values.shape[0]
    slots = halo_count * halo_refs[0].shape[0]
    firsts = [order[entries + 1 + i] for i in range(slots)]
    project(tile, combine, firsts, halo_refs, weight, projected)
    add_entries(combine, values, weight, projected, order, order[entries], pre)
    if last:
        hand_out(tile, here(), pre, outs)


def project(tile, combine, firsts, halo_refs, weight, projected):
    relations = weight.shape[0]
    blocks = [halo_block(first, halo_refs, i, tile) for i, first in enumerate(firsts)]
    if not combine:
        for i, block in enumerate(blocks):
            projected[i] = block
        return
    stacked = jnp.concatenate(blocks, axis=0)
    for r in range(relations):
        product = jnp.dot(stacked, weight[r], preferred_element_type=F32).astype(BF16)
        for i in range(len(blocks)):
            projected[i * relations + r] = product[i * tile : (i + 1) * tile]


def add_entries(combine, values, weight, projected, order, total, pre):
    entries, relations, spare = values.shape[0], weight.shape[0], pre.shape[0] - 1

    def body(positions):
        terms = []
        for position, real in positions:
            e, target, place = unpacked(entries, spare, order[position])
            if combine:
                term = jnp.dot(values[e], projected[place], preferred_element_type=F32)
            else:
                message = jnp.dot(
                    values[e], projected[place // relations], preferred_element_type=F32
                )
                term = jnp.dot(
                    message.astype(BF16), weight[place % relations], preferred_element_type=F32
                )
            terms.append((jnp.where(real, target, spare), term))
        for target, term in terms:
            pre[target] = pre[target] + term

    for_entries(total, body)


def hand_out(tile, places, pre, outs):
    keeps, sends = outs[:-2], outs[-2:]
    panels, per_owner = len(keeps), keeps[0].shape[0] // tile
    groups = (pre.shape[0] - 1) // (panels * per_owner)
    for distance in reversed(range(panels)):
        panel = places[1] ^ distance
        for part in range(per_owner):
            rows = pl.ds(part * tile, tile)
            mine = (panel * groups + places[2]) * per_owner + part
            other = (panel * groups + (places[2] ^ 1)) * per_owner + part
            if distance == panels - 1:
                sends[0][rows, :] = pre[other].astype(BF16)
            else:
                sends[1][distance, rows, :] = pre[other].astype(BF16)
            keeps[distance][rows, :] = pre[mine]


def chip_kernel(*refs):
    count = (len(refs) - 1) // 2
    keeps, arrived, outs = refs[:count], refs[count], refs[count + 1 :]
    for m in range(count):
        outs[m][...] = (keeps[m][...] + arrived[m].astype(F32)).astype(outs[m].dtype)


def grad_kernel(own, first, second, third, cotangent, grad):
    pre = own[...] + first[...].astype(F32) + second[...].astype(F32) + third[...].astype(F32)
    grad[...] = (cotangent[...].astype(F32) * silu_slope(pre)).astype(BF16)


def turn_kernel(masked, tile, panels, chosen, *refs):
    halo_refs, halo_turned, scratch = refs[:-2], refs[-2], refs[-1]
    places = here()
    share = scratch.shape[0] // panels
    for slot in range(len(halo_refs) * halo_refs[0].shape[0]):
        block = halo_block(chosen[slot_of(places, slot, masked)], halo_refs, slot, tile)
        scratch[...] = block.astype(F32).T
        for m in range(panels):
            start = pl.multiple_of((places[1] ^ m) * share, share)
            halo_turned[pl.ds(m * share, share), pl.ds(slot * tile, tile)] = (
                scratch[pl.ds(start, share), :].astype(BF16)
            )


def collect_kernel(tile, *refs):
    grad_refs, grads = refs[:-1], refs[-1]
    panels = len(grad_refs) // 2
    per_owner = grad_refs[0].shape[0] // tile
    for g in range(2):
        for m in range(panels):
            owner = (lax.axis_index("src") ^ m) * 2 + (lax.axis_index("rel") ^ g)
            for part in range(per_owner):
                grads[owner * per_owner + part] = grad_refs[g * panels + m][
                    pl.ds(part * tile, tile), :
                ]


def weight_kernel(tile, combine, listed, *refs):
    values_turned, halo_turned, grads = refs[:3]
    outs, sums = refs[4:-1], refs[-1]
    features = halo_turned.shape[0]
    slots = halo_turned.shape[1] // tile
    relations, share = outs[0].shape[0], outs[0].shape[1]
    entries, targets, spare = values_turned.shape[0], grads.shape[0], sums.shape[0] - 1

    def body(positions):
        terms = []
        for position, real in positions:
            e, target, place = unpacked(entries, targets, listed[position])
            term = jnp.dot(values_turned[e], grads[target], preferred_element_type=F32)
            if not combine:
                columns = pl.ds(pl.multiple_of(place % slots * tile, tile), tile)
                term = jnp.dot(
                    halo_turned[:, columns], term.astype(BF16), preferred_element_type=F32
                )
                place = place // slots
            terms.append((jnp.where(real, place, spare), term))
        for place, term in terms:
            sums[place] = sums[place] + term

    for_entries(listed[entries], body)
    for r in range(relations):
        if combine:
            stacked = sums[r * slots : (r + 1) * slots].reshape(slots * tile, features)
            grad = jnp.dot(halo_turned[...], stacked.astype(BF16), preferred_element_type=F32)
        else:
            grad = sums[r]
        for m, out in enumerate(outs):
            out[r] = grad[m * share : (m + 1) * share].astype(out.dtype)


def spread_kernel(first_relation, *refs):
    out, scratch, sems = refs[-3:]
    shares = refs[: scratch.shape[0]]
    relations, share = scratch.shape[1], scratch.shape[2]
    copies = []
    for m in reversed(range(len(shares))):
        scratch[m] = shares[m][...].astype(F32)
        panel = lax.axis_index("src") ^ m
        rows = pl.ds(pl.multiple_of(panel * share, share), share)
        copies.append(
            pltpu.make_async_copy(
                scratch.at[m],
                out.at[pl.ds(first_relation, relations), rows, :],
                sems.at[m],
            )
        )
        copies[-1].start()
    for copy in copies:
        copy.wait()


def spread(first_relation, shares, total, so_far):
    scratch = jax.ShapeDtypeStruct((len(shares), *shares[0].shape), F32)
    return pl.pallas_call(
        functools.partial(spread_kernel, first_relation),
        out_shape=total,
        in_specs=[WHOLE] * len(shares) + [ANYWHERE] * len(so_far),
        out_specs=ANYWHERE,
        scratch_shapes=[
            pltpu.VMEM(scratch.shape, F32),
            pltpu.SemaphoreType.DMA((len(shares),)),
        ],
        input_output_aliases={len(shares): 0} if so_far else {},
        compiler_params=vmem_for(scratch, *shares),
        name="spread",
    )(*shares, *so_far)


def sum_kernel(*refs):
    total = refs[0][...].astype(F32)
    for ref in refs[1:-1]:
        total = total + ref[...].astype(F32)
    refs[-1][...] = total.astype(refs[-1].dtype)


def summed(values, dtype=BF16):
    out = jax.ShapeDtypeStruct(values[0].shape, dtype)
    return pl.pallas_call(
        sum_kernel,
        out_shape=out,
        in_specs=[WHOLE] * len(values),
        out_specs=WHOLE,
        compiler_params=vmem_for(out, *values),
        name="sum",
    )(*values)


def silu_slope(pre_values):
    logistic = jax.nn.sigmoid(pre_values)
    return logistic * (1.0 + pre_values * (1.0 - logistic))


def exchange(pieces, axis):
    return [swap(pieces[m].astype(BF16), axis, m) for m in range(len(pieces) - 1, 0, -1)]


def added(own, arrived):
    total = own.astype(F32)
    for value in arrived:
        total = total + value.astype(F32)
    return total


def gather(value, axis):
    return [value] + [swap(value, axis, m) for m in range(1, lax.axis_size(axis))]


def local(source_feats, rel_weight, halo_pick, entry_index, entry_count, entry_values, cotangent):
    partitions, panels = lax.axis_size("dom"), lax.axis_size("src")
    groups = lax.axis_size("rel")
    tile = entry_values.shape[-1]
    own_rows, features = cotangent.shape
    relations = rel_weight.shape[0]
    values = entry_values.reshape(-1, tile, tile)
    table = entry_index.reshape(3, -1)
    entries = table.shape[1]
    count = entry_count.reshape(1)
    chosen = halo_pick.reshape(-1)
    targets = own_rows * panels * groups // tile
    direct = partitions <= 8
    share = features // panels
    bounds = tuple(sorted({0, relations // 2, relations}))
    chunks = len(bounds) - 1

    panel_f32 = jax.ShapeDtypeStruct((own_rows, features), F32)
    panel_bf16 = jax.ShapeDtypeStruct((own_rows, features), BF16)
    kept = (panel_f32,) * panels + (
        panel_bf16,
        jax.ShapeDtypeStruct((panels - 1, own_rows, features), BF16),
    )
    pre_sums = jax.ShapeDtypeStruct((targets + 1, tile, features), F32)
    if direct:
        halo = [h[None] for h in gather(source_feats, "dom")]
    else:
        halo = [lax.all_gather(source_feats, "dom", axis=0)]
    slots = sum(h.shape[0] for h in halo)
    combine = slots * relations <= entries
    near = partitions // 2
    slot_bounds = (0, near, slots) if direct else (0, slots)
    sums = [
        jax.ShapeDtypeStruct(
            ((high - low) * slots + 1, tile, features)
            if combine
            else (high - low + 1, features, features),
            F32,
        )
        for low, high in zip(bounds, bounds[1:])
    ]
    listings = [
        jax.ShapeDtypeStruct((entries + 1 + high - low,), I32)
        for low, high in zip(slot_bounds, slot_bounds[1:])
    ] + [jax.ShapeDtypeStruct((entries + 1,), I32)] * chunks
    held = [jax.ShapeDtypeStruct(v.shape, BF16) for v in (values, rel_weight, values)]
    values, rel_weight, values_turned, *others = pl.pallas_call(
        functools.partial(prepare_kernel, direct, combine, slot_bounds, bounds, targets),
        out_shape=(*held, *listings, pre_sums, *sums),
        in_specs=[SCALARS] * 3 + [ANYWHERE] * 2,
        out_specs=(WHOLE,) * 3 + (SCALARS,) * len(listings) + (WHOLE,) * (1 + chunks),
        scratch_shapes=[pltpu.SemaphoreType.DMA((5,))],
        compiler_params=vmem_for(*held, pre_sums, *sums),
        cost_estimate=pl.CostEstimate(
            flops=0, bytes_accessed=6 * values.size, transcendentals=0
        ),
        name="prepare",
    )(chosen, table, count, values, rel_weight)
    listings, pre, sums_in = others[: len(listings)], others[len(listings)], others[-chunks:]
    lists = listings[-chunks:]

    for call, (low, high) in enumerate(zip(slot_bounds, slot_bounds[1:])):
        last = high == slots
        blocks = halo[low:high] if direct else halo
        projected = jax.ShapeDtypeStruct(
            ((high - low) * (relations if combine else 1), tile, features), BF16
        )
        outs = (pre_sums, *kept) if last else (pre_sums,)
        pre, *given = pl.pallas_call(
            functools.partial(forward_kernel, tile, combine, len(blocks), last),
            out_shape=outs,
            in_specs=[SCALARS] + [WHOLE] * (len(blocks) + 3),
            out_specs=(WHOLE,) * len(outs),
            scratch_shapes=[pltpu.VMEM(projected.shape, BF16)],
            input_output_aliases={3 + len(blocks): 0},
            compiler_params=vmem_for(*outs, projected, *blocks, rel_weight, values),
            cost_estimate=pl.CostEstimate(
                flops=4 * entries * tile * tile * features,
                bytes_accessed=values.size,
                transcendentals=0,
            ),
            name="forward",
        )(listings[call], *blocks, rel_weight, values, pre)

    *keeps, farthest, rest = given
    farthest = summed([keeps[-1], swap(farthest, "rel", 1)])
    nearer = (panel_f32,) + (panel_bf16,) * (panels - 2)
    leaving = pl.pallas_call(
        chip_kernel,
        out_shape=nearer,
        in_specs=[WHOLE] * panels,
        out_specs=(WHOLE,) * (panels - 1),
        compiler_params=vmem_for(*nearer, *keeps, rest),
        name="chip",
    )(*keeps[:-1], swap(rest, "rel", 1))
    leaving = [*leaving, farthest]
    leaving, chosen_then = lax.optimization_barrier((leaving, chosen))
    arrived = exchange(leaving, "src")
    halo_turned = jax.ShapeDtypeStruct((features, slots * tile), BF16)
    turned = (values, halo_turned)
    halo_turned = pl.pallas_call(
        functools.partial(turn_kernel, direct, tile, panels),
        out_shape=halo_turned,
        in_specs=[SCALARS] + [WHOLE] * len(halo),
        out_specs=WHOLE,
        scratch_shapes=[pltpu.VMEM((features, tile), F32)],
        compiler_params=vmem_for(halo_turned, halo_turned, *halo),
        cost_estimate=pl.CostEstimate(
            flops=0, bytes_accessed=4 * halo_turned.size, transcendentals=0
        ),
        name="turn",
    )(chosen_then, *halo)
    arrived, halo_turned = lax.optimization_barrier((arrived, halo_turned))
    block = jax.ShapeDtypeStruct((own_rows, features), BF16)
    if len(arrived) == 3:
        local_grad = pl.pallas_call(
            grad_kernel,
            out_shape=block,
            in_specs=[WHOLE] * 5,
            out_specs=WHOLE,
            compiler_params=vmem_for(leaving[0], block, block, block, block, block),
            name="grad",
        )(leaving[0], *arrived, cotangent)
    else:
        local_grad = cotangent.astype(F32) * silu_slope(added(leaving[0], arrived))
        local_grad = local_grad.astype(BF16)
    out_feats = jax.nn.silu(added(leaving[0], arrived)).astype(BF16)

    core_grads = gather(local_grad, "src")
    other_grads = [swap(value, "rel", 1) for value in core_grads]

    by_target = jax.ShapeDtypeStruct((targets, tile, features), BF16)
    grads = pl.pallas_call(
        functools.partial(collect_kernel, tile),
        out_shape=by_target,
        in_specs=[WHOLE] * (2 * panels),
        out_specs=WHOLE,
        compiler_params=vmem_for(by_target, by_target),
        name="collect",
    )(*core_grads, *other_grads)

    total = jax.ShapeDtypeStruct((relations, features, features), F32)
    panel_sums, pieces, done = [], [], []
    for c in range(chunks):
        own_share = jax.ShapeDtypeStruct((bounds[c + 1] - bounds[c], share, features), F32)
        sent_share = jax.ShapeDtypeStruct(own_share.shape, BF16)
        *shares, _ = pl.pallas_call(
            functools.partial(weight_kernel, tile, combine),
            out_shape=(own_share,) + (sent_share,) * (panels - 1) + (sums[c],),
            in_specs=[SCALARS] + [WHOLE] * 4,
            out_specs=(WHOLE,) * (panels + 1),
            input_output_aliases={4: panels},
            compiler_params=vmem_for(*(own_share,) * panels, sums[c], by_target, *turned),
            name="weight_terms",
        )(lists[c], values_turned, halo_turned, grads, sums_in[c])
        panel_sums.append(
            summed([shares[0]] + exchange(shares, "src"), BF16 if direct else F32)
        )
    for c, panel_sum in enumerate(panel_sums):
        if direct:
            masks = [1 << i for i in range(partitions.bit_length() - 1)]
            for mask in masks if c % 2 else reversed(masks):
                panel_sum = summed([panel_sum, swap(panel_sum, "dom", mask)])
        else:
            panel_sum = lax.psum(panel_sum, "dom").astype(BF16)
        pieces.append(gather(panel_sum, "src"))
    for c in range(chunks):
        done = [spread(bounds[c], pieces[c], total, done)]
    grad_rel = done[0]
    return (out_feats, grad_rel)


def solution(mesh):
    return jax.shard_map(
        local,
        mesh=mesh,
        in_specs=(
            P(("dom", "src", "rel"), None),
            P("rel", None, None),
            P("dom", "src", "rel", None),
            P("dom", "src", "rel", None, None),
            P("dom", "src", "rel"),
            P("dom", "src", "rel", None, None, None),
            P(("dom", "src", "rel"), None),
        ),
        out_specs=(P(("dom", "src", "rel"), None), P("rel", None, None)),
        check_vma=False,
    )
```

```python
import functools
import math

import jax
import jax.numpy as jnp
from jax import lax
from jax.experimental import pallas as pl
from jax.experimental.pallas import tpu as pltpu
from jax.sharding import PartitionSpec as P

F32, BF16, I32 = jnp.float32, jnp.bfloat16, jnp.int32
WHOLE = pl.BlockSpec(memory_space=pltpu.VMEM)
SCALARS = pl.BlockSpec(memory_space=pltpu.SMEM)
ANYWHERE = pl.BlockSpec(memory_space=pl.ANY)
UNROLL = 16


def vmem_for(*arrays):
    held = sum(math.prod(a.shape) * jnp.dtype(a.dtype).itemsize for a in arrays)
    return pltpu.CompilerParams(vmem_limit_bytes=held + held // 8 + 3 * 1024 * 1024)


def partner_pairs(size, mask):
    return [(i, i ^ mask) for i in range(size)]


def swap(value, axis, mask):
    return lax.ppermute(value, axis, partner_pairs(lax.axis_size(axis), mask))


def here():
    return [lax.axis_index(axis) for axis in ("dom", "src", "rel")]


def slot_of(places, partition, masked):
    return partition ^ places[0] if masked else partition


def packed(entries, targets, e, target, place):
    bits = (entries - 1).bit_length()
    return e | (target << bits) | (place << (bits + (targets - 1).bit_length()))


def unpacked(entries, targets, code):
    bits, more = (entries - 1).bit_length(), (targets - 1).bit_length()
    return code & ((1 << bits) - 1), (code >> bits) & ((1 << more) - 1), code >> (bits + more)


def for_entries(total, body):
    def step(i, carry):
        body([(jnp.minimum(i * UNROLL + u, total - 1), i * UNROLL + u < total) for u in range(UNROLL)])
        return carry

    lax.fori_loop(0, (total + UNROLL - 1) // UNROLL, step, 0)


def halo_block(first_block, halo_refs, i, tile):
    per_call = halo_refs[0].shape[0]
    rows = pl.ds(pl.multiple_of(first_block * tile, tile), tile)
    return halo_refs[i // per_call][i % per_call, rows, :]


def prepare_kernel(masked, owners, groups, bounds, targets, chosen, table, count, *refs):
    values, weight, values_here, weight_here = refs[:4]
    by_slot, refs = refs[4 : 4 + len(groups)], refs[4 + len(groups) :]
    by_relation, (pre, sems) = refs[: len(bounds) - 1], refs[len(bounds) - 1 :]
    entries, relations = values.shape[0], weight.shape[0]
    copies = [
        pltpu.make_async_copy(values, values_here, sems.at[0]),
        pltpu.make_async_copy(weight, weight_here, sems.at[1]),
    ]
    for copy in copies:
        copy.start()
    pre[...] = jnp.zeros_like(pre)
    places = here()
    cores, per_owner = owners
    slots = groups[-1][1]

    def put(e, found):
        target, relation = table[0, e], table[2, e]
        slot = slot_of(places, table[1, e], masked)
        own = (target >> (per_owner.bit_length() - 1)) & (cores - 1) == places[2]
        now = []
        for listed, (low, high, side) in zip(by_slot, groups):
            place = (slot - low) * relations + relation
            listed[found[len(now)]] = packed(entries, targets, e, target, place)
            inside = (slot >= low) & (slot < high)
            now.append(inside if side is None else inside & (own == side))
        for listed, low, high in zip(by_relation, bounds, bounds[1:]):
            place = (relation - low) * slots + slot
            listed[found[len(now)]] = packed(entries, targets, e, target, place)
            now.append((relation >= low) & (relation < high))
        return tuple(f + n.astype(I32) for f, n in zip(found, now))

    lists = (*by_slot, *by_relation)
    found = lax.fori_loop(0, count[0], put, (jnp.int32(0),) * len(lists))
    for listed, number in zip(lists, found):
        listed[entries] = number
    for listed, (low, high, _) in zip(by_slot, groups):
        for i in range(low, high):
            listed[entries + 1 + i - low] = chosen[slot_of(places, i, masked)]

    for copy in copies:
        copy.wait()


def near_kernel(tile, combine, order, *refs):
    *halo_refs, weight, values, before, pre, projected = refs
    entries = values.shape[0]
    firsts = [order[entries + 1 + i] for i in range(order.shape[0] - entries - 1)]
    project(tile, combine, firsts, halo_refs, weight, projected)
    add_entries(combine, values, weight, projected, order, order[entries], pre)


def theirs_kernel(tile, combine, owners, first, order, *refs):
    near_kernel(tile, combine, order, *refs[:-2])
    pre, sends = refs[-4], refs[-2:]
    panels = sends[1].shape[0] + 1
    others = [m for m in range(panels) if m != first]
    for out, distance in ((sends[0], first), *((sends[1].at[i], m) for i, m in enumerate(others))):
        for rows, block in blocks_of(tile, owners, here(), distance, 1):
            out[rows, :] = pre[block].astype(BF16)


def ours_kernel(tile, combine, owners, order, projected, weight, values, before, pre, *keeps):
    del before
    add_entries(combine, values, weight, projected, order, order[values.shape[0]], pre)
    for distance, keep in enumerate(keeps):
        for rows, block in blocks_of(tile, owners, here(), distance, 0):
            keep[rows, :] = pre[block]


def blocks_of(tile, owners, places, distance, other):
    cores, per_owner = owners
    owner = (places[1] ^ distance) * cores + (places[2] ^ other)
    return [(pl.ds(i * tile, tile), owner * per_owner + i) for i in range(per_owner)]


def project(tile, combine, firsts, halo_refs, weight, projected):
    relations = weight.shape[0]
    blocks = [halo_block(first, halo_refs, i, tile) for i, first in enumerate(firsts)]
    if not combine:
        for i, block in enumerate(blocks):
            projected[i] = block
        return
    stacked = jnp.concatenate(blocks, axis=0)
    for r in range(relations):
        product = jnp.dot(stacked, weight[r], preferred_element_type=F32).astype(BF16)
        for i in range(len(blocks)):
            projected[i * relations + r] = product[i * tile : (i + 1) * tile]


def add_entries(combine, values, weight, projected, order, total, pre):
    entries, relations, spare = values.shape[0], weight.shape[0], pre.shape[0] - 1

    def body(positions):
        terms = []
        for position, real in positions:
            e, target, place = unpacked(entries, spare, order[position])
            if combine:
                term = jnp.dot(values[e], projected[place], preferred_element_type=F32)
            else:
                message = jnp.dot(
                    values[e], projected[place // relations], preferred_element_type=F32
                )
                term = jnp.dot(
                    message.astype(BF16), weight[place % relations], preferred_element_type=F32
                )
            terms.append((jnp.where(real, target, spare), term))
        for target, term in terms:
            pre[target] = pre[target] + term

    for_entries(total, body)


def chip_kernel(*refs):
    count = (len(refs) - 1) // 2
    keeps, arrived, outs = refs[:count], refs[count], refs[count + 1 :]
    for m in range(count):
        outs[m][...] = (keeps[m][...] + arrived[m].astype(F32)).astype(outs[m].dtype)


def grad_kernel(own, first, second, third, cotangent, grad):
    pre = own[...] + first[...].astype(F32) + second[...].astype(F32) + third[...].astype(F32)
    grad[...] = (cotangent[...].astype(F32) * silu_slope(pre)).astype(BF16)


def turn_kernel(masked, tile, panels, halo_count, chosen, values, *refs):
    halo_refs, refs = refs[:halo_count], refs[halo_count:]
    values_turned, halo_turned, zeros, scratch = refs[0], refs[1], refs[2:-1], refs[-1]
    places = here()
    for each in zeros:
        each[...] = jnp.zeros_like(each)
    share = scratch.shape[0] // panels
    for slot in range(len(halo_refs) * halo_refs[0].shape[0]):
        block = halo_block(chosen[slot_of(places, slot, masked)], halo_refs, slot, tile)
        scratch[...] = block.astype(F32).T
        for m in range(panels):
            start = pl.multiple_of((places[1] ^ m) * share, share)
            halo_turned[pl.ds(m * share, share), pl.ds(slot * tile, tile)] = (
                scratch[pl.ds(start, share), :].astype(BF16)
            )

    batch = 8

    def step(i, carry):
        for u in range(batch):
            values_turned[i * batch + u] = values[i * batch + u].T
        return carry

    lax.fori_loop(0, values.shape[0] // batch, step, 0)


def collect_kernel(tile, *refs):
    grad_refs, grads = refs[:-1], refs[-1]
    panels = len(grad_refs) // 2
    per_owner = grad_refs[0].shape[0] // tile
    for g in range(2):
        for m in range(panels):
            owner = (lax.axis_index("src") ^ m) * 2 + (lax.axis_index("rel") ^ g)
            for part in range(per_owner):
                grads[owner * per_owner + part] = grad_refs[g * panels + m][
                    pl.ds(part * tile, tile), :
                ]


def weight_kernel(tile, combine, listed, *refs):
    values_turned, halo_turned, grads = refs[:3]
    outs, sums = refs[4:-1], refs[-1]
    features = halo_turned.shape[0]
    slots = halo_turned.shape[1] // tile
    relations, share = outs[0].shape[0], outs[0].shape[1]
    entries, targets, spare = values_turned.shape[0], grads.shape[0], sums.shape[0] - 1

    def body(positions):
        terms = []
        for position, real in positions:
            e, target, place = unpacked(entries, targets, listed[position])
            term = jnp.dot(values_turned[e], grads[target], preferred_element_type=F32)
            if not combine:
                columns = pl.ds(pl.multiple_of(place % slots * tile, tile), tile)
                term = jnp.dot(
                    halo_turned[:, columns], term.astype(BF16), preferred_element_type=F32
                )
                place = place // slots
            terms.append((jnp.where(real, place, spare), term))
        for place, term in terms:
            sums[place] = sums[place] + term

    for_entries(listed[entries], body)
    for r in range(relations):
        if combine:
            stacked = sums[r * slots : (r + 1) * slots].reshape(slots * tile, features)
            grad = jnp.dot(halo_turned[...], stacked.astype(BF16), preferred_element_type=F32)
        else:
            grad = sums[r]
        for m, out in enumerate(outs):
            out[r] = grad[m * share : (m + 1) * share].astype(out.dtype)


def spread_kernel(first_relation, *refs):
    out, scratch, sems = refs[-3:]
    shares = refs[: scratch.shape[0]]
    relations, share = scratch.shape[1], scratch.shape[2]
    copies = []
    for m in reversed(range(len(shares))):
        scratch[m] = shares[m][...].astype(F32)
        panel = lax.axis_index("src") ^ m
        rows = pl.ds(pl.multiple_of(panel * share, share), share)
        copies.append(
            pltpu.make_async_copy(
                scratch.at[m],
                out.at[pl.ds(first_relation, relations), rows, :],
                sems.at[m],
            )
        )
        copies[-1].start()
    for copy in copies:
        copy.wait()


def spread(first_relation, shares, total, so_far):
    scratch = jax.ShapeDtypeStruct((len(shares), *shares[0].shape), F32)
    return pl.pallas_call(
        functools.partial(spread_kernel, first_relation),
        out_shape=total,
        in_specs=[WHOLE] * len(shares) + [ANYWHERE] * len(so_far),
        out_specs=ANYWHERE,
        scratch_shapes=[
            pltpu.VMEM(scratch.shape, F32),
            pltpu.SemaphoreType.DMA((len(shares),)),
        ],
        input_output_aliases={len(shares): 0} if so_far else {},
        compiler_params=vmem_for(scratch, *shares),
        name="spread",
    )(*shares, *so_far)


def sum_kernel(*refs):
    total = refs[0][...].astype(F32)
    for ref in refs[1:-1]:
        total = total + ref[...].astype(F32)
    refs[-1][...] = total.astype(refs[-1].dtype)


def summed(values, dtype=BF16):
    out = jax.ShapeDtypeStruct(values[0].shape, dtype)
    return pl.pallas_call(
        sum_kernel,
        out_shape=out,
        in_specs=[WHOLE] * len(values),
        out_specs=WHOLE,
        compiler_params=vmem_for(out, *values),
        name="sum",
    )(*values)


def silu_slope(pre_values):
    logistic = jax.nn.sigmoid(pre_values)
    return logistic * (1.0 + pre_values * (1.0 - logistic))


def exchange(pieces, axis):
    return [swap(pieces[m].astype(BF16), axis, m) for m in range(len(pieces) - 1, 0, -1)]


def added(own, arrived):
    total = own.astype(F32)
    for value in arrived:
        total = total + value.astype(F32)
    return total


def gather(value, axis):
    return [value] + [swap(value, axis, m) for m in range(1, lax.axis_size(axis))]


def local(source_feats, rel_weight, halo_pick, entry_index, entry_count, entry_values, cotangent):
    partitions, panels = lax.axis_size("dom"), lax.axis_size("src")
    groups = lax.axis_size("rel")
    tile = entry_values.shape[-1]
    own_rows, features = cotangent.shape
    relations = rel_weight.shape[0]
    values = entry_values.reshape(-1, tile, tile)
    table = entry_index.reshape(3, -1)
    entries = table.shape[1]
    count = entry_count.reshape(1)
    chosen = halo_pick.reshape(-1)
    targets = own_rows * panels * groups // tile
    direct = partitions <= 8
    share = features // panels
    bounds = tuple(sorted({0, relations // 2, relations}))
    chunks = len(bounds) - 1

    panel_f32 = jax.ShapeDtypeStruct((own_rows, features), F32)
    panel_bf16 = jax.ShapeDtypeStruct((own_rows, features), BF16)
    pre_sums = jax.ShapeDtypeStruct((targets + 1, tile, features), F32)
    if direct:
        halo = [h[None] for h in gather(source_feats, "dom")]
    else:
        halo = [lax.all_gather(source_feats, "dom", axis=0)]
    slots = sum(h.shape[0] for h in halo)
    combine = slots * relations <= entries
    near = partitions // 2
    owners = groups, own_rows // tile
    start = near if direct else 0
    slot_groups = ((0, near, None),) * direct + ((start, slots, False), (start, slots, True))
    sums = [
        jax.ShapeDtypeStruct(
            ((high - low) * slots + 1, tile, features)
            if combine
            else (high - low + 1, features, features),
            F32,
        )
        for low, high in zip(bounds, bounds[1:])
    ]
    listings = [
        jax.ShapeDtypeStruct((entries + 1 + high - low,), I32)
        for low, high, _ in slot_groups
    ] + [jax.ShapeDtypeStruct((entries + 1,), I32)] * chunks
    held = [jax.ShapeDtypeStruct(v.shape, BF16) for v in (values, rel_weight)]
    values, rel_weight, *listings, pre = pl.pallas_call(
        functools.partial(prepare_kernel, direct, owners, slot_groups, bounds, targets),
        out_shape=(*held, *listings, pre_sums),
        in_specs=[SCALARS] * 3 + [ANYWHERE] * 2,
        out_specs=(WHOLE,) * 2 + (SCALARS,) * len(listings) + (WHOLE,),
        scratch_shapes=[pltpu.SemaphoreType.DMA((2,))],
        compiler_params=vmem_for(*held, pre_sums),
        cost_estimate=pl.CostEstimate(
            flops=0, bytes_accessed=4 * values.size, transcendentals=0
        ),
        name="prepare",
    )(chosen, table, count, values, rel_weight)
    lists = listings[-chunks:]

    first = 1 if panels > 1 else 0
    sends = (panel_bf16, jax.ShapeDtypeStruct((panels - 1, own_rows, features), BF16))
    cost = pl.CostEstimate(
        flops=4 * entries * tile * tile * features, bytes_accessed=values.size, transcendentals=0
    )
    for call, (low, high, _) in enumerate(slot_groups[:-1]):
        last = call == len(slot_groups) - 2
        blocks = halo[low:high] if direct else halo
        projected = jax.ShapeDtypeStruct(
            ((high - low) * (relations if combine else 1), tile, features), BF16
        )
        kernel = functools.partial(near_kernel, tile, combine)
        if last:
            kernel = functools.partial(theirs_kernel, tile, combine, owners, first)
        outs = (pre_sums, projected, *sends) if last else (pre_sums,)
        pre, *given = pl.pallas_call(
            kernel,
            out_shape=outs,
            in_specs=[SCALARS] + [WHOLE] * (len(blocks) + 3),
            out_specs=(WHOLE,) * len(outs),
            scratch_shapes=[] if last else [pltpu.VMEM(projected.shape, BF16)],
            input_output_aliases={3 + len(blocks): 0},
            compiler_params=vmem_for(*outs, projected, *blocks, rel_weight, values),
            cost_estimate=cost,
            name="forward",
        )(listings[call], *blocks, rel_weight, values, pre)
    projected, *given = given
    _, *keeps = pl.pallas_call(
        functools.partial(ours_kernel, tile, combine, owners),
        out_shape=(pre_sums,) + (panel_f32,) * panels,
        in_specs=[SCALARS] + [WHOLE] * 4,
        out_specs=(WHOLE,) * (1 + panels),
        input_output_aliases={4: 0},
        compiler_params=vmem_for(pre_sums, pre_sums, projected, rel_weight, values),
        cost_estimate=cost,
        name="forward_ours",
    )(listings[len(slot_groups) - 1], projected, rel_weight, values, pre)
    first_sum = summed([keeps[first], swap(given[0], "rel", 1)])
    rest = [m for m in range(panels) if m != first]
    rest_sums = (panel_f32,) + (panel_bf16,) * (panels - 2)
    leaving = pl.pallas_call(
        chip_kernel,
        out_shape=rest_sums,
        in_specs=[WHOLE] * panels,
        out_specs=(WHOLE,) * (panels - 1),
        compiler_params=vmem_for(*rest_sums, *keeps, sends[1]),
        name="chip",
    )(*(keeps[m] for m in rest), swap(given[1], "rel", 1))
    leaving = [leaving[0], first_sum, *leaving[1:]]
    leaving, chosen_then = lax.optimization_barrier((leaving, chosen))
    arrived = exchange(leaving, "src")
    turned = (held[0], jax.ShapeDtypeStruct((features, slots * tile), BF16))
    prepared = pl.pallas_call(
        functools.partial(turn_kernel, direct, tile, panels, len(halo)),
        out_shape=(*turned, *sums),
        in_specs=[SCALARS] + [WHOLE] * (1 + len(halo)),
        out_specs=(WHOLE,) * (2 + chunks),
        scratch_shapes=[pltpu.VMEM((features, tile), F32)],
        compiler_params=vmem_for(*turned, *sums, values, *halo),
        cost_estimate=pl.CostEstimate(
            flops=0, bytes_accessed=4 * values.size, transcendentals=0
        ),
        name="turn",
    )(chosen_then, values, *halo)
    arrived, prepared = lax.optimization_barrier((arrived, prepared))
    block = jax.ShapeDtypeStruct((own_rows, features), BF16)
    if len(arrived) == 3:
        local_grad = pl.pallas_call(
            grad_kernel,
            out_shape=block,
            in_specs=[WHOLE] * 5,
            out_specs=WHOLE,
            compiler_params=vmem_for(leaving[0], block, block, block, block, block),
            name="grad",
        )(leaving[0], *arrived, cotangent)
    else:
        local_grad = cotangent.astype(F32) * silu_slope(added(leaving[0], arrived))
        local_grad = local_grad.astype(BF16)
    out_feats = jax.nn.silu(added(leaving[0], arrived)).astype(BF16)

    core_grads = gather(local_grad, "src")
    other_grads = [swap(value, "rel", 1) for value in core_grads]

    by_target = jax.ShapeDtypeStruct((targets, tile, features), BF16)
    grads = pl.pallas_call(
        functools.partial(collect_kernel, tile),
        out_shape=by_target,
        in_specs=[WHOLE] * (2 * panels),
        out_specs=WHOLE,
        compiler_params=vmem_for(by_target, by_target),
        name="collect",
    )(*core_grads, *other_grads)

    total = jax.ShapeDtypeStruct((relations, features, features), F32)
    panel_sums, pieces, done = [], [], []
    for c in range(chunks):
        own_share = jax.ShapeDtypeStruct((bounds[c + 1] - bounds[c], share, features), F32)
        sent_share = jax.ShapeDtypeStruct(own_share.shape, BF16)
        *shares, _ = pl.pallas_call(
            functools.partial(weight_kernel, tile, combine),
            out_shape=(own_share,) + (sent_share,) * (panels - 1) + (sums[c],),
            in_specs=[SCALARS] + [WHOLE] * 4,
            out_specs=(WHOLE,) * (panels + 1),
            input_output_aliases={4: panels},
            compiler_params=vmem_for(*(own_share,) * panels, sums[c], by_target, *turned),
            name="weight_terms",
        )(lists[c], *prepared[:2], grads, prepared[2 + c])
        panel_sums.append(
            summed([shares[0]] + exchange(shares, "src"), BF16 if direct else F32)
        )
    for c, panel_sum in enumerate(panel_sums):
        if direct:
            masks = [1 << i for i in range(partitions.bit_length() - 1)]
            for mask in masks if c % 2 else reversed(masks):
                panel_sum = summed([panel_sum, swap(panel_sum, "dom", mask)])
        else:
            panel_sum = lax.psum(panel_sum, "dom").astype(BF16)
        pieces.append(gather(panel_sum, "src"))
    for c in range(chunks):
        done = [spread(bounds[c], pieces[c], total, done)]
    grad_rel = done[0]
    return (out_feats, grad_rel)


def solution(mesh):
    return jax.shard_map(
        local,
        mesh=mesh,
        in_specs=(
            P(("dom", "src", "rel"), None),
            P("rel", None, None),
            P("dom", "src", "rel", None),
            P("dom", "src", "rel", None, None),
            P("dom", "src", "rel"),
            P("dom", "src", "rel", None, None, None),
            P(("dom", "src", "rel"), None),
        ),
        out_specs=(P(("dom", "src", "rel"), None), P("rel", None, None)),
        check_vma=False,
    )
```

```python
import functools
import math

import jax
import jax.numpy as jnp
from jax import lax
from jax.experimental import pallas as pl
from jax.experimental.pallas import tpu as pltpu
from jax.sharding import PartitionSpec as P

F32, BF16, I32 = jnp.float32, jnp.bfloat16, jnp.int32
WHOLE = pl.BlockSpec(memory_space=pltpu.VMEM)
SCALARS = pl.BlockSpec(memory_space=pltpu.SMEM)
ANYWHERE = pl.BlockSpec(memory_space=pl.ANY)
UNROLL = 20


def vmem_for(*arrays):
    held = sum(math.prod(a.shape) * jnp.dtype(a.dtype).itemsize for a in arrays)
    return pltpu.CompilerParams(vmem_limit_bytes=held + held // 8 + 3 * 1024 * 1024)


def partner_pairs(size, mask):
    return [(i, i ^ mask) for i in range(size)]


def swap(value, axis, mask):
    return lax.ppermute(value, axis, partner_pairs(lax.axis_size(axis), mask))


def here():
    return [lax.axis_index(axis) for axis in ("dom", "src", "rel")]


def slot_of(places, partition, masked):
    return partition ^ places[0] if masked else partition


def packed(entries, targets, e, target, place):
    bits = (entries - 1).bit_length()
    return e | (target << bits) | (place << (bits + (targets - 1).bit_length()))


def unpacked(entries, targets, code):
    bits, more = (entries - 1).bit_length(), (targets - 1).bit_length()
    return code & ((1 << bits) - 1), (code >> bits) & ((1 << more) - 1), code >> (bits + more)


def for_entries(total, body):
    def step(i, carry):
        body([(jnp.minimum(i * UNROLL + u, total - 1), i * UNROLL + u < total) for u in range(UNROLL)])
        return carry

    lax.fori_loop(0, (total + UNROLL - 1) // UNROLL, step, 0)


def halo_block(first_block, halo_refs, i, tile):
    per_call = halo_refs[0].shape[0]
    rows = pl.ds(pl.multiple_of(first_block * tile, tile), tile)
    return halo_refs[i // per_call][i % per_call, rows, :]


def prepare_kernel(masked, owners, groups, bounds, targets, chosen, table, count, *refs):
    values, weight, values_here, weight_here = refs[:4]
    by_slot, refs = refs[4 : 4 + len(groups)], refs[4 + len(groups) :]
    by_relation, (pre, sems) = refs[: len(bounds) - 1], refs[len(bounds) - 1 :]
    entries, relations = values.shape[0], weight.shape[0]
    copies = [
        pltpu.make_async_copy(values, values_here, sems.at[0]),
        pltpu.make_async_copy(weight, weight_here, sems.at[1]),
    ]
    for copy in copies:
        copy.start()
    pre[...] = jnp.zeros_like(pre)
    places = here()
    cores, per_owner = owners
    slots = groups[-1][1]

    def put(e, found):
        target, relation = table[0, e], table[2, e]
        slot = slot_of(places, table[1, e], masked)
        own = (target >> (per_owner.bit_length() - 1)) & (cores - 1) == places[2]
        now = []
        for listed, (low, high, side) in zip(by_slot, groups):
            place = (slot - low) * relations + relation
            listed[found[len(now)]] = packed(entries, targets, e, target, place)
            inside = (slot >= low) & (slot < high)
            now.append(inside if side is None else inside & (own == side))
        for listed, low, high in zip(by_relation, bounds, bounds[1:]):
            place = (relation - low) * slots + slot
            listed[found[len(now)]] = packed(entries, targets, e, target, place)
            now.append((relation >= low) & (relation < high))
        return tuple(f + n.astype(I32) for f, n in zip(found, now))

    lists = (*by_slot, *by_relation)
    found = lax.fori_loop(0, count[0], put, (jnp.int32(0),) * len(lists))
    for listed, number in zip(lists, found):
        listed[entries] = number
    for listed, (low, high, _) in zip(by_slot, groups):
        for i in range(low, high):
            listed[entries + 1 + i - low] = chosen[slot_of(places, i, masked)]

    for copy in copies:
        copy.wait()


def near_kernel(tile, combine, order, *refs):
    *halo_refs, weight, values, before, pre, projected = refs
    entries = values.shape[0]
    firsts = [order[entries + 1 + i] for i in range(order.shape[0] - entries - 1)]
    project(tile, combine, firsts, halo_refs, weight, projected)
    add_entries(combine, values, weight, projected, order, order[entries], pre)


def theirs_kernel(tile, combine, owners, first, order, *refs):
    near_kernel(tile, combine, order, *refs[:-2])
    pre, sends = refs[-4], refs[-2:]
    panels = sends[1].shape[0] + 1
    others = [m for m in range(panels) if m != first]
    for out, distance in ((sends[0], first), *((sends[1].at[i], m) for i, m in enumerate(others))):
        for rows, block in blocks_of(tile, owners, here(), distance, 1):
            out[rows, :] = pre[block].astype(BF16)


def ours_kernel(tile, combine, owners, order, projected, weight, values, before, pre, *keeps):
    del before
    add_entries(combine, values, weight, projected, order, order[values.shape[0]], pre)
    for distance, keep in enumerate(keeps):
        for rows, block in blocks_of(tile, owners, here(), distance, 0):
            keep[rows, :] = pre[block]


def blocks_of(tile, owners, places, distance, other):
    cores, per_owner = owners
    owner = (places[1] ^ distance) * cores + (places[2] ^ other)
    return [(pl.ds(i * tile, tile), owner * per_owner + i) for i in range(per_owner)]


def halves(value):
    high = value.astype(BF16)
    return high, (value - high.astype(F32)).astype(BF16)


def project(tile, combine, firsts, halo_refs, weight, projected):
    relations = weight.shape[0]
    blocks = [halo_block(first, halo_refs, i, tile) for i, first in enumerate(firsts)]
    if not combine:
        for i, block in enumerate(blocks):
            projected[i] = block
        return
    stacked = jnp.concatenate(blocks, axis=0)
    for r in range(relations):
        high, low = halves(jnp.dot(stacked, weight[r], preferred_element_type=F32))
        for i in range(len(blocks)):
            rows = slice(i * tile, (i + 1) * tile)
            projected[i * relations + r, :tile, :] = high[rows]
            projected[i * relations + r, tile:, :] = low[rows]


def add_entries(combine, values, weight, projected, order, total, pre):
    entries, relations, spare = values.shape[0], weight.shape[0], pre.shape[0] - 1

    def body(positions):
        terms = []
        for position, real in positions:
            e, target, place = unpacked(entries, spare, order[position])
            if combine:
                twice = jnp.concatenate([values[e], values[e]], axis=1)
                term = jnp.dot(twice, projected[place], preferred_element_type=F32)
            else:
                message = jnp.dot(
                    values[e], projected[place // relations], preferred_element_type=F32
                )
                term = jnp.dot(
                    message.astype(BF16), weight[place % relations], preferred_element_type=F32
                )
            terms.append((jnp.where(real, target, spare), term))
        for target, term in terms:
            pre[target] = pre[target] + term

    for_entries(total, body)


def chip_kernel(*refs):
    count = (len(refs) - 1) // 2
    keeps, arrived, outs = refs[:count], refs[count], refs[count + 1 :]
    for m in range(count):
        outs[m][...] = (keeps[m][...] + arrived[m].astype(F32)).astype(outs[m].dtype)


def grad_kernel(own, first, second, third, cotangent, grad):
    pre = own[...] + first[...].astype(F32) + second[...].astype(F32) + third[...].astype(F32)
    grad[...] = (cotangent[...].astype(F32) * silu_slope(pre)).astype(BF16)


def turn_kernel(masked, tile, panels, halo_count, chosen, values, *refs):
    halo_refs, refs = refs[:halo_count], refs[halo_count:]
    values_turned, halo_turned, zeros, scratch = refs[0], refs[1], refs[2:-1], refs[-1]
    places = here()
    for each in zeros:
        each[...] = jnp.zeros_like(each)
    share = scratch.shape[0] // panels
    for slot in range(len(halo_refs) * halo_refs[0].shape[0]):
        block = halo_block(chosen[slot_of(places, slot, masked)], halo_refs, slot, tile)
        scratch[...] = block.astype(F32).T
        for m in range(panels):
            start = pl.multiple_of((places[1] ^ m) * share, share)
            halo_turned[pl.ds(m * share, share), pl.ds(slot * tile, tile)] = (
                scratch[pl.ds(start, share), :].astype(BF16)
            )

    batch = 8

    def step(i, carry):
        for u in range(batch):
            values_turned[i * batch + u] = values[i * batch + u].T
        return carry

    lax.fori_loop(0, values.shape[0] // batch, step, 0)


def collect_kernel(tile, *refs):
    grad_refs, grads = refs[:-1], refs[-1]
    panels = len(grad_refs) // 2
    per_owner = grad_refs[0].shape[0] // tile
    for g in range(2):
        for m in range(panels):
            owner = (lax.axis_index("src") ^ m) * 2 + (lax.axis_index("rel") ^ g)
            for part in range(per_owner):
                grads[owner * per_owner + part] = grad_refs[g * panels + m][
                    pl.ds(part * tile, tile), :
                ]


def weight_kernel(tile, combine, listed, *refs):
    values_turned, halo_turned, grads = refs[:3]
    outs, sums = refs[4:-1], refs[-1]
    features = halo_turned.shape[0]
    slots = halo_turned.shape[1] // tile
    relations, share = outs[0].shape[0], outs[0].shape[1]
    entries, targets, spare = values_turned.shape[0], grads.shape[0], sums.shape[0] - 1

    def body(positions):
        terms = []
        for position, real in positions:
            e, target, place = unpacked(entries, targets, listed[position])
            term = jnp.dot(values_turned[e], grads[target], preferred_element_type=F32)
            if not combine:
                columns = pl.ds(pl.multiple_of(place % slots * tile, tile), tile)
                term = jnp.dot(
                    halo_turned[:, columns], term.astype(BF16), preferred_element_type=F32
                )
                place = place // slots
            terms.append((jnp.where(real, place, spare), term))
        for place, term in terms:
            sums[place] = sums[place] + term

    for_entries(listed[entries], body)
    for r in range(relations):
        if combine:
            stacked = sums[r * slots : (r + 1) * slots].reshape(slots * tile, features)
            high, low = halves(stacked)
            grad = jnp.dot(halo_turned[...], high, preferred_element_type=F32)
            grad = grad + jnp.dot(halo_turned[...], low, preferred_element_type=F32)
        else:
            grad = sums[r]
        for m, out in enumerate(outs):
            out[r] = grad[m * share : (m + 1) * share].astype(out.dtype)


def spread_kernel(first_relation, *refs):
    out, scratch, sems = refs[-3:]
    shares = refs[: scratch.shape[0]]
    relations, share = scratch.shape[1], scratch.shape[2]
    copies = []
    for m in reversed(range(len(shares))):
        scratch[m] = shares[m][...].astype(F32)
        panel = lax.axis_index("src") ^ m
        rows = pl.ds(pl.multiple_of(panel * share, share), share)
        copies.append(
            pltpu.make_async_copy(
                scratch.at[m],
                out.at[pl.ds(first_relation, relations), rows, :],
                sems.at[m],
            )
        )
        copies[-1].start()
    for copy in copies:
        copy.wait()


def spread(first_relation, shares, total, so_far):
    scratch = jax.ShapeDtypeStruct((len(shares), *shares[0].shape), F32)
    return pl.pallas_call(
        functools.partial(spread_kernel, first_relation),
        out_shape=total,
        in_specs=[WHOLE] * len(shares) + [ANYWHERE] * len(so_far),
        out_specs=ANYWHERE,
        scratch_shapes=[
            pltpu.VMEM(scratch.shape, F32),
            pltpu.SemaphoreType.DMA((len(shares),)),
        ],
        input_output_aliases={len(shares): 0} if so_far else {},
        compiler_params=vmem_for(scratch, *shares),
        name="spread",
    )(*shares, *so_far)


def sum_kernel(*refs):
    total = refs[0][...].astype(F32)
    for ref in refs[1:-1]:
        total = total + ref[...].astype(F32)
    refs[-1][...] = total.astype(refs[-1].dtype)


def summed(values, dtype=BF16):
    out = jax.ShapeDtypeStruct(values[0].shape, dtype)
    return pl.pallas_call(
        sum_kernel,
        out_shape=out,
        in_specs=[WHOLE] * len(values),
        out_specs=WHOLE,
        compiler_params=vmem_for(out, *values),
        name="sum",
    )(*values)


def silu_slope(pre_values):
    logistic = jax.nn.sigmoid(pre_values)
    return logistic * (1.0 + pre_values * (1.0 - logistic))


def exchange(pieces, axis):
    return [swap(pieces[m].astype(BF16), axis, m) for m in range(len(pieces) - 1, 0, -1)]


def added(own, arrived):
    total = own.astype(F32)
    for value in arrived:
        total = total + value.astype(F32)
    return total


def gather(value, axis):
    return [value] + [swap(value, axis, m) for m in range(1, lax.axis_size(axis))]


def local(source_feats, rel_weight, halo_pick, entry_index, entry_count, entry_values, cotangent):
    partitions, panels = lax.axis_size("dom"), lax.axis_size("src")
    groups = lax.axis_size("rel")
    tile = entry_values.shape[-1]
    own_rows, features = cotangent.shape
    relations = rel_weight.shape[0]
    values = entry_values.reshape(-1, tile, tile)
    table = entry_index.reshape(3, -1)
    entries = table.shape[1]
    count = entry_count.reshape(1)
    chosen = halo_pick.reshape(-1)
    targets = own_rows * panels * groups // tile
    direct = partitions <= 8
    share = features // panels
    bounds = tuple(sorted({0, relations // 2, relations}))
    chunks = len(bounds) - 1

    panel_f32 = jax.ShapeDtypeStruct((own_rows, features), F32)
    panel_bf16 = jax.ShapeDtypeStruct((own_rows, features), BF16)
    pre_sums = jax.ShapeDtypeStruct((targets + 1, tile, features), F32)
    if direct:
        halo = [h[None] for h in gather(source_feats, "dom")]
    else:
        halo = [lax.all_gather(source_feats, "dom", axis=0)]
    slots = sum(h.shape[0] for h in halo)
    combine = slots * relations <= entries
    near = partitions // 2
    owners = groups, own_rows // tile
    start = near if direct else 0
    slot_groups = ((0, near, None),) * direct + ((start, slots, False), (start, slots, True))
    sums = [
        jax.ShapeDtypeStruct(
            ((high - low) * slots + 1, tile, features)
            if combine
            else (high - low + 1, features, features),
            F32,
        )
        for low, high in zip(bounds, bounds[1:])
    ]
    listings = [
        jax.ShapeDtypeStruct((entries + 1 + high - low,), I32)
        for low, high, _ in slot_groups
    ] + [jax.ShapeDtypeStruct((entries + 1,), I32)] * chunks
    held = [jax.ShapeDtypeStruct(v.shape, BF16) for v in (values, rel_weight)]
    values, rel_weight, *listings, pre = pl.pallas_call(
        functools.partial(prepare_kernel, direct, owners, slot_groups, bounds, targets),
        out_shape=(*held, *listings, pre_sums),
        in_specs=[SCALARS] * 3 + [ANYWHERE] * 2,
        out_specs=(WHOLE,) * 2 + (SCALARS,) * len(listings) + (WHOLE,),
        scratch_shapes=[pltpu.SemaphoreType.DMA((2,))],
        compiler_params=vmem_for(*held, pre_sums),
        cost_estimate=pl.CostEstimate(
            flops=0, bytes_accessed=4 * values.size, transcendentals=0
        ),
        name="prepare",
    )(chosen, table, count, values, rel_weight)
    lists = listings[-chunks:]

    first = 1 if panels > 1 else 0
    sends = (panel_bf16, jax.ShapeDtypeStruct((panels - 1, own_rows, features), BF16))
    cost = pl.CostEstimate(
        flops=4 * entries * tile * tile * features, bytes_accessed=values.size, transcendentals=0
    )
    for call, (low, high, _) in enumerate(slot_groups[:-1]):
        last = call == len(slot_groups) - 2
        blocks = halo[low:high] if direct else halo
        projected = jax.ShapeDtypeStruct(
            ((high - low) * relations, 2 * tile, features)
            if combine
            else (high - low, tile, features),
            BF16,
        )
        kernel = functools.partial(near_kernel, tile, combine)
        if last:
            kernel = functools.partial(theirs_kernel, tile, combine, owners, first)
        outs = (pre_sums, projected, *sends) if last else (pre_sums,)
        pre, *given = pl.pallas_call(
            kernel,
            out_shape=outs,
            in_specs=[SCALARS] + [WHOLE] * (len(blocks) + 3),
            out_specs=(WHOLE,) * len(outs),
            scratch_shapes=[] if last else [pltpu.VMEM(projected.shape, BF16)],
            input_output_aliases={3 + len(blocks): 0},
            compiler_params=vmem_for(*outs, projected, *blocks, rel_weight, values),
            cost_estimate=cost,
            name="forward",
        )(listings[call], *blocks, rel_weight, values, pre)
    projected, *given = given
    _, *keeps = pl.pallas_call(
        functools.partial(ours_kernel, tile, combine, owners),
        out_shape=(pre_sums,) + (panel_f32,) * panels,
        in_specs=[SCALARS] + [WHOLE] * 4,
        out_specs=(WHOLE,) * (1 + panels),
        input_output_aliases={4: 0},
        compiler_params=vmem_for(pre_sums, pre_sums, projected, rel_weight, values),
        cost_estimate=cost,
        name="forward_ours",
    )(listings[len(slot_groups) - 1], projected, rel_weight, values, pre)
    first_sum = summed([keeps[first], swap(given[0], "rel", 1)])
    rest = [m for m in range(panels) if m != first]
    rest_sums = (panel_f32,) + (panel_bf16,) * (panels - 2)
    leaving = pl.pallas_call(
        chip_kernel,
        out_shape=rest_sums,
        in_specs=[WHOLE] * panels,
        out_specs=(WHOLE,) * (panels - 1),
        compiler_params=vmem_for(*rest_sums, *keeps, sends[1]),
        name="chip",
    )(*(keeps[m] for m in rest), swap(given[1], "rel", 1))
    leaving = [leaving[0], first_sum, *leaving[1:]]
    leaving, chosen_then = lax.optimization_barrier((leaving, chosen))
    arrived = exchange(leaving, "src")
    turned = (held[0], jax.ShapeDtypeStruct((features, slots * tile), BF16))
    prepared = pl.pallas_call(
        functools.partial(turn_kernel, direct, tile, panels, len(halo)),
        out_shape=(*turned, *sums),
        in_specs=[SCALARS] + [WHOLE] * (1 + len(halo)),
        out_specs=(WHOLE,) * (2 + chunks),
        scratch_shapes=[pltpu.VMEM((features, tile), F32)],
        compiler_params=vmem_for(*turned, *sums, values, *halo),
        cost_estimate=pl.CostEstimate(
            flops=0, bytes_accessed=4 * values.size, transcendentals=0
        ),
        name="turn",
    )(chosen_then, values, *halo)
    arrived, prepared = lax.optimization_barrier((arrived, prepared))
    block = jax.ShapeDtypeStruct((own_rows, features), BF16)
    if len(arrived) == 3:
        local_grad = pl.pallas_call(
            grad_kernel,
            out_shape=block,
            in_specs=[WHOLE] * 5,
            out_specs=WHOLE,
            compiler_params=vmem_for(leaving[0], block, block, block, block, block),
            name="grad",
        )(leaving[0], *arrived, cotangent)
    else:
        local_grad = cotangent.astype(F32) * silu_slope(added(leaving[0], arrived))
        local_grad = local_grad.astype(BF16)
    out_feats = jax.nn.silu(added(leaving[0], arrived)).astype(BF16)

    core_grads = gather(local_grad, "src")
    other_grads = [swap(value, "rel", 1) for value in core_grads]

    by_target = jax.ShapeDtypeStruct((targets, tile, features), BF16)
    grads = pl.pallas_call(
        functools.partial(collect_kernel, tile),
        out_shape=by_target,
        in_specs=[WHOLE] * (2 * panels),
        out_specs=WHOLE,
        compiler_params=vmem_for(by_target, by_target),
        name="collect",
    )(*core_grads, *other_grads)

    total = jax.ShapeDtypeStruct((relations, features, features), F32)
    panel_sums, pieces, done = [], [], []
    for c in range(chunks):
        own_share = jax.ShapeDtypeStruct((bounds[c + 1] - bounds[c], share, features), F32)
        sent_share = jax.ShapeDtypeStruct(own_share.shape, BF16)
        *shares, _ = pl.pallas_call(
            functools.partial(weight_kernel, tile, combine),
            out_shape=(own_share,) + (sent_share,) * (panels - 1) + (sums[c],),
            in_specs=[SCALARS] + [WHOLE] * 4,
            out_specs=(WHOLE,) * (panels + 1),
            input_output_aliases={4: panels},
            compiler_params=vmem_for(*(own_share,) * panels, sums[c], by_target, *turned),
            name="weight_terms",
        )(lists[c], *prepared[:2], grads, prepared[2 + c])
        panel_sums.append(
            summed([shares[0]] + exchange(shares, "src"), BF16 if direct else F32)
        )
    for c, panel_sum in enumerate(panel_sums):
        if direct:
            masks = [1 << i for i in range(partitions.bit_length() - 1)]
            for mask in masks if c % 2 else reversed(masks):
                panel_sum = summed([panel_sum, swap(panel_sum, "dom", mask)])
        else:
            panel_sum = lax.psum(panel_sum, "dom").astype(BF16)
        pieces.append(gather(panel_sum, "src"))
    for c in range(chunks):
        done = [spread(bounds[c], pieces[c], total, done)]
    grad_rel = done[0]
    return (out_feats, grad_rel)


def solution(mesh):
    return jax.shard_map(
        local,
        mesh=mesh,
        in_specs=(
            P(("dom", "src", "rel"), None),
            P("rel", None, None),
            P("dom", "src", "rel", None),
            P("dom", "src", "rel", None, None),
            P("dom", "src", "rel"),
            P("dom", "src", "rel", None, None, None),
            P(("dom", "src", "rel"), None),
        ),
        out_specs=(P(("dom", "src", "rel"), None), P("rel", None, None)),
        check_vma=False,
    )
```

```python
import functools
import math

import jax
import jax.numpy as jnp
from jax import lax
from jax.experimental import pallas as pl
from jax.experimental.pallas import tpu as pltpu
from jax.sharding import PartitionSpec as P

F32, BF16, I32 = jnp.float32, jnp.bfloat16, jnp.int32
WHOLE = pl.BlockSpec(memory_space=pltpu.VMEM)
SCALARS = pl.BlockSpec(memory_space=pltpu.SMEM)
ANYWHERE = pl.BlockSpec(memory_space=pl.ANY)
UNROLL = 20


def vmem_for(*arrays):
    held = sum(math.prod(a.shape) * jnp.dtype(a.dtype).itemsize for a in arrays)
    return pltpu.CompilerParams(vmem_limit_bytes=held + held // 8 + 3 * 1024 * 1024)


def partner_pairs(size, mask):
    return [(i, i ^ mask) for i in range(size)]


def swap(value, axis, mask):
    return lax.ppermute(value, axis, partner_pairs(lax.axis_size(axis), mask))


def here():
    return [lax.axis_index(axis) for axis in ("dom", "src", "rel")]


def slot_of(places, partition, masked):
    return partition ^ places[0] if masked else partition


def packed(entries, targets, e, target, place):
    bits = (entries - 1).bit_length()
    return e | (target << bits) | (place << (bits + (targets - 1).bit_length()))


def unpacked(entries, targets, code):
    bits, more = (entries - 1).bit_length(), (targets - 1).bit_length()
    return code & ((1 << bits) - 1), (code >> bits) & ((1 << more) - 1), code >> (bits + more)


def for_entries(total, body):
    def step(i, carry):
        body([(jnp.minimum(i * UNROLL + u, total - 1), i * UNROLL + u < total) for u in range(UNROLL)])
        return carry

    lax.fori_loop(0, (total + UNROLL - 1) // UNROLL, step, 0)


def halo_block(first_block, halo_refs, i, tile):
    per_call = halo_refs[0].shape[0]
    rows = pl.ds(pl.multiple_of(first_block * tile, tile), tile)
    return halo_refs[i // per_call][i % per_call, rows, :]


def prepare_kernel(masked, owners, groups, bounds, targets, chosen, table, count, *refs):
    values, weight, values_here, weight_here = refs[:4]
    by_slot, refs = refs[4 : 4 + len(groups)], refs[4 + len(groups) :]
    by_relation, (pre, sems) = refs[: len(bounds) - 1], refs[len(bounds) - 1 :]
    entries, relations = values.shape[0], weight.shape[0]
    copies = [
        pltpu.make_async_copy(values, values_here, sems.at[0]),
        pltpu.make_async_copy(weight, weight_here, sems.at[1]),
    ]
    for copy in copies:
        copy.start()
    pre[...] = jnp.zeros_like(pre)
    places = here()
    cores, per_owner = owners
    slots = groups[-1][1]

    def put(e, found):
        target, relation = table[0, e], table[2, e]
        slot = slot_of(places, table[1, e], masked)
        own = (target >> (per_owner.bit_length() - 1)) & (cores - 1) == places[2]
        now = []
        for listed, (low, high, side) in zip(by_slot, groups):
            place = (slot - low) * relations + relation
            listed[found[len(now)]] = packed(entries, targets, e, target, place)
            inside = (slot >= low) & (slot < high)
            now.append(inside if side is None else inside & (own == side))
        for listed, low, high in zip(by_relation, bounds, bounds[1:]):
            place = (relation - low) * slots + slot
            listed[found[len(now)]] = packed(entries, targets, e, target, place)
            now.append((relation >= low) & (relation < high))
        return tuple(f + n.astype(I32) for f, n in zip(found, now))

    lists = (*by_slot, *by_relation)
    found = lax.fori_loop(0, count[0], put, (jnp.int32(0),) * len(lists))
    for listed, number in zip(lists, found):
        listed[entries] = number
    for listed, (low, high, _) in zip(by_slot, groups):
        for i in range(low, high):
            listed[entries + 1 + i - low] = chosen[slot_of(places, i, masked)]

    for copy in copies:
        copy.wait()


def near_kernel(tile, combine, order, *refs):
    *halo_refs, weight, values, before, pre, projected = refs
    entries = values.shape[0]
    firsts = [order[entries + 1 + i] for i in range(order.shape[0] - entries - 1)]
    project(tile, combine, firsts, halo_refs, weight, projected)
    add_entries(combine, values, weight, projected, order, order[entries], pre)


def theirs_kernel(tile, combine, owners, first, order, *refs):
    near_kernel(tile, combine, order, *refs[:-2])
    pre, sends = refs[-4], refs[-2:]
    panels = sends[1].shape[0] + 1
    others = [m for m in range(panels) if m != first]
    for out, distance in ((sends[0], first), *((sends[1].at[i], m) for i, m in enumerate(others))):
        for rows, block in blocks_of(tile, owners, here(), distance, 1):
            out[rows, :] = pre[block].astype(BF16)


def ours_kernel(tile, combine, owners, order, projected, weight, values, before, pre, *keeps):
    del before
    add_entries(combine, values, weight, projected, order, order[values.shape[0]], pre)
    for distance, keep in enumerate(keeps):
        for rows, block in blocks_of(tile, owners, here(), distance, 0):
            keep[rows, :] = pre[block]


def blocks_of(tile, owners, places, distance, other):
    cores, per_owner = owners
    owner = (places[1] ^ distance) * cores + (places[2] ^ other)
    return [(pl.ds(i * tile, tile), owner * per_owner + i) for i in range(per_owner)]


def halves(value):
    high = value.astype(BF16)
    return high, (value - high.astype(F32)).astype(BF16)


def project(tile, combine, firsts, halo_refs, weight, projected):
    relations = weight.shape[0]
    blocks = [halo_block(first, halo_refs, i, tile) for i, first in enumerate(firsts)]
    if not combine:
        for i, block in enumerate(blocks):
            projected[i] = block
        return
    stacked = jnp.concatenate(blocks, axis=0)
    for r in range(relations):
        high, low = halves(jnp.dot(stacked, weight[r], preferred_element_type=F32))
        for i in range(len(blocks)):
            rows = slice(i * tile, (i + 1) * tile)
            projected[i * relations + r, :tile, :] = high[rows]
            projected[i * relations + r, tile:, :] = low[rows]


def add_entries(combine, values, weight, projected, order, total, pre):
    entries, relations, spare = values.shape[0], weight.shape[0], pre.shape[0] - 1

    def body(positions):
        terms = []
        for position, real in positions:
            e, target, place = unpacked(entries, spare, order[position])
            if combine:
                twice = jnp.concatenate([values[e], values[e]], axis=1)
                term = jnp.dot(twice, projected[place], preferred_element_type=F32)
            else:
                message = jnp.dot(
                    values[e], projected[place // relations], preferred_element_type=F32
                )
                term = jnp.dot(
                    message.astype(BF16), weight[place % relations], preferred_element_type=F32
                )
            terms.append((jnp.where(real, target, spare), term))
        for target, term in terms:
            pre[target] = pre[target] + term

    for_entries(total, body)


def chip_kernel(*refs):
    count = (len(refs) - 1) // 2
    keeps, arrived, outs = refs[:count], refs[count], refs[count + 1 :]
    for m in range(count):
        outs[m][...] = (keeps[m][...] + arrived[m].astype(F32)).astype(outs[m].dtype)


def grad_kernel(own, first, second, third, cotangent, grad):
    pre = own[...] + first[...].astype(F32) + second[...].astype(F32) + third[...].astype(F32)
    grad[...] = (cotangent[...].astype(F32) * silu_slope(pre)).astype(BF16)


def turn_kernel(masked, tile, panels, halo_count, chosen, values, *refs):
    halo_refs, refs = refs[:halo_count], refs[halo_count:]
    values_turned, halo_turned, zeros, scratch = refs[0], refs[1], refs[2:-1], refs[-1]
    places = here()
    for each in zeros:
        each[...] = jnp.zeros_like(each)
    share = scratch.shape[0] // panels
    for slot in range(len(halo_refs) * halo_refs[0].shape[0]):
        block = halo_block(chosen[slot_of(places, slot, masked)], halo_refs, slot, tile)
        scratch[...] = block.astype(F32).T
        for m in range(panels):
            start = pl.multiple_of((places[1] ^ m) * share, share)
            halo_turned[pl.ds(m * share, share), pl.ds(slot * tile, tile)] = (
                scratch[pl.ds(start, share), :].astype(BF16)
            )

    batch = 8

    def step(i, carry):
        for u in range(batch):
            values_turned[i * batch + u] = values[i * batch + u].T
        return carry

    lax.fori_loop(0, values.shape[0] // batch, step, 0)


def collect_kernel(tile, *refs):
    grad_refs, grads = refs[:-1], refs[-1]
    panels = len(grad_refs) // 2
    per_owner = grad_refs[0].shape[0] // tile
    for g in range(2):
        for m in range(panels):
            owner = (lax.axis_index("src") ^ m) * 2 + (lax.axis_index("rel") ^ g)
            for part in range(per_owner):
                grads[owner * per_owner + part] = grad_refs[g * panels + m][
                    pl.ds(part * tile, tile), :
                ]


def weight_kernel(tile, combine, listed, *refs):
    values_turned, halo_turned, grads = refs[:3]
    outs, sums = refs[4:-1], refs[-1]
    features = halo_turned.shape[0]
    slots = halo_turned.shape[1] // tile
    relations, share = outs[0].shape[0], outs[0].shape[1]
    entries, targets, spare = values_turned.shape[0], grads.shape[0], sums.shape[0] - 1

    def body(positions):
        terms = []
        for position, real in positions:
            e, target, place = unpacked(entries, targets, listed[position])
            term = jnp.dot(values_turned[e], grads[target], preferred_element_type=F32)
            if not combine:
                columns = pl.ds(pl.multiple_of(place % slots * tile, tile), tile)
                term = jnp.dot(
                    halo_turned[:, columns], term.astype(BF16), preferred_element_type=F32
                )
                place = place // slots
            terms.append((jnp.where(real, place, spare), term))
        for place, term in terms:
            sums[place] = sums[place] + term

    for_entries(listed[entries], body)
    for r in range(relations):
        if combine:
            stacked = sums[r * slots : (r + 1) * slots].reshape(slots * tile, features)
            high, low = halves(stacked)
            grad = jnp.dot(halo_turned[...], high, preferred_element_type=F32)
            grad = grad + jnp.dot(halo_turned[...], low, preferred_element_type=F32)
        else:
            grad = sums[r]
        for m, out in enumerate(outs):
            out[r] = grad[m * share : (m + 1) * share].astype(out.dtype)


def spread_kernel(first_relation, *refs):
    out, scratch, sems = refs[-3:]
    shares = refs[: scratch.shape[0]]
    relations, share = scratch.shape[1], scratch.shape[2]
    copies = []
    for m in reversed(range(len(shares))):
        scratch[m] = shares[m][...].astype(F32)
        panel = lax.axis_index("src") ^ m
        rows = pl.ds(pl.multiple_of(panel * share, share), share)
        copies.append(
            pltpu.make_async_copy(
                scratch.at[m],
                out.at[pl.ds(first_relation, relations), rows, :],
                sems.at[m],
            )
        )
        copies[-1].start()
    for copy in copies:
        copy.wait()


def spread(first_relation, shares, total, so_far):
    scratch = jax.ShapeDtypeStruct((len(shares), *shares[0].shape), F32)
    return pl.pallas_call(
        functools.partial(spread_kernel, first_relation),
        out_shape=total,
        in_specs=[WHOLE] * len(shares) + [ANYWHERE] * len(so_far),
        out_specs=ANYWHERE,
        scratch_shapes=[
            pltpu.VMEM(scratch.shape, F32),
            pltpu.SemaphoreType.DMA((len(shares),)),
        ],
        input_output_aliases={len(shares): 0} if so_far else {},
        compiler_params=vmem_for(scratch, *shares),
        name="spread",
    )(*shares, *so_far)


def sum_kernel(*refs):
    total = refs[0][...].astype(F32)
    for ref in refs[1:-1]:
        total = total + ref[...].astype(F32)
    refs[-1][...] = total.astype(refs[-1].dtype)


def summed(values, dtype=BF16):
    out = jax.ShapeDtypeStruct(values[0].shape, dtype)
    return pl.pallas_call(
        sum_kernel,
        out_shape=out,
        in_specs=[WHOLE] * len(values),
        out_specs=WHOLE,
        compiler_params=vmem_for(out, *values),
        name="sum",
    )(*values)


def silu_slope(pre_values):
    logistic = jax.nn.sigmoid(pre_values)
    return logistic * (1.0 + pre_values * (1.0 - logistic))


def exchange(pieces, axis):
    return [swap(pieces[m].astype(BF16), axis, m) for m in range(len(pieces) - 1, 0, -1)]


def added(own, arrived):
    total = own.astype(F32)
    for value in arrived:
        total = total + value.astype(F32)
    return total


def gather(value, axis):
    return [value] + [swap(value, axis, m) for m in range(1, lax.axis_size(axis))]


def local(source_feats, rel_weight, halo_pick, entry_index, entry_count, entry_values, cotangent):
    partitions, panels = lax.axis_size("dom"), lax.axis_size("src")
    groups = lax.axis_size("rel")
    tile = entry_values.shape[-1]
    own_rows, features = cotangent.shape
    relations = rel_weight.shape[0]
    values = entry_values.reshape(-1, tile, tile)
    table = entry_index.reshape(3, -1)
    entries = table.shape[1]
    count = entry_count.reshape(1)
    chosen = halo_pick.reshape(-1)
    targets = own_rows * panels * groups // tile
    direct = partitions <= 8
    share = features // panels
    bounds = tuple(sorted({0, relations // 2, relations}))
    chunks = len(bounds) - 1

    panel_f32 = jax.ShapeDtypeStruct((own_rows, features), F32)
    panel_bf16 = jax.ShapeDtypeStruct((own_rows, features), BF16)
    pre_sums = jax.ShapeDtypeStruct((targets + 1, tile, features), F32)
    if direct:
        halo = [h[None] for h in gather(source_feats, "dom")]
    else:
        halo = [lax.all_gather(source_feats, "dom", axis=0)]
    slots = sum(h.shape[0] for h in halo)
    combine = slots * relations <= entries
    near = partitions // 2
    owners = groups, own_rows // tile
    start = near if direct else 0
    slot_groups = ((0, near, None),) * direct + ((start, slots, False), (start, slots, True))
    sums = [
        jax.ShapeDtypeStruct(
            ((high - low) * slots + 1, tile, features)
            if combine
            else (high - low + 1, features, features),
            F32,
        )
        for low, high in zip(bounds, bounds[1:])
    ]
    listings = [
        jax.ShapeDtypeStruct((entries + 1 + high - low,), I32)
        for low, high, _ in slot_groups
    ] + [jax.ShapeDtypeStruct((entries + 1,), I32)] * chunks
    held = [jax.ShapeDtypeStruct(v.shape, BF16) for v in (values, rel_weight)]
    values, rel_weight, *listings, pre = pl.pallas_call(
        functools.partial(prepare_kernel, direct, owners, slot_groups, bounds, targets),
        out_shape=(*held, *listings, pre_sums),
        in_specs=[SCALARS] * 3 + [ANYWHERE] * 2,
        out_specs=(WHOLE,) * 2 + (SCALARS,) * len(listings) + (WHOLE,),
        scratch_shapes=[pltpu.SemaphoreType.DMA((2,))],
        compiler_params=vmem_for(*held, pre_sums),
        cost_estimate=pl.CostEstimate(
            flops=0, bytes_accessed=4 * values.size, transcendentals=0
        ),
        name="prepare",
    )(chosen, table, count, values, rel_weight)
    lists = listings[-chunks:]

    first = panels - 1
    sends = (panel_bf16, jax.ShapeDtypeStruct((panels - 1, own_rows, features), BF16))
    cost = pl.CostEstimate(
        flops=4 * entries * tile * tile * features, bytes_accessed=values.size, transcendentals=0
    )
    for call, (low, high, _) in enumerate(slot_groups[:-1]):
        last = call == len(slot_groups) - 2
        blocks = halo[low:high] if direct else halo
        projected = jax.ShapeDtypeStruct(
            ((high - low) * relations, 2 * tile, features)
            if combine
            else (high - low, tile, features),
            BF16,
        )
        kernel = functools.partial(near_kernel, tile, combine)
        if last:
            kernel = functools.partial(theirs_kernel, tile, combine, owners, first)
        outs = (pre_sums, projected, *sends) if last else (pre_sums,)
        pre, *given = pl.pallas_call(
            kernel,
            out_shape=outs,
            in_specs=[SCALARS] + [WHOLE] * (len(blocks) + 3),
            out_specs=(WHOLE,) * len(outs),
            scratch_shapes=[] if last else [pltpu.VMEM(projected.shape, BF16)],
            input_output_aliases={3 + len(blocks): 0},
            compiler_params=vmem_for(*outs, projected, *blocks, rel_weight, values),
            cost_estimate=cost,
            name="forward",
        )(listings[call], *blocks, rel_weight, values, pre)
    projected, *given = given
    _, *keeps = pl.pallas_call(
        functools.partial(ours_kernel, tile, combine, owners),
        out_shape=(pre_sums,) + (panel_f32,) * panels,
        in_specs=[SCALARS] + [WHOLE] * 4,
        out_specs=(WHOLE,) * (1 + panels),
        input_output_aliases={4: 0},
        compiler_params=vmem_for(pre_sums, pre_sums, projected, rel_weight, values),
        cost_estimate=cost,
        name="forward_ours",
    )(listings[len(slot_groups) - 1], projected, rel_weight, values, pre)
    first_sum = summed([keeps[first], swap(given[0], "rel", 1)])
    rest = [m for m in range(panels) if m != first]
    rest_sums = (panel_f32,) + (panel_bf16,) * (panels - 2)
    leaving = pl.pallas_call(
        chip_kernel,
        out_shape=rest_sums,
        in_specs=[WHOLE] * panels,
        out_specs=(WHOLE,) * (panels - 1),
        compiler_params=vmem_for(*rest_sums, *keeps, sends[1]),
        name="chip",
    )(*(keeps[m] for m in rest), swap(given[1], "rel", 1))
    leaving = [*leaving, first_sum]
    leaving, chosen_then = lax.optimization_barrier((leaving, chosen))
    arrived = exchange(leaving, "src")
    turned = (held[0], jax.ShapeDtypeStruct((features, slots * tile), BF16))
    prepared = pl.pallas_call(
        functools.partial(turn_kernel, direct, tile, panels, len(halo)),
        out_shape=(*turned, *sums),
        in_specs=[SCALARS] + [WHOLE] * (1 + len(halo)),
        out_specs=(WHOLE,) * (2 + chunks),
        scratch_shapes=[pltpu.VMEM((features, tile), F32)],
        compiler_params=vmem_for(*turned, *sums, values, *halo),
        cost_estimate=pl.CostEstimate(
            flops=0, bytes_accessed=4 * values.size, transcendentals=0
        ),
        name="turn",
    )(chosen_then, values, *halo)
    arrived, prepared = lax.optimization_barrier((arrived, prepared))
    block = jax.ShapeDtypeStruct((own_rows, features), BF16)
    if len(arrived) == 3:
        local_grad = pl.pallas_call(
            grad_kernel,
            out_shape=block,
            in_specs=[WHOLE] * 5,
            out_specs=WHOLE,
            compiler_params=vmem_for(leaving[0], block, block, block, block, block),
            name="grad",
        )(leaving[0], *arrived, cotangent)
    else:
        local_grad = cotangent.astype(F32) * silu_slope(added(leaving[0], arrived))
        local_grad = local_grad.astype(BF16)
    out_feats = jax.nn.silu(added(leaving[0], arrived)).astype(BF16)

    core_grads = gather(local_grad, "src")
    other_grads = [swap(value, "rel", 1) for value in core_grads]

    by_target = jax.ShapeDtypeStruct((targets, tile, features), BF16)
    grads = pl.pallas_call(
        functools.partial(collect_kernel, tile),
        out_shape=by_target,
        in_specs=[WHOLE] * (2 * panels),
        out_specs=WHOLE,
        compiler_params=vmem_for(by_target, by_target),
        name="collect",
    )(*core_grads, *other_grads)

    total = jax.ShapeDtypeStruct((relations, features, features), F32)
    panel_sums, pieces, done = [], [], []
    for c in range(chunks):
        own_share = jax.ShapeDtypeStruct((bounds[c + 1] - bounds[c], share, features), F32)
        sent_share = jax.ShapeDtypeStruct(own_share.shape, BF16)
        *shares, _ = pl.pallas_call(
            functools.partial(weight_kernel, tile, combine),
            out_shape=(own_share,) + (sent_share,) * (panels - 1) + (sums[c],),
            in_specs=[SCALARS] + [WHOLE] * 4,
            out_specs=(WHOLE,) * (panels + 1),
            input_output_aliases={4: panels},
            compiler_params=vmem_for(*(own_share,) * panels, sums[c], by_target, *turned),
            name="weight_terms",
        )(lists[c], *prepared[:2], grads, prepared[2 + c])
        panel_sums.append(
            summed([shares[0]] + exchange(shares, "src"), BF16 if direct else F32)
        )
    for c, panel_sum in enumerate(panel_sums):
        if direct:
            masks = [1 << i for i in range(partitions.bit_length() - 1)]
            for mask in masks if c % 2 else reversed(masks):
                panel_sum = summed([panel_sum, swap(panel_sum, "dom", mask)])
        else:
            panel_sum = lax.psum(panel_sum, "dom").astype(BF16)
        pieces.append(gather(panel_sum, "src"))
    for c in range(chunks):
        done = [spread(bounds[c], pieces[c], total, done)]
    grad_rel = done[0]
    return (out_feats, grad_rel)


def solution(mesh):
    return jax.shard_map(
        local,
        mesh=mesh,
        in_specs=(
            P(("dom", "src", "rel"), None),
            P("rel", None, None),
            P("dom", "src", "rel", None),
            P("dom", "src", "rel", None, None),
            P("dom", "src", "rel"),
            P("dom", "src", "rel", None, None, None),
            P(("dom", "src", "rel"), None),
        ),
        out_specs=(P(("dom", "src", "rel"), None), P("rel", None, None)),
        check_vma=False,
    )
```

```python
import functools
import math

import jax
import jax.numpy as jnp
from jax import lax
from jax.experimental import pallas as pl
from jax.experimental.pallas import tpu as pltpu
from jax.sharding import PartitionSpec as P

F32, BF16, I32 = jnp.float32, jnp.bfloat16, jnp.int32
WHOLE = pl.BlockSpec(memory_space=pltpu.VMEM)
SCALARS = pl.BlockSpec(memory_space=pltpu.SMEM)
ANYWHERE = pl.BlockSpec(memory_space=pl.ANY)
UNROLL = 20


def vmem_for(*arrays):
    held = sum(math.prod(a.shape) * jnp.dtype(a.dtype).itemsize for a in arrays)
    return pltpu.CompilerParams(vmem_limit_bytes=held + held // 8 + 3 * 1024 * 1024)


def partner_pairs(size, mask):
    return [(i, i ^ mask) for i in range(size)]


def swap(value, axis, mask):
    return lax.ppermute(value, axis, partner_pairs(lax.axis_size(axis), mask))


def here():
    return [lax.axis_index(axis) for axis in ("dom", "src", "rel")]


def slot_of(places, partition, masked):
    return partition ^ places[0] if masked else partition


def packed(entries, targets, e, target, place):
    bits = (entries - 1).bit_length()
    return e | (target << bits) | (place << (bits + (targets - 1).bit_length()))


def unpacked(entries, targets, code):
    bits, more = (entries - 1).bit_length(), (targets - 1).bit_length()
    return code & ((1 << bits) - 1), (code >> bits) & ((1 << more) - 1), code >> (bits + more)


def for_entries(total, body):
    def step(i, carry):
        body([(jnp.minimum(i * UNROLL + u, total - 1), i * UNROLL + u < total) for u in range(UNROLL)])
        return carry

    lax.fori_loop(0, (total + UNROLL - 1) // UNROLL, step, 0)


def halo_block(first_block, halo_refs, i, tile):
    per_call = halo_refs[0].shape[0]
    rows = pl.ds(pl.multiple_of(first_block * tile, tile), tile)
    return halo_refs[i // per_call][i % per_call, rows, :]


def prepare_kernel(masked, owners, groups, bounds, targets, chosen, table, count, *refs):
    values, weight, values_here, weight_here = refs[:4]
    by_slot, refs = refs[4 : 4 + len(groups)], refs[4 + len(groups) :]
    by_relation, (pre, sems) = refs[: len(bounds) - 1], refs[len(bounds) - 1 :]
    entries, relations = values.shape[0], weight.shape[0]
    copies = [
        pltpu.make_async_copy(values, values_here, sems.at[0]),
        pltpu.make_async_copy(weight, weight_here, sems.at[1]),
    ]
    for copy in copies:
        copy.start()
    pre[...] = jnp.zeros_like(pre)
    places = here()
    cores, per_owner = owners
    slots = groups[-1][1]

    def put(e, found):
        target, relation = table[0, e], table[2, e]
        slot = slot_of(places, table[1, e], masked)
        own = (target >> (per_owner.bit_length() - 1)) & (cores - 1) == places[2]
        now = []
        for listed, (low, high, side) in zip(by_slot, groups):
            place = (slot - low) * relations + relation
            listed[found[len(now)]] = packed(entries, targets, e, target, place)
            inside = (slot >= low) & (slot < high)
            now.append(inside if side is None else inside & (own == side))
        for listed, low, high in zip(by_relation, bounds, bounds[1:]):
            place = (relation - low) * slots + slot
            listed[found[len(now)]] = packed(entries, targets, e, target, place)
            now.append((relation >= low) & (relation < high))
        return tuple(f + n.astype(I32) for f, n in zip(found, now))

    lists = (*by_slot, *by_relation)
    found = lax.fori_loop(0, count[0], put, (jnp.int32(0),) * len(lists))
    for listed, number in zip(lists, found):
        listed[entries] = number
    for listed, (low, high, _) in zip(by_slot, groups):
        for i in range(low, high):
            listed[entries + 1 + i - low] = chosen[slot_of(places, i, masked)]

    for copy in copies:
        copy.wait()


def near_kernel(tile, combine, order, *refs):
    *halo_refs, weight, values, before, pre, projected = refs
    entries = values.shape[0]
    firsts = [order[entries + 1 + i] for i in range(order.shape[0] - entries - 1)]
    project(tile, combine, firsts, halo_refs, weight, projected)
    add_entries(combine, values, weight, projected, order, order[entries], pre)


def theirs_kernel(tile, combine, owners, order, *refs):
    near_kernel(tile, combine, order, *refs[:-1])
    pre, sends = refs[-3], refs[-1]
    for distance in range(sends.shape[0]):
        for rows, block in blocks_of(tile, owners, here(), distance, 1):
            sends[distance, rows, :] = pre[block].astype(BF16)


def ours_kernel(tile, combine, owners, order, projected, weight, values, before, pre, *keeps):
    del before
    add_entries(combine, values, weight, projected, order, order[values.shape[0]], pre)
    for distance, keep in enumerate(keeps):
        for rows, block in blocks_of(tile, owners, here(), distance, 0):
            keep[rows, :] = pre[block]


def blocks_of(tile, owners, places, distance, other):
    cores, per_owner = owners
    owner = (places[1] ^ distance) * cores + (places[2] ^ other)
    return [(pl.ds(i * tile, tile), owner * per_owner + i) for i in range(per_owner)]


def halves(value):
    high = value.astype(BF16)
    return high, (value - high.astype(F32)).astype(BF16)


def project(tile, combine, firsts, halo_refs, weight, projected):
    relations = weight.shape[0]
    blocks = [halo_block(first, halo_refs, i, tile) for i, first in enumerate(firsts)]
    if not combine:
        for i, block in enumerate(blocks):
            projected[i] = block
        return
    stacked = jnp.concatenate(blocks, axis=0)
    for r in range(relations):
        high, low = halves(jnp.dot(stacked, weight[r], preferred_element_type=F32))
        for i in range(len(blocks)):
            rows = slice(i * tile, (i + 1) * tile)
            projected[i * relations + r, :tile, :] = high[rows]
            projected[i * relations + r, tile:, :] = low[rows]


def add_entries(combine, values, weight, projected, order, total, pre):
    entries, relations, spare = values.shape[0], weight.shape[0], pre.shape[0] - 1

    def body(positions):
        terms = []
        for position, real in positions:
            e, target, place = unpacked(entries, spare, order[position])
            if combine:
                twice = jnp.concatenate([values[e], values[e]], axis=1)
                term = jnp.dot(twice, projected[place], preferred_element_type=F32)
            else:
                message = jnp.dot(
                    values[e], projected[place // relations], preferred_element_type=F32
                )
                term = jnp.dot(
                    message.astype(BF16), weight[place % relations], preferred_element_type=F32
                )
            terms.append((jnp.where(real, target, spare), term))
        for target, term in terms:
            pre[target] = pre[target] + term

    for_entries(total, body)


def chip_kernel(*refs):
    count = (len(refs) - 1) // 2
    keeps, arrived, outs = refs[:count], refs[count], refs[count + 1 :]
    for m in range(count):
        outs[m][...] = (keeps[m][...] + arrived[m].astype(F32)).astype(outs[m].dtype)


def grad_kernel(own, first, second, third, cotangent, grad):
    pre = own[...] + first[...].astype(F32) + second[...].astype(F32) + third[...].astype(F32)
    grad[...] = (cotangent[...].astype(F32) * silu_slope(pre)).astype(BF16)


def turn_kernel(masked, tile, panels, halo_count, chosen, values, *refs):
    halo_refs, refs = refs[:halo_count], refs[halo_count:]
    values_turned, halo_turned, zeros, scratch = refs[0], refs[1], refs[2:-1], refs[-1]
    places = here()
    for each in zeros:
        each[...] = jnp.zeros_like(each)
    share = scratch.shape[0] // panels
    for slot in range(len(halo_refs) * halo_refs[0].shape[0]):
        block = halo_block(chosen[slot_of(places, slot, masked)], halo_refs, slot, tile)
        scratch[...] = block.astype(F32).T
        for m in range(panels):
            start = pl.multiple_of((places[1] ^ m) * share, share)
            halo_turned[pl.ds(m * share, share), pl.ds(slot * tile, tile)] = (
                scratch[pl.ds(start, share), :].astype(BF16)
            )

    batch = 8

    def step(i, carry):
        for u in range(batch):
            values_turned[i * batch + u] = values[i * batch + u].T
        return carry

    lax.fori_loop(0, values.shape[0] // batch, step, 0)


def collect_kernel(tile, *refs):
    grad_refs, grads = refs[:-1], refs[-1]
    panels = len(grad_refs) // 2
    per_owner = grad_refs[0].shape[0] // tile
    for g in range(2):
        for m in range(panels):
            owner = (lax.axis_index("src") ^ m) * 2 + (lax.axis_index("rel") ^ g)
            for part in range(per_owner):
                grads[owner * per_owner + part] = grad_refs[g * panels + m][
                    pl.ds(part * tile, tile), :
                ]


def weight_kernel(tile, combine, listed, *refs):
    values_turned, halo_turned, grads = refs[:3]
    outs, sums = refs[4:-1], refs[-1]
    features = halo_turned.shape[0]
    slots = halo_turned.shape[1] // tile
    relations, share = outs[0].shape[0], outs[0].shape[1]
    entries, targets, spare = values_turned.shape[0], grads.shape[0], sums.shape[0] - 1

    def body(positions):
        terms = []
        for position, real in positions:
            e, target, place = unpacked(entries, targets, listed[position])
            term = jnp.dot(values_turned[e], grads[target], preferred_element_type=F32)
            if not combine:
                columns = pl.ds(pl.multiple_of(place % slots * tile, tile), tile)
                term = jnp.dot(
                    halo_turned[:, columns], term.astype(BF16), preferred_element_type=F32
                )
                place = place // slots
            terms.append((jnp.where(real, place, spare), term))
        for place, term in terms:
            sums[place] = sums[place] + term

    for_entries(listed[entries], body)
    for r in range(relations):
        if combine:
            stacked = sums[r * slots : (r + 1) * slots].reshape(slots * tile, features)
            high, low = halves(stacked)
            grad = jnp.dot(halo_turned[...], high, preferred_element_type=F32)
            grad = grad + jnp.dot(halo_turned[...], low, preferred_element_type=F32)
        else:
            grad = sums[r]
        for m, out in enumerate(outs):
            out[r] = grad[m * share : (m + 1) * share].astype(out.dtype)


def spread_kernel(first_relation, *refs):
    out, scratch, sems = refs[-3:]
    shares = refs[: scratch.shape[0]]
    relations, share = scratch.shape[1], scratch.shape[2]
    copies = []
    for m in reversed(range(len(shares))):
        scratch[m] = shares[m][...].astype(F32)
        panel = lax.axis_index("src") ^ m
        rows = pl.ds(pl.multiple_of(panel * share, share), share)
        copies.append(
            pltpu.make_async_copy(
                scratch.at[m],
                out.at[pl.ds(first_relation, relations), rows, :],
                sems.at[m],
            )
        )
        copies[-1].start()
    for copy in copies:
        copy.wait()


def spread(first_relation, shares, total, so_far):
    scratch = jax.ShapeDtypeStruct((len(shares), *shares[0].shape), F32)
    return pl.pallas_call(
        functools.partial(spread_kernel, first_relation),
        out_shape=total,
        in_specs=[WHOLE] * len(shares) + [ANYWHERE] * len(so_far),
        out_specs=ANYWHERE,
        scratch_shapes=[
            pltpu.VMEM(scratch.shape, F32),
            pltpu.SemaphoreType.DMA((len(shares),)),
        ],
        input_output_aliases={len(shares): 0} if so_far else {},
        compiler_params=vmem_for(scratch, *shares),
        name="spread",
    )(*shares, *so_far)


def sum_kernel(*refs):
    total = refs[0][...].astype(F32)
    for ref in refs[1:-1]:
        total = total + ref[...].astype(F32)
    refs[-1][...] = total.astype(refs[-1].dtype)


def summed(values, dtype=BF16):
    out = jax.ShapeDtypeStruct(values[0].shape, dtype)
    return pl.pallas_call(
        sum_kernel,
        out_shape=out,
        in_specs=[WHOLE] * len(values),
        out_specs=WHOLE,
        compiler_params=vmem_for(out, *values),
        name="sum",
    )(*values)


def silu_slope(pre_values):
    logistic = jax.nn.sigmoid(pre_values)
    return logistic * (1.0 + pre_values * (1.0 - logistic))


def exchange(pieces, axis):
    return [swap(pieces[m].astype(BF16), axis, m) for m in range(len(pieces) - 1, 0, -1)]


def added(own, arrived):
    total = own.astype(F32)
    for value in arrived:
        total = total + value.astype(F32)
    return total


def gather(value, axis):
    return [value] + [swap(value, axis, m) for m in range(1, lax.axis_size(axis))]


def local(source_feats, rel_weight, halo_pick, entry_index, entry_count, entry_values, cotangent):
    partitions, panels = lax.axis_size("dom"), lax.axis_size("src")
    groups = lax.axis_size("rel")
    tile = entry_values.shape[-1]
    own_rows, features = cotangent.shape
    relations = rel_weight.shape[0]
    values = entry_values.reshape(-1, tile, tile)
    table = entry_index.reshape(3, -1)
    entries = table.shape[1]
    count = entry_count.reshape(1)
    chosen = halo_pick.reshape(-1)
    targets = own_rows * panels * groups // tile
    direct = partitions <= 8
    share = features // panels
    bounds = tuple(sorted({0, relations // 2, relations}))
    chunks = len(bounds) - 1

    panel_f32 = jax.ShapeDtypeStruct((own_rows, features), F32)
    panel_bf16 = jax.ShapeDtypeStruct((own_rows, features), BF16)
    pre_sums = jax.ShapeDtypeStruct((targets + 1, tile, features), F32)
    if direct:
        halo = [h[None] for h in gather(source_feats, "dom")]
    else:
        halo = [lax.all_gather(source_feats, "dom", axis=0)]
    slots = sum(h.shape[0] for h in halo)
    combine = slots * relations <= entries
    near = partitions // 2
    owners = groups, own_rows // tile
    start = near if direct else 0
    slot_groups = ((0, near, None),) * direct + ((start, slots, False), (start, slots, True))
    sums = [
        jax.ShapeDtypeStruct(
            ((high - low) * slots + 1, tile, features)
            if combine
            else (high - low + 1, features, features),
            F32,
        )
        for low, high in zip(bounds, bounds[1:])
    ]
    listings = [
        jax.ShapeDtypeStruct((entries + 1 + high - low,), I32)
        for low, high, _ in slot_groups
    ] + [jax.ShapeDtypeStruct((entries + 1,), I32)] * chunks
    held = [jax.ShapeDtypeStruct(v.shape, BF16) for v in (values, rel_weight)]
    values, rel_weight, *listings, pre = pl.pallas_call(
        functools.partial(prepare_kernel, direct, owners, slot_groups, bounds, targets),
        out_shape=(*held, *listings, pre_sums),
        in_specs=[SCALARS] * 3 + [ANYWHERE] * 2,
        out_specs=(WHOLE,) * 2 + (SCALARS,) * len(listings) + (WHOLE,),
        scratch_shapes=[pltpu.SemaphoreType.DMA((2,))],
        compiler_params=vmem_for(*held, pre_sums),
        cost_estimate=pl.CostEstimate(
            flops=0, bytes_accessed=4 * values.size, transcendentals=0
        ),
        name="prepare",
    )(chosen, table, count, values, rel_weight)
    lists = listings[-chunks:]

    sends = (jax.ShapeDtypeStruct((panels, own_rows, features), BF16),)
    cost = pl.CostEstimate(
        flops=4 * entries * tile * tile * features, bytes_accessed=values.size, transcendentals=0
    )
    for call, (low, high, _) in enumerate(slot_groups[:-1]):
        last = call == len(slot_groups) - 2
        blocks = halo[low:high] if direct else halo
        projected = jax.ShapeDtypeStruct(
            ((high - low) * relations, 2 * tile, features)
            if combine
            else (high - low, tile, features),
            BF16,
        )
        kernel = functools.partial(near_kernel, tile, combine)
        if last:
            kernel = functools.partial(theirs_kernel, tile, combine, owners)
        outs = (pre_sums, projected, *sends) if last else (pre_sums,)
        pre, *given = pl.pallas_call(
            kernel,
            out_shape=outs,
            in_specs=[SCALARS] + [WHOLE] * (len(blocks) + 3),
            out_specs=(WHOLE,) * len(outs),
            scratch_shapes=[] if last else [pltpu.VMEM(projected.shape, BF16)],
            input_output_aliases={3 + len(blocks): 0},
            compiler_params=vmem_for(*outs, projected, *blocks, rel_weight, values),
            cost_estimate=cost,
            name="forward",
        )(listings[call], *blocks, rel_weight, values, pre)
    projected, *given = given
    _, *keeps = pl.pallas_call(
        functools.partial(ours_kernel, tile, combine, owners),
        out_shape=(pre_sums,) + (panel_f32,) * panels,
        in_specs=[SCALARS] + [WHOLE] * 4,
        out_specs=(WHOLE,) * (1 + panels),
        input_output_aliases={4: 0},
        compiler_params=vmem_for(pre_sums, pre_sums, projected, rel_weight, values),
        cost_estimate=cost,
        name="forward_ours",
    )(listings[len(slot_groups) - 1], projected, rel_weight, values, pre)
    panel_sums = (panel_f32,) + (panel_bf16,) * (panels - 1)
    leaving = pl.pallas_call(
        chip_kernel,
        out_shape=panel_sums,
        in_specs=[WHOLE] * (panels + 1),
        out_specs=(WHOLE,) * panels,
        compiler_params=vmem_for(*panel_sums, *keeps, *sends),
        name="chip",
    )(*keeps, swap(given[0], "rel", 1))
    leaving, chosen_then = lax.optimization_barrier((leaving, chosen))
    arrived = exchange(leaving, "src")
    turned = (held[0], jax.ShapeDtypeStruct((features, slots * tile), BF16))
    prepared = pl.pallas_call(
        functools.partial(turn_kernel, direct, tile, panels, len(halo)),
        out_shape=(*turned, *sums),
        in_specs=[SCALARS] + [WHOLE] * (1 + len(halo)),
        out_specs=(WHOLE,) * (2 + chunks),
        scratch_shapes=[pltpu.VMEM((features, tile), F32)],
        compiler_params=vmem_for(*turned, *sums, values, *halo),
        cost_estimate=pl.CostEstimate(
            flops=0, bytes_accessed=4 * values.size, transcendentals=0
        ),
        name="turn",
    )(chosen_then, values, *halo)
    arrived, prepared = lax.optimization_barrier((arrived, prepared))
    block = jax.ShapeDtypeStruct((own_rows, features), BF16)
    if len(arrived) == 3:
        local_grad = pl.pallas_call(
            grad_kernel,
            out_shape=block,
            in_specs=[WHOLE] * 5,
            out_specs=WHOLE,
            compiler_params=vmem_for(leaving[0], block, block, block, block, block),
            name="grad",
        )(leaving[0], *arrived, cotangent)
    else:
        local_grad = cotangent.astype(F32) * silu_slope(added(leaving[0], arrived))
        local_grad = local_grad.astype(BF16)
    out_feats = jax.nn.silu(added(leaving[0], arrived)).astype(BF16)

    core_grads = gather(local_grad, "src")
    other_grads = [swap(value, "rel", 1) for value in core_grads]

    by_target = jax.ShapeDtypeStruct((targets, tile, features), BF16)
    grads = pl.pallas_call(
        functools.partial(collect_kernel, tile),
        out_shape=by_target,
        in_specs=[WHOLE] * (2 * panels),
        out_specs=WHOLE,
        compiler_params=vmem_for(by_target, by_target),
        name="collect",
    )(*core_grads, *other_grads)

    total = jax.ShapeDtypeStruct((relations, features, features), F32)
    panel_sums, pieces, done = [], [], []
    for c in range(chunks):
        own_share = jax.ShapeDtypeStruct((bounds[c + 1] - bounds[c], share, features), F32)
        sent_share = jax.ShapeDtypeStruct(own_share.shape, BF16)
        *shares, _ = pl.pallas_call(
            functools.partial(weight_kernel, tile, combine),
            out_shape=(own_share,) + (sent_share,) * (panels - 1) + (sums[c],),
            in_specs=[SCALARS] + [WHOLE] * 4,
            out_specs=(WHOLE,) * (panels + 1),
            input_output_aliases={4: panels},
            compiler_params=vmem_for(*(own_share,) * panels, sums[c], by_target, *turned),
            name="weight_terms",
        )(lists[c], *prepared[:2], grads, prepared[2 + c])
        panel_sums.append(
            summed([shares[0]] + exchange(shares, "src"), BF16 if direct else F32)
        )
    for c, panel_sum in enumerate(panel_sums):
        if direct:
            masks = [1 << i for i in range(partitions.bit_length() - 1)]
            for mask in masks if c % 2 else reversed(masks):
                panel_sum = summed([panel_sum, swap(panel_sum, "dom", mask)])
        else:
            panel_sum = lax.psum(panel_sum, "dom").astype(BF16)
        pieces.append(gather(panel_sum, "src"))
    for c in range(chunks):
        done = [spread(bounds[c], pieces[c], total, done)]
    grad_rel = done[0]
    return (out_feats, grad_rel)


def solution(mesh):
    return jax.shard_map(
        local,
        mesh=mesh,
        in_specs=(
            P(("dom", "src", "rel"), None),
            P("rel", None, None),
            P("dom", "src", "rel", None),
            P("dom", "src", "rel", None, None),
            P("dom", "src", "rel"),
            P("dom", "src", "rel", None, None, None),
            P(("dom", "src", "rel"), None),
        ),
        out_specs=(P(("dom", "src", "rel"), None), P("rel", None, None)),
        check_vma=False,
    )
```

```python
import functools
import math

import jax
import jax.numpy as jnp
from jax import lax
from jax.experimental import pallas as pl
from jax.experimental.pallas import tpu as pltpu
from jax.sharding import PartitionSpec as P

F32, BF16, I32 = jnp.float32, jnp.bfloat16, jnp.int32
WHOLE = pl.BlockSpec(memory_space=pltpu.VMEM)
SCALARS = pl.BlockSpec(memory_space=pltpu.SMEM)
ANYWHERE = pl.BlockSpec(memory_space=pl.ANY)
UNROLL = 20


def vmem_for(*arrays):
    held = sum(math.prod(a.shape) * jnp.dtype(a.dtype).itemsize for a in arrays)
    return pltpu.CompilerParams(vmem_limit_bytes=held + held // 8 + 3 * 1024 * 1024)


def partner_pairs(size, mask):
    return [(i, i ^ mask) for i in range(size)]


def swap(value, axis, mask):
    return lax.ppermute(value, axis, partner_pairs(lax.axis_size(axis), mask))


def here():
    return [lax.axis_index(axis) for axis in ("dom", "src", "rel")]


def slot_of(places, partition, masked):
    return partition ^ places[0] if masked else partition


def packed(entries, targets, e, target, place):
    bits = (entries - 1).bit_length()
    return e | (target << bits) | (place << (bits + (targets - 1).bit_length()))


def unpacked(entries, targets, code):
    bits, more = (entries - 1).bit_length(), (targets - 1).bit_length()
    return code & ((1 << bits) - 1), (code >> bits) & ((1 << more) - 1), code >> (bits + more)


def for_entries(total, body):
    def step(i, carry):
        body([(jnp.minimum(i * UNROLL + u, total - 1), i * UNROLL + u < total) for u in range(UNROLL)])
        return carry

    lax.fori_loop(0, (total + UNROLL - 1) // UNROLL, step, 0)


def halo_block(first_block, halo_refs, i, tile):
    per_call = halo_refs[0].shape[0]
    rows = pl.ds(pl.multiple_of(first_block * tile, tile), tile)
    return halo_refs[i // per_call][i % per_call, rows, :]


def prepare_kernel(masked, owners, groups, bounds, targets, chosen, table, count, *refs):
    values, weight, values_here, weight_here = refs[:4]
    by_slot, refs = refs[4 : 4 + len(groups)], refs[4 + len(groups) :]
    by_relation, (pre, sems) = refs[: len(bounds) - 1], refs[len(bounds) - 1 :]
    entries, relations = values.shape[0], weight.shape[0]
    copies = [
        pltpu.make_async_copy(values, values_here, sems.at[0]),
        pltpu.make_async_copy(weight, weight_here, sems.at[1]),
    ]
    for copy in copies:
        copy.start()
    pre[...] = jnp.zeros_like(pre)
    places = here()
    cores, per_owner = owners
    slots = groups[-1][1]

    def put(e, found):
        target, relation = table[0, e], table[2, e]
        slot = slot_of(places, table[1, e], masked)
        own = (target >> (per_owner.bit_length() - 1)) & (cores - 1) == places[2]
        now = []
        for listed, (low, high, side) in zip(by_slot, groups):
            place = (slot - low) * relations + relation
            listed[found[len(now)]] = packed(entries, targets, e, target, place)
            inside = (slot >= low) & (slot < high)
            now.append(inside if side is None else inside & (own == side))
        for listed, low, high in zip(by_relation, bounds, bounds[1:]):
            place = (relation - low) * slots + slot
            listed[found[len(now)]] = packed(entries, targets, e, target, place)
            now.append((relation >= low) & (relation < high))
        return tuple(f + n.astype(I32) for f, n in zip(found, now))

    lists = (*by_slot, *by_relation)
    found = lax.fori_loop(0, count[0], put, (jnp.int32(0),) * len(lists))
    for listed, number in zip(lists, found):
        listed[entries] = number
    for listed, (low, high, _) in zip(by_slot, groups):
        for i in range(low, high):
            listed[entries + 1 + i - low] = chosen[slot_of(places, i, masked)]

    for copy in copies:
        copy.wait()


def near_kernel(tile, combine, order, *refs):
    *halo_refs, weight, values, before, pre, projected = refs
    entries = values.shape[0]
    firsts = [order[entries + 1 + i] for i in range(order.shape[0] - entries - 1)]
    project(tile, combine, firsts, halo_refs, weight, projected)
    add_entries(combine, values, weight, projected, order, order[entries], pre)


def theirs_kernel(tile, combine, owners, order, *refs):
    near_kernel(tile, combine, order, *refs[:-1])
    pre, sends = refs[-3], refs[-1]
    for distance in range(sends.shape[0]):
        for rows, block in blocks_of(tile, owners, here(), distance, 1):
            sends[distance, rows, :] = pre[block].astype(BF16)


def ours_kernel(tile, combine, owners, order, projected, weight, values, before, pre, *keeps):
    del before
    add_entries(combine, values, weight, projected, order, order[values.shape[0]], pre)
    for distance, keep in enumerate(keeps):
        for rows, block in blocks_of(tile, owners, here(), distance, 0):
            keep[rows, :] = pre[block]


def blocks_of(tile, owners, places, distance, other):
    cores, per_owner = owners
    owner = (places[1] ^ distance) * cores + (places[2] ^ other)
    return [(pl.ds(i * tile, tile), owner * per_owner + i) for i in range(per_owner)]


def halves(value):
    high = value.astype(BF16)
    return high, (value - high.astype(F32)).astype(BF16)


def project(tile, combine, firsts, halo_refs, weight, projected):
    relations = weight.shape[0]
    blocks = [halo_block(first, halo_refs, i, tile) for i, first in enumerate(firsts)]
    if not combine:
        for i, block in enumerate(blocks):
            projected[i] = block
        return
    stacked = jnp.concatenate(blocks, axis=0)
    for r in range(relations):
        high, low = halves(jnp.dot(stacked, weight[r], preferred_element_type=F32))
        for i in range(len(blocks)):
            rows = slice(i * tile, (i + 1) * tile)
            projected[i * relations + r, :tile, :] = high[rows]
            projected[i * relations + r, tile:, :] = low[rows]


def add_entries(combine, values, weight, projected, order, total, pre):
    entries, relations, spare = values.shape[0], weight.shape[0], pre.shape[0] - 1

    def body(positions):
        terms = []
        for position, real in positions:
            e, target, place = unpacked(entries, spare, order[position])
            if combine:
                twice = jnp.concatenate([values[e], values[e]], axis=1)
                term = jnp.dot(twice, projected[place], preferred_element_type=F32)
            else:
                message = jnp.dot(
                    values[e], projected[place // relations], preferred_element_type=F32
                )
                term = jnp.dot(
                    message.astype(BF16), weight[place % relations], preferred_element_type=F32
                )
            terms.append((jnp.where(real, target, spare), term))
        for target, term in terms:
            pre[target] = pre[target] + term

    for_entries(total, body)


def chip_kernel(*refs):
    count = (len(refs) - 1) // 2
    keeps, arrived, outs = refs[:count], refs[count], refs[count + 1 :]
    for m in range(count):
        outs[m][...] = (keeps[m][...] + arrived[m].astype(F32)).astype(outs[m].dtype)


def grad_kernel(own, first, second, third, cotangent, grad):
    pre = own[...] + first[...].astype(F32) + second[...].astype(F32) + third[...].astype(F32)
    grad[...] = (cotangent[...].astype(F32) * silu_slope(pre)).astype(BF16)


def turn_kernel(masked, tile, panels, halo_count, chosen, values, *refs):
    halo_refs, refs = refs[:halo_count], refs[halo_count:]
    values_turned, halo_turned, zeros, scratch = refs[0], refs[1], refs[2:-1], refs[-1]
    places = here()
    for each in zeros:
        each[...] = jnp.zeros_like(each)
    share = scratch.shape[0] // panels
    for slot in range(len(halo_refs) * halo_refs[0].shape[0]):
        block = halo_block(chosen[slot_of(places, slot, masked)], halo_refs, slot, tile)
        scratch[...] = block.astype(F32).T
        for m in range(panels):
            start = pl.multiple_of((places[1] ^ m) * share, share)
            halo_turned[pl.ds(m * share, share), pl.ds(slot * tile, tile)] = (
                scratch[pl.ds(start, share), :].astype(BF16)
            )

    batch = 8

    def step(i, carry):
        for u in range(batch):
            values_turned[i * batch + u] = values[i * batch + u].T
        return carry

    lax.fori_loop(0, values.shape[0] // batch, step, 0)


def collect_kernel(tile, *refs):
    grad_refs, grads = refs[:-1], refs[-1]
    panels = len(grad_refs) // 2
    per_owner = grad_refs[0].shape[0] // tile
    for g in range(2):
        for m in range(panels):
            owner = (lax.axis_index("src") ^ m) * 2 + (lax.axis_index("rel") ^ g)
            for part in range(per_owner):
                grads[owner * per_owner + part] = grad_refs[g * panels + m][
                    pl.ds(part * tile, tile), :
                ]


def weight_kernel(tile, combine, listed, *refs):
    values_turned, halo_turned, grads = refs[:3]
    outs, sums = refs[4:-1], refs[-1]
    features = halo_turned.shape[0]
    slots = halo_turned.shape[1] // tile
    relations, share = outs[0].shape[0], outs[0].shape[1]
    entries, targets, spare = values_turned.shape[0], grads.shape[0], sums.shape[0] - 1

    def body(positions):
        terms = []
        for position, real in positions:
            e, target, place = unpacked(entries, targets, listed[position])
            term = jnp.dot(values_turned[e], grads[target], preferred_element_type=F32)
            if not combine:
                columns = pl.ds(pl.multiple_of(place % slots * tile, tile), tile)
                term = jnp.dot(
                    halo_turned[:, columns], term.astype(BF16), preferred_element_type=F32
                )
                place = place // slots
            terms.append((jnp.where(real, place, spare), term))
        for place, term in terms:
            sums[place] = sums[place] + term

    for_entries(listed[entries], body)
    for r in range(relations):
        if combine:
            stacked = sums[r * slots : (r + 1) * slots].reshape(slots * tile, features)
            high, low = halves(stacked)
            grad = jnp.dot(halo_turned[...], high, preferred_element_type=F32)
            grad = grad + jnp.dot(halo_turned[...], low, preferred_element_type=F32)
        else:
            grad = sums[r]
        for m, out in enumerate(outs):
            out[r] = grad[m * share : (m + 1) * share].astype(out.dtype)


def spread_kernel(first_relation, *refs):
    out, scratch, sems = refs[-3:]
    shares = refs[: scratch.shape[0]]
    relations, share = scratch.shape[1], scratch.shape[2]
    copies = []
    for m in reversed(range(len(shares))):
        scratch[m] = shares[m][...].astype(F32)
        panel = lax.axis_index("src") ^ m
        rows = pl.ds(pl.multiple_of(panel * share, share), share)
        copies.append(
            pltpu.make_async_copy(
                scratch.at[m],
                out.at[pl.ds(first_relation, relations), rows, :],
                sems.at[m],
            )
        )
        copies[-1].start()
    for copy in copies:
        copy.wait()


def spread(first_relation, shares, total, so_far):
    scratch = jax.ShapeDtypeStruct((len(shares), *shares[0].shape), F32)
    return pl.pallas_call(
        functools.partial(spread_kernel, first_relation),
        out_shape=total,
        in_specs=[WHOLE] * len(shares) + [ANYWHERE] * len(so_far),
        out_specs=ANYWHERE,
        scratch_shapes=[
            pltpu.VMEM(scratch.shape, F32),
            pltpu.SemaphoreType.DMA((len(shares),)),
        ],
        input_output_aliases={len(shares): 0} if so_far else {},
        compiler_params=vmem_for(scratch, *shares),
        name="spread",
    )(*shares, *so_far)


def sum_kernel(*refs):
    total = refs[0][...].astype(F32)
    for ref in refs[1:-1]:
        total = total + ref[...].astype(F32)
    refs[-1][...] = total.astype(refs[-1].dtype)


def summed(values, dtype=BF16):
    out = jax.ShapeDtypeStruct(values[0].shape, dtype)
    return pl.pallas_call(
        sum_kernel,
        out_shape=out,
        in_specs=[WHOLE] * len(values),
        out_specs=WHOLE,
        compiler_params=vmem_for(out, *values),
        name="sum",
    )(*values)


def silu_slope(pre_values):
    logistic = jax.nn.sigmoid(pre_values)
    return logistic * (1.0 + pre_values * (1.0 - logistic))


def exchange(pieces, axis):
    return [swap(pieces[m].astype(BF16), axis, m) for m in range(len(pieces) - 1, 0, -1)]


def added(own, arrived):
    total = own.astype(F32)
    for value in arrived:
        total = total + value.astype(F32)
    return total


def gather(value, axis):
    return [value] + [swap(value, axis, m) for m in range(1, lax.axis_size(axis))]


def local(source_feats, rel_weight, halo_pick, entry_index, entry_count, entry_values, cotangent):
    partitions, panels = lax.axis_size("dom"), lax.axis_size("src")
    groups = lax.axis_size("rel")
    tile = entry_values.shape[-1]
    own_rows, features = cotangent.shape
    relations = rel_weight.shape[0]
    values = entry_values.reshape(-1, tile, tile)
    table = entry_index.reshape(3, -1)
    entries = table.shape[1]
    count = entry_count.reshape(1)
    chosen = halo_pick.reshape(-1)
    targets = own_rows * panels * groups // tile
    direct = partitions <= 8
    share = features // panels
    bounds = tuple(sorted({0, relations // 2, relations}))
    chunks = len(bounds) - 1

    panel_f32 = jax.ShapeDtypeStruct((own_rows, features), F32)
    panel_bf16 = jax.ShapeDtypeStruct((own_rows, features), BF16)
    pre_sums = jax.ShapeDtypeStruct((targets + 1, tile, features), F32)
    if direct:
        halo = [h[None] for h in gather(source_feats, "dom")]
    else:
        halo = [lax.all_gather(source_feats, "dom", axis=0)]
    slots = sum(h.shape[0] for h in halo)
    combine = slots * relations <= entries
    near = 1
    owners = groups, own_rows // tile
    start = near if direct else 0
    slot_groups = ((0, near, None),) * direct + ((start, slots, False), (start, slots, True))
    sums = [
        jax.ShapeDtypeStruct(
            ((high - low) * slots + 1, tile, features)
            if combine
            else (high - low + 1, features, features),
            F32,
        )
        for low, high in zip(bounds, bounds[1:])
    ]
    listings = [
        jax.ShapeDtypeStruct((entries + 1 + high - low,), I32)
        for low, high, _ in slot_groups
    ] + [jax.ShapeDtypeStruct((entries + 1,), I32)] * chunks
    held = [jax.ShapeDtypeStruct(v.shape, BF16) for v in (values, rel_weight)]
    values, rel_weight, *listings, pre = pl.pallas_call(
        functools.partial(prepare_kernel, direct, owners, slot_groups, bounds, targets),
        out_shape=(*held, *listings, pre_sums),
        in_specs=[SCALARS] * 3 + [ANYWHERE] * 2,
        out_specs=(WHOLE,) * 2 + (SCALARS,) * len(listings) + (WHOLE,),
        scratch_shapes=[pltpu.SemaphoreType.DMA((2,))],
        compiler_params=vmem_for(*held, pre_sums),
        cost_estimate=pl.CostEstimate(
            flops=0, bytes_accessed=4 * values.size, transcendentals=0
        ),
        name="prepare",
    )(chosen, table, count, values, rel_weight)
    lists = listings[-chunks:]

    sends = (jax.ShapeDtypeStruct((panels, own_rows, features), BF16),)
    cost = pl.CostEstimate(
        flops=4 * entries * tile * tile * features, bytes_accessed=values.size, transcendentals=0
    )
    for call, (low, high, _) in enumerate(slot_groups[:-1]):
        last = call == len(slot_groups) - 2
        blocks = halo[low:high] if direct else halo
        projected = jax.ShapeDtypeStruct(
            ((high - low) * relations, 2 * tile, features)
            if combine
            else (high - low, tile, features),
            BF16,
        )
        kernel = functools.partial(near_kernel, tile, combine)
        if last:
            kernel = functools.partial(theirs_kernel, tile, combine, owners)
        outs = (pre_sums, projected, *sends) if last else (pre_sums,)
        pre, *given = pl.pallas_call(
            kernel,
            out_shape=outs,
            in_specs=[SCALARS] + [WHOLE] * (len(blocks) + 3),
            out_specs=(WHOLE,) * len(outs),
            scratch_shapes=[] if last else [pltpu.VMEM(projected.shape, BF16)],
            input_output_aliases={3 + len(blocks): 0},
            compiler_params=vmem_for(*outs, projected, *blocks, rel_weight, values),
            cost_estimate=cost,
            name="forward",
        )(listings[call], *blocks, rel_weight, values, pre)
    projected, *given = given
    _, *keeps = pl.pallas_call(
        functools.partial(ours_kernel, tile, combine, owners),
        out_shape=(pre_sums,) + (panel_f32,) * panels,
        in_specs=[SCALARS] + [WHOLE] * 4,
        out_specs=(WHOLE,) * (1 + panels),
        input_output_aliases={4: 0},
        compiler_params=vmem_for(pre_sums, pre_sums, projected, rel_weight, values),
        cost_estimate=cost,
        name="forward_ours",
    )(listings[len(slot_groups) - 1], projected, rel_weight, values, pre)
    panel_sums = (panel_f32,) + (panel_bf16,) * (panels - 1)
    leaving = pl.pallas_call(
        chip_kernel,
        out_shape=panel_sums,
        in_specs=[WHOLE] * (panels + 1),
        out_specs=(WHOLE,) * panels,
        compiler_params=vmem_for(*panel_sums, *keeps, *sends),
        name="chip",
    )(*keeps, swap(given[0], "rel", 1))
    leaving, chosen_then = lax.optimization_barrier((leaving, chosen))
    arrived = exchange(leaving, "src")
    turned = (held[0], jax.ShapeDtypeStruct((features, slots * tile), BF16))
    prepared = pl.pallas_call(
        functools.partial(turn_kernel, direct, tile, panels, len(halo)),
        out_shape=(*turned, *sums),
        in_specs=[SCALARS] + [WHOLE] * (1 + len(halo)),
        out_specs=(WHOLE,) * (2 + chunks),
        scratch_shapes=[pltpu.VMEM((features, tile), F32)],
        compiler_params=vmem_for(*turned, *sums, values, *halo),
        cost_estimate=pl.CostEstimate(
            flops=0, bytes_accessed=4 * values.size, transcendentals=0
        ),
        name="turn",
    )(chosen_then, values, *halo)
    arrived, prepared = lax.optimization_barrier((arrived, prepared))
    block = jax.ShapeDtypeStruct((own_rows, features), BF16)
    if len(arrived) == 3:
        local_grad = pl.pallas_call(
            grad_kernel,
            out_shape=block,
            in_specs=[WHOLE] * 5,
            out_specs=WHOLE,
            compiler_params=vmem_for(leaving[0], block, block, block, block, block),
            name="grad",
        )(leaving[0], *arrived, cotangent)
    else:
        local_grad = cotangent.astype(F32) * silu_slope(added(leaving[0], arrived))
        local_grad = local_grad.astype(BF16)
    out_feats = jax.nn.silu(added(leaving[0], arrived)).astype(BF16)

    core_grads = gather(local_grad, "src")
    other_grads = [swap(value, "rel", 1) for value in core_grads]

    by_target = jax.ShapeDtypeStruct((targets, tile, features), BF16)
    grads = pl.pallas_call(
        functools.partial(collect_kernel, tile),
        out_shape=by_target,
        in_specs=[WHOLE] * (2 * panels),
        out_specs=WHOLE,
        compiler_params=vmem_for(by_target, by_target),
        name="collect",
    )(*core_grads, *other_grads)

    total = jax.ShapeDtypeStruct((relations, features, features), F32)
    panel_sums, pieces, done = [], [], []
    for c in range(chunks):
        own_share = jax.ShapeDtypeStruct((bounds[c + 1] - bounds[c], share, features), F32)
        sent_share = jax.ShapeDtypeStruct(own_share.shape, BF16)
        *shares, _ = pl.pallas_call(
            functools.partial(weight_kernel, tile, combine),
            out_shape=(own_share,) + (sent_share,) * (panels - 1) + (sums[c],),
            in_specs=[SCALARS] + [WHOLE] * 4,
            out_specs=(WHOLE,) * (panels + 1),
            input_output_aliases={4: panels},
            compiler_params=vmem_for(*(own_share,) * panels, sums[c], by_target, *turned),
            name="weight_terms",
        )(lists[c], *prepared[:2], grads, prepared[2 + c])
        panel_sums.append(
            summed([shares[0]] + exchange(shares, "src"), BF16 if direct else F32)
        )
    for c, panel_sum in enumerate(panel_sums):
        if direct:
            masks = [1 << i for i in range(partitions.bit_length() - 1)]
            for mask in masks if c % 2 else reversed(masks):
                panel_sum = summed([panel_sum, swap(panel_sum, "dom", mask)])
        else:
            panel_sum = lax.psum(panel_sum, "dom").astype(BF16)
        pieces.append(gather(panel_sum, "src"))
    for c in range(chunks):
        done = [spread(bounds[c], pieces[c], total, done)]
    grad_rel = done[0]
    return (out_feats, grad_rel)


def solution(mesh):
    return jax.shard_map(
        local,
        mesh=mesh,
        in_specs=(
            P(("dom", "src", "rel"), None),
            P("rel", None, None),
            P("dom", "src", "rel", None),
            P("dom", "src", "rel", None, None),
            P("dom", "src", "rel"),
            P("dom", "src", "rel", None, None, None),
            P(("dom", "src", "rel"), None),
        ),
        out_specs=(P(("dom", "src", "rel"), None), P("rel", None, None)),
        check_vma=False,
    )
```

```python
import functools
import math

import jax
import jax.numpy as jnp
from jax import lax
from jax.experimental import pallas as pl
from jax.experimental.pallas import tpu as pltpu
from jax.sharding import PartitionSpec as P

F32, BF16, I32 = jnp.float32, jnp.bfloat16, jnp.int32
WHOLE = pl.BlockSpec(memory_space=pltpu.VMEM)
SCALARS = pl.BlockSpec(memory_space=pltpu.SMEM)
ANYWHERE = pl.BlockSpec(memory_space=pl.ANY)
UNROLL = 20


def vmem_for(*arrays):
    held = sum(math.prod(a.shape) * jnp.dtype(a.dtype).itemsize for a in arrays)
    return pltpu.CompilerParams(vmem_limit_bytes=held + held // 8 + 3 * 1024 * 1024)


def partner_pairs(size, mask):
    return [(i, i ^ mask) for i in range(size)]


def swap(value, axis, mask):
    return lax.ppermute(value, axis, partner_pairs(lax.axis_size(axis), mask))


def here():
    return [lax.axis_index(axis) for axis in ("dom", "src", "rel")]


def slot_of(places, partition, masked):
    return partition ^ places[0] if masked else partition


def packed(entries, targets, e, target, place):
    bits = (entries - 1).bit_length()
    return e | (target << bits) | (place << (bits + (targets - 1).bit_length()))


def unpacked(entries, targets, code):
    bits, more = (entries - 1).bit_length(), (targets - 1).bit_length()
    return code & ((1 << bits) - 1), (code >> bits) & ((1 << more) - 1), code >> (bits + more)


def for_entries(total, body, unroll=UNROLL):
    def step(i, carry):
        body([(jnp.minimum(i * unroll + u, total - 1), i * unroll + u < total) for u in range(unroll)])
        return carry

    lax.fori_loop(0, (total + unroll - 1) // unroll, step, 0)


def halo_block(first_block, halo_refs, i, tile):
    per_call = halo_refs[0].shape[0]
    rows = pl.ds(pl.multiple_of(first_block * tile, tile), tile)
    return halo_refs[i // per_call][i % per_call, rows, :]


def prepare_kernel(masked, owners, groups, bounds, targets, chosen, table, count, *refs):
    values, weight, values_here, weight_here = refs[:4]
    by_slot, refs = refs[4 : 4 + len(groups)], refs[4 + len(groups) :]
    by_relation, (pre, sems) = refs[: len(bounds) - 1], refs[len(bounds) - 1 :]
    entries, relations = values.shape[0], weight.shape[0]
    copies = [
        pltpu.make_async_copy(values, values_here, sems.at[0]),
        pltpu.make_async_copy(weight, weight_here, sems.at[1]),
    ]
    for copy in copies:
        copy.start()
    pre[...] = jnp.zeros_like(pre)
    places = here()
    cores, per_owner = owners
    slots = groups[-1][1]

    def put(e, found):
        target, relation = table[0, e], table[2, e]
        slot = slot_of(places, table[1, e], masked)
        own = (target >> (per_owner.bit_length() - 1)) & (cores - 1) == places[2]
        now = []
        for listed, (low, high, side) in zip(by_slot, groups):
            place = (slot - low) * relations + relation
            listed[found[len(now)]] = packed(entries, targets, e, target, place)
            inside = (slot >= low) & (slot < high)
            now.append(inside if side is None else inside & (own == side))
        for listed, low, high in zip(by_relation, bounds, bounds[1:]):
            place = (relation - low) * slots + slot
            listed[found[len(now)]] = packed(entries, targets, e, target, place)
            now.append((relation >= low) & (relation < high))
        return tuple(f + n.astype(I32) for f, n in zip(found, now))

    lists = (*by_slot, *by_relation)
    found = lax.fori_loop(0, count[0], put, (jnp.int32(0),) * len(lists))
    for listed, number in zip(lists, found):
        listed[entries] = number
    for listed, (low, high, _) in zip(by_slot, groups):
        for i in range(low, high):
            listed[entries + 1 + i - low] = chosen[slot_of(places, i, masked)]

    for copy in copies:
        copy.wait()


def near_kernel(tile, combine, order, *refs):
    *halo_refs, weight, values, before, pre, projected = refs
    entries = values.shape[0]
    firsts = [order[entries + 1 + i] for i in range(order.shape[0] - entries - 1)]
    project(tile, combine, firsts, halo_refs, weight, projected)
    add_entries(combine, values, weight, projected, order, order[entries], pre)


def theirs_kernel(tile, combine, owners, order, *refs):
    near_kernel(tile, combine, order, *refs[:-1])
    pre, sends = refs[-3], refs[-1]
    for distance in range(sends.shape[0]):
        for rows, block in blocks_of(tile, owners, here(), distance, 1):
            sends[distance, rows, :] = pre[block].astype(BF16)


def ours_kernel(tile, combine, owners, order, projected, weight, values, before, pre, *keeps):
    del before
    add_entries(combine, values, weight, projected, order, order[values.shape[0]], pre)
    for distance, keep in enumerate(keeps):
        for rows, block in blocks_of(tile, owners, here(), distance, 0):
            keep[rows, :] = pre[block]


def blocks_of(tile, owners, places, distance, other):
    cores, per_owner = owners
    owner = (places[1] ^ distance) * cores + (places[2] ^ other)
    return [(pl.ds(i * tile, tile), owner * per_owner + i) for i in range(per_owner)]


def halves(value):
    high = value.astype(BF16)
    return high, (value - high.astype(F32)).astype(BF16)


def project(tile, combine, firsts, halo_refs, weight, projected):
    relations = weight.shape[0]
    blocks = [halo_block(first, halo_refs, i, tile) for i, first in enumerate(firsts)]
    if not combine:
        for i, block in enumerate(blocks):
            projected[i] = block
        return
    stacked = jnp.concatenate(blocks, axis=0)
    for r in range(relations):
        high, low = halves(jnp.dot(stacked, weight[r], preferred_element_type=F32))
        for i in range(len(blocks)):
            rows = slice(i * tile, (i + 1) * tile)
            projected[i * relations + r, :tile, :] = high[rows]
            projected[i * relations + r, tile:, :] = low[rows]


def add_entries(combine, values, weight, projected, order, total, pre):
    entries, relations, spare = values.shape[0], weight.shape[0], pre.shape[0] - 1

    def body(positions):
        terms = []
        for position, real in positions:
            e, target, place = unpacked(entries, spare, order[position])
            if combine:
                twice = jnp.concatenate([values[e], values[e]], axis=1)
                term = jnp.dot(twice, projected[place], preferred_element_type=F32)
            else:
                message = jnp.dot(
                    values[e], projected[place // relations], preferred_element_type=F32
                )
                term = jnp.dot(
                    message.astype(BF16), weight[place % relations], preferred_element_type=F32
                )
            terms.append((jnp.where(real, target, spare), term))
        for target, term in terms:
            pre[target] = pre[target] + term

    for_entries(total, body, 16 if order.shape[0] == entries + 2 else 28)


def chip_kernel(*refs):
    count = (len(refs) - 1) // 2
    keeps, arrived, outs = refs[:count], refs[count], refs[count + 1 :]
    for m in range(count):
        outs[m][...] = (keeps[m][...] + arrived[m].astype(F32)).astype(outs[m].dtype)


def grad_kernel(own, first, second, third, cotangent, grad):
    pre = own[...] + first[...].astype(F32) + second[...].astype(F32) + third[...].astype(F32)
    grad[...] = (cotangent[...].astype(F32) * silu_slope(pre)).astype(BF16)


def turn_kernel(masked, tile, panels, halo_count, chosen, values, *refs):
    halo_refs, refs = refs[:halo_count], refs[halo_count:]
    values_turned, halo_turned, zeros, scratch = refs[0], refs[1], refs[2:-1], refs[-1]
    places = here()
    for each in zeros:
        each[...] = jnp.zeros_like(each)
    share = scratch.shape[0] // panels
    for slot in range(len(halo_refs) * halo_refs[0].shape[0]):
        block = halo_block(chosen[slot_of(places, slot, masked)], halo_refs, slot, tile)
        scratch[...] = block.astype(F32).T
        for m in range(panels):
            start = pl.multiple_of((places[1] ^ m) * share, share)
            halo_turned[pl.ds(m * share, share), pl.ds(slot * tile, tile)] = (
                scratch[pl.ds(start, share), :].astype(BF16)
            )

    batch = 8

    def step(i, carry):
        for u in range(batch):
            values_turned[i * batch + u] = values[i * batch + u].T
        return carry

    lax.fori_loop(0, values.shape[0] // batch, step, 0)


def collect_kernel(tile, *refs):
    grad_refs, grads = refs[:-1], refs[-1]
    panels = len(grad_refs) // 2
    per_owner = grad_refs[0].shape[0] // tile
    for g in range(2):
        for m in range(panels):
            owner = (lax.axis_index("src") ^ m) * 2 + (lax.axis_index("rel") ^ g)
            for part in range(per_owner):
                grads[owner * per_owner + part] = grad_refs[g * panels + m][
                    pl.ds(part * tile, tile), :
                ]


def weight_kernel(tile, combine, listed, *refs):
    values_turned, halo_turned, grads = refs[:3]
    outs, sums = refs[4:-1], refs[-1]
    features = halo_turned.shape[0]
    slots = halo_turned.shape[1] // tile
    relations, share = outs[0].shape[0], outs[0].shape[1]
    entries, targets, spare = values_turned.shape[0], grads.shape[0], sums.shape[0] - 1

    def body(positions):
        terms = []
        for position, real in positions:
            e, target, place = unpacked(entries, targets, listed[position])
            term = jnp.dot(values_turned[e], grads[target], preferred_element_type=F32)
            if not combine:
                columns = pl.ds(pl.multiple_of(place % slots * tile, tile), tile)
                term = jnp.dot(
                    halo_turned[:, columns], term.astype(BF16), preferred_element_type=F32
                )
                place = place // slots
            terms.append((jnp.where(real, place, spare), term))
        for place, term in terms:
            sums[place] = sums[place] + term

    for_entries(listed[entries], body)
    for r in range(relations):
        if combine:
            stacked = sums[r * slots : (r + 1) * slots].reshape(slots * tile, features)
            high, low = halves(stacked)
            grad = jnp.dot(halo_turned[...], high, preferred_element_type=F32)
            grad = grad + jnp.dot(halo_turned[...], low, preferred_element_type=F32)
        else:
            grad = sums[r]
        for m, out in enumerate(outs):
            out[r] = grad[m * share : (m + 1) * share].astype(out.dtype)


def spread_kernel(first_relation, *refs):
    out, scratch, sems = refs[-3:]
    shares = refs[: scratch.shape[0]]
    relations, share = scratch.shape[1], scratch.shape[2]
    copies = []
    for m in reversed(range(len(shares))):
        scratch[m] = shares[m][...].astype(F32)
        panel = lax.axis_index("src") ^ m
        rows = pl.ds(pl.multiple_of(panel * share, share), share)
        copies.append(
            pltpu.make_async_copy(
                scratch.at[m],
                out.at[pl.ds(first_relation, relations), rows, :],
                sems.at[m],
            )
        )
        copies[-1].start()
    for copy in copies:
        copy.wait()


def spread(first_relation, shares, total, so_far):
    scratch = jax.ShapeDtypeStruct((len(shares), *shares[0].shape), F32)
    return pl.pallas_call(
        functools.partial(spread_kernel, first_relation),
        out_shape=total,
        in_specs=[WHOLE] * len(shares) + [ANYWHERE] * len(so_far),
        out_specs=ANYWHERE,
        scratch_shapes=[
            pltpu.VMEM(scratch.shape, F32),
            pltpu.SemaphoreType.DMA((len(shares),)),
        ],
        input_output_aliases={len(shares): 0} if so_far else {},
        compiler_params=vmem_for(scratch, *shares),
        name="spread",
    )(*shares, *so_far)


def sum_kernel(*refs):
    total = refs[0][...].astype(F32)
    for ref in refs[1:-1]:
        total = total + ref[...].astype(F32)
    refs[-1][...] = total.astype(refs[-1].dtype)


def summed(values, dtype=BF16):
    out = jax.ShapeDtypeStruct(values[0].shape, dtype)
    return pl.pallas_call(
        sum_kernel,
        out_shape=out,
        in_specs=[WHOLE] * len(values),
        out_specs=WHOLE,
        compiler_params=vmem_for(out, *values),
        name="sum",
    )(*values)


def silu_slope(pre_values):
    logistic = jax.nn.sigmoid(pre_values)
    return logistic * (1.0 + pre_values * (1.0 - logistic))


def exchange(pieces, axis):
    return [swap(pieces[m].astype(BF16), axis, m) for m in range(len(pieces) - 1, 0, -1)]


def added(own, arrived):
    total = own.astype(F32)
    for value in arrived:
        total = total + value.astype(F32)
    return total


def gather(value, axis):
    return [value] + [swap(value, axis, m) for m in range(1, lax.axis_size(axis))]


def local(source_feats, rel_weight, halo_pick, entry_index, entry_count, entry_values, cotangent):
    partitions, panels = lax.axis_size("dom"), lax.axis_size("src")
    groups = lax.axis_size("rel")
    tile = entry_values.shape[-1]
    own_rows, features = cotangent.shape
    relations = rel_weight.shape[0]
    values = entry_values.reshape(-1, tile, tile)
    table = entry_index.reshape(3, -1)
    entries = table.shape[1]
    count = entry_count.reshape(1)
    chosen = halo_pick.reshape(-1)
    targets = own_rows * panels * groups // tile
    direct = partitions <= 8
    share = features // panels
    bounds = tuple(sorted({0, relations // 2, relations}))
    chunks = len(bounds) - 1

    panel_f32 = jax.ShapeDtypeStruct((own_rows, features), F32)
    panel_bf16 = jax.ShapeDtypeStruct((own_rows, features), BF16)
    pre_sums = jax.ShapeDtypeStruct((targets + 1, tile, features), F32)
    if direct:
        halo = [h[None] for h in gather(source_feats, "dom")]
    else:
        halo = [lax.all_gather(source_feats, "dom", axis=0)]
    slots = sum(h.shape[0] for h in halo)
    combine = slots * relations <= entries
    near = 1
    owners = groups, own_rows // tile
    start = near if direct else 0
    slot_groups = ((0, near, None),) * direct + ((start, slots, False), (start, slots, True))
    sums = [
        jax.ShapeDtypeStruct(
            ((high - low) * slots + 1, tile, features)
            if combine
            else (high - low + 1, features, features),
            F32,
        )
        for low, high in zip(bounds, bounds[1:])
    ]
    listings = [
        jax.ShapeDtypeStruct((entries + 1 + high - low,), I32)
        for low, high, _ in slot_groups
    ] + [jax.ShapeDtypeStruct((entries + 1,), I32)] * chunks
    held = [jax.ShapeDtypeStruct(v.shape, BF16) for v in (values, rel_weight)]
    values, rel_weight, *listings, pre = pl.pallas_call(
        functools.partial(prepare_kernel, direct, owners, slot_groups, bounds, targets),
        out_shape=(*held, *listings, pre_sums),
        in_specs=[SCALARS] * 3 + [ANYWHERE] * 2,
        out_specs=(WHOLE,) * 2 + (SCALARS,) * len(listings) + (WHOLE,),
        scratch_shapes=[pltpu.SemaphoreType.DMA((2,))],
        compiler_params=vmem_for(*held, pre_sums),
        cost_estimate=pl.CostEstimate(
            flops=0, bytes_accessed=4 * values.size, transcendentals=0
        ),
        name="prepare",
    )(chosen, table, count, values, rel_weight)
    lists = listings[-chunks:]

    sends = (jax.ShapeDtypeStruct((panels, own_rows, features), BF16),)
    cost = pl.CostEstimate(
        flops=4 * entries * tile * tile * features, bytes_accessed=values.size, transcendentals=0
    )
    for call, (low, high, _) in enumerate(slot_groups[:-1]):
        last = call == len(slot_groups) - 2
        blocks = halo[low:high] if direct else halo
        projected = jax.ShapeDtypeStruct(
            ((high - low) * relations, 2 * tile, features)
            if combine
            else (high - low, tile, features),
            BF16,
        )
        kernel = functools.partial(near_kernel, tile, combine)
        if last:
            kernel = functools.partial(theirs_kernel, tile, combine, owners)
        outs = (pre_sums, projected, *sends) if last else (pre_sums,)
        pre, *given = pl.pallas_call(
            kernel,
            out_shape=outs,
            in_specs=[SCALARS] + [WHOLE] * (len(blocks) + 3),
            out_specs=(WHOLE,) * len(outs),
            scratch_shapes=[] if last else [pltpu.VMEM(projected.shape, BF16)],
            input_output_aliases={3 + len(blocks): 0},
            compiler_params=vmem_for(*outs, projected, *blocks, rel_weight, values),
            cost_estimate=cost,
            name="forward",
        )(listings[call], *blocks, rel_weight, values, pre)
    projected, *given = given
    _, *keeps = pl.pallas_call(
        functools.partial(ours_kernel, tile, combine, owners),
        out_shape=(pre_sums,) + (panel_f32,) * panels,
        in_specs=[SCALARS] + [WHOLE] * 4,
        out_specs=(WHOLE,) * (1 + panels),
        input_output_aliases={4: 0},
        compiler_params=vmem_for(pre_sums, pre_sums, projected, rel_weight, values),
        cost_estimate=cost,
        name="forward_ours",
    )(listings[len(slot_groups) - 1], projected, rel_weight, values, pre)
    panel_sums = (panel_f32,) + (panel_bf16,) * (panels - 1)
    leaving = pl.pallas_call(
        chip_kernel,
        out_shape=panel_sums,
        in_specs=[WHOLE] * (panels + 1),
        out_specs=(WHOLE,) * panels,
        compiler_params=vmem_for(*panel_sums, *keeps, *sends),
        name="chip",
    )(*keeps, swap(given[0], "rel", 1))
    leaving, chosen_then = lax.optimization_barrier((leaving, chosen))
    arrived = exchange(leaving, "src")
    turned = (held[0], jax.ShapeDtypeStruct((features, slots * tile), BF16))
    prepared = pl.pallas_call(
        functools.partial(turn_kernel, direct, tile, panels, len(halo)),
        out_shape=(*turned, *sums),
        in_specs=[SCALARS] + [WHOLE] * (1 + len(halo)),
        out_specs=(WHOLE,) * (2 + chunks),
        scratch_shapes=[pltpu.VMEM((features, tile), F32)],
        compiler_params=vmem_for(*turned, *sums, values, *halo),
        cost_estimate=pl.CostEstimate(
            flops=0, bytes_accessed=4 * values.size, transcendentals=0
        ),
        name="turn",
    )(chosen_then, values, *halo)
    arrived, prepared = lax.optimization_barrier((arrived, prepared))
    block = jax.ShapeDtypeStruct((own_rows, features), BF16)
    if len(arrived) == 3:
        local_grad = pl.pallas_call(
            grad_kernel,
            out_shape=block,
            in_specs=[WHOLE] * 5,
            out_specs=WHOLE,
            compiler_params=vmem_for(leaving[0], block, block, block, block, block),
            name="grad",
        )(leaving[0], *arrived, cotangent)
    else:
        local_grad = cotangent.astype(F32) * silu_slope(added(leaving[0], arrived))
        local_grad = local_grad.astype(BF16)
    out_feats = jax.nn.silu(added(leaving[0], arrived)).astype(BF16)

    core_grads = gather(local_grad, "src")
    other_grads = [swap(value, "rel", 1) for value in core_grads]

    by_target = jax.ShapeDtypeStruct((targets, tile, features), BF16)
    grads = pl.pallas_call(
        functools.partial(collect_kernel, tile),
        out_shape=by_target,
        in_specs=[WHOLE] * (2 * panels),
        out_specs=WHOLE,
        compiler_params=vmem_for(by_target, by_target),
        name="collect",
    )(*core_grads, *other_grads)

    total = jax.ShapeDtypeStruct((relations, features, features), F32)
    panel_sums, pieces, done = [], [], []
    for c in range(chunks):
        own_share = jax.ShapeDtypeStruct((bounds[c + 1] - bounds[c], share, features), F32)
        sent_share = jax.ShapeDtypeStruct(own_share.shape, BF16)
        *shares, _ = pl.pallas_call(
            functools.partial(weight_kernel, tile, combine),
            out_shape=(own_share,) + (sent_share,) * (panels - 1) + (sums[c],),
            in_specs=[SCALARS] + [WHOLE] * 4,
            out_specs=(WHOLE,) * (panels + 1),
            input_output_aliases={4: panels},
            compiler_params=vmem_for(*(own_share,) * panels, sums[c], by_target, *turned),
            name="weight_terms",
        )(lists[c], *prepared[:2], grads, prepared[2 + c])
        panel_sums.append(
            summed([shares[0]] + exchange(shares, "src"), BF16 if direct else F32)
        )
    for c, panel_sum in enumerate(panel_sums):
        if direct:
            masks = [1 << i for i in range(partitions.bit_length() - 1)]
            for mask in masks if c % 2 else reversed(masks):
                panel_sum = summed([panel_sum, swap(panel_sum, "dom", mask)])
        else:
            panel_sum = lax.psum(panel_sum, "dom").astype(BF16)
        pieces.append(gather(panel_sum, "src"))
    for c in range(chunks):
        done = [spread(bounds[c], pieces[c], total, done)]
    grad_rel = done[0]
    return (out_feats, grad_rel)


def solution(mesh):
    return jax.shard_map(
        local,
        mesh=mesh,
        in_specs=(
            P(("dom", "src", "rel"), None),
            P("rel", None, None),
            P("dom", "src", "rel", None),
            P("dom", "src", "rel", None, None),
            P("dom", "src", "rel"),
            P("dom", "src", "rel", None, None, None),
            P(("dom", "src", "rel"), None),
        ),
        out_specs=(P(("dom", "src", "rel"), None), P("rel", None, None)),
        check_vma=False,
    )
```
